256 devices in a mesh: row: 32 (over y_lo, z, core), col: 8 (over x, y_hi).
Axes of the slice: x: 4, y: 4 (y_hi: 2, y_lo: 2; y = y_hi * 2 + y_lo), z: 8, core: 2. Of those that a mesh axis runs over, the one named last changes fastest.
Arguments:
- features: bfloat16 [1024, 1024, 64], P('row', 'col'), may hold values from -6 to 6
- conv_weight: bfloat16 [3, 3, 64, 64], replicated, may hold values from -0.25 to 0.25
- head_weight: bfloat16 [64, 37], replicated, may hold values from -8 to 8
- head_bias: float32 [37], replicated, may hold values from -4 to 4
- labels: int32 [1024, 1024], P('row', 'col'), may hold values from 0 to 36
- valid: int32 [1024, 1024], P('row', 'col'), may hold values 0 or 1
Outputs:
- loss: float32 [], replicated
- grad_features: bfloat16 [1024, 1024, 64], P('row', 'col')
- conv_grad: float32 [3, 3, 64, 64], replicated
- head_grad: float32 [64, 37], replicated
- bias_grad: float32 [37], replicated
The draws below stay inside these ranges and needn't reach their ends.
All inputs are finite; a program needn't handle non-finite values. No bound on the sum of `valid` on one device may be relied on, other than what follows from the above.
Results may differ from the reference program's by a relative error of at most 0.0035.
The reference program's roundings to bfloat16 on the way count: a program that leaves them out, or rounds other values in their place, can miss the bound.
Values may be sent and summed in bfloat16 or wider, within the bound.
No kernel may reach another device: no remote copies, remote signals or barrier semaphores. Data moves between devices by JAX's collectives and lax.ppermute only.
A program may use at most 64 MiB of HBM per device.

```python
import jax
import jax.numpy as jnp
from jax import lax

RESIDUE_COUNT = 1024
PAIR_CHANNELS = 64
NB = 37
DILATION_STEP = 8


def draw_head_weight(key, part):
    key = jax.random.fold_in(key, 7)
    first = jax.random.fold_in(key, 0)
    base = jax.random.normal(first, (PAIR_CHANNELS, NB), jnp.float32)
    values = jnp.clip(base / PAIR_CHANNELS ** 0.5, -0.75, 0.75)
    return values.astype(jnp.bfloat16)


def place_ends(array, key, least, largest):
    extent = array.shape
    spot = [jax.random.randint(jax.random.fold_in(key, axis), (), 0, extent[axis]) for axis in range(len(extent))]
    array = array.at[tuple(spot)].set(least)
    longest = extent.index(max(extent))
    spot[longest] = (spot[longest] + 1) % extent[longest]
    return array.at[tuple(spot)].set(largest)


def shard_levels(stream_key, extent, cuts, smallest, high):
    factor_of = 1.0
    for axis_at, blocks in cuts:
        draws = jax.random.uniform(jax.random.fold_in(jax.random.fold_in(stream_key, 6), axis_at), (blocks,), jnp.float32, smallest / len(cuts), high / len(cuts))
        factor_of = factor_of * jnp.repeat(jnp.exp(draws), extent[axis_at] // blocks).reshape((-1,) + (1,) * (len(extent) - 1 - axis_at))
    return factor_of


def bell_draw(key, dims, deviation, bound, shards=(), kind=jnp.bfloat16):
    gain = shard_levels(key, dims, shards, -0.22, 0.18) if shards else 1.0
    values = jax.random.normal(key, dims, jnp.float32) * deviation * gain
    return jnp.minimum(jnp.maximum(values, -bound), bound).astype(kind)


def setup_inputs(seed: int = 0) -> dict:
    key_list = jax.random.split(jax.random.key(seed), 7)
    return {
        "features": bell_draw(key_list[0], (RESIDUE_COUNT, RESIDUE_COUNT, PAIR_CHANNELS), 1.0, 6.0, ((0, 32), (1, 8))),
        "conv_weight": bell_draw(key_list[1], (3, 3, PAIR_CHANNELS, PAIR_CHANNELS), (9 * PAIR_CHANNELS) ** -0.5, 0.25),
        "head_weight": draw_head_weight(jax.random.fold_in(key_list[6], 71), 0),
        "head_bias": bell_draw(key_list[3], (NB,), 1.0, 4.0, (), jnp.float32),
        "labels": place_ends(jax.random.randint(key_list[4], (RESIDUE_COUNT, RESIDUE_COUNT), 0, NB), jax.random.fold_in(key_list[4], 1), 0, NB - 1).astype(jnp.int32),
        "valid": place_ends((jax.random.randint(key_list[5], (RESIDUE_COUNT, RESIDUE_COUNT), 0, 4) < 3).astype(jnp.int32), jax.random.fold_in(key_list[5], 1), 0, 1),
    }


def taps_product(padded_input, weight, row_span, column_span, flip):
    width = padded_input.shape[-1]
    total = jnp.zeros((row_span * column_span, weight.shape[-1]), jnp.float32)
    for kernel_row in range(3):
        for kernel_column in range(3):
            row_offset = (2 - kernel_row) if flip else kernel_row
            column_offset = (2 - kernel_column) if flip else kernel_column
            input_window = padded_input[row_offset * DILATION_STEP:row_offset * DILATION_STEP + row_span, column_offset * DILATION_STEP:column_offset * DILATION_STEP + column_span]
            kernel = weight[kernel_row, kernel_column].T if flip else weight[kernel_row, kernel_column]
            total = total + jnp.dot(input_window.reshape(-1, width), kernel, preferred_element_type=jnp.float32)
    return total.reshape(row_span, column_span, -1)


def reference(features, conv_weight, head_weight, head_bias, labels, valid):
    block_index = 128 if RESIDUE_COUNT % 128 == 0 else RESIDUE_COUNT
    nblk = RESIDUE_COUNT // block_index
    feat32 = features.astype(jnp.float32)
    activation = jax.nn.elu(feat32).astype(jnp.bfloat16)
    padded_input = jnp.pad(activation, ((DILATION_STEP, DILATION_STEP), (DILATION_STEP, DILATION_STEP), (0, 0)))

    def forward_block(position_index):
        feature_strip = lax.dynamic_slice_in_dim(padded_input, position_index * block_index, block_index + 2 * DILATION_STEP, 0)
        return taps_product(feature_strip, conv_weight, block_index, RESIDUE_COUNT, False)

    conv_out = lax.map(forward_block, jnp.arange(nblk, dtype=jnp.int32)).reshape(RESIDUE_COUNT, RESIDUE_COUNT, PAIR_CHANNELS)
    mixed = (feat32 + conv_out).astype(jnp.bfloat16)
    flat = mixed.reshape(-1, PAIR_CHANNELS)
    logits = (jnp.dot(flat, head_weight, preferred_element_type=jnp.float32) + head_bias).reshape(RESIDUE_COUNT, RESIDUE_COUNT, NB)
    sym = 0.5 * (logits + jnp.swapaxes(logits, 0, 1))
    lse = jax.nn.logsumexp(sym, axis=-1)
    onehot = (labels[..., None] == jnp.arange(NB, dtype=jnp.int32)).astype(jnp.float32)
    picked = jnp.sum(sym * onehot, axis=-1)
    maskf = valid.astype(jnp.float32)
    count = jnp.maximum(jnp.sum(maskf), 1.0)
    loss = jnp.sum(maskf * (lse - picked)) / count
    prob = jnp.exp(sym - lse[..., None])
    grad_cells = maskf[..., None] * (prob - onehot) / count
    grad_logits = 0.5 * (grad_cells + jnp.swapaxes(grad_cells, 0, 1))
    glflat = grad_logits.reshape(-1, NB)
    head_grad = jnp.dot(flat.astype(jnp.float32).T, glflat, precision=lax.Precision.HIGHEST)
    bias_grad = jnp.sum(glflat, axis=0)
    grad_mixed = jnp.dot(glflat, head_weight.astype(jnp.float32).T, precision=lax.Precision.HIGHEST).reshape(RESIDUE_COUNT, RESIDUE_COUNT, PAIR_CHANNELS)
    lower_gradient = grad_mixed.astype(jnp.bfloat16)
    padded_gradient = jnp.pad(lower_gradient, ((DILATION_STEP, DILATION_STEP), (DILATION_STEP, DILATION_STEP), (0, 0)))

    def backward_block(position_index):
        feature_strip = lax.dynamic_slice_in_dim(padded_gradient, position_index * block_index, block_index + 2 * DILATION_STEP, 0)
        return taps_product(feature_strip, conv_weight, block_index, RESIDUE_COUNT, True)

    back = lax.map(backward_block, jnp.arange(nblk, dtype=jnp.int32)).reshape(RESIDUE_COUNT, RESIDUE_COUNT, PAIR_CHANNELS)
    slope = jnp.where(feat32 > 0, 1.0, jnp.exp(feat32))
    grad_features = (grad_mixed + slope * back).astype(jnp.bfloat16)

    def kernel_block(total, position_index):
        feature_strip = lax.dynamic_slice_in_dim(padded_input, position_index * block_index, block_index + 2 * DILATION_STEP, 0)
        lower = lax.dynamic_slice_in_dim(lower_gradient, position_index * block_index, block_index, 0).reshape(-1, PAIR_CHANNELS)
        parts = []
        for kernel_row in range(3):
            for kernel_column in range(3):
                input_window = feature_strip[kernel_row * DILATION_STEP:kernel_row * DILATION_STEP + block_index, kernel_column * DILATION_STEP:kernel_column * DILATION_STEP + RESIDUE_COUNT].reshape(-1, PAIR_CHANNELS)
                parts.append(jnp.dot(input_window.T, lower, preferred_element_type=jnp.float32))
        return total + jnp.stack(parts).reshape(3, 3, PAIR_CHANNELS, PAIR_CHANNELS), None

    conv_grad, unused = lax.scan(kernel_block, jnp.zeros((3, 3, PAIR_CHANNELS, PAIR_CHANNELS), jnp.float32), jnp.arange(nblk, dtype=jnp.int32))
    return loss, grad_features, conv_grad, head_grad, bias_grad
```

```python
import jax
import jax.numpy as jnp
from jax import lax
from jax.sharding import PartitionSpec as P

DILATION_STEP = 8
GRID = ("row", "col")


def send(block, target):
    nrow, ncol = lax.axis_size("row"), lax.axis_size("col")
    pairs = []
    for r in range(nrow):
        for c in range(ncol):
            r2, c2 = target(r, c)
            pairs.append((r * ncol + c, r2 * ncol + c2))
    return lax.ppermute(block, GRID, pairs)


def padded(block, sides, width):
    for axis, dim in sides:
        count = lax.axis_size(axis)
        forward = [(i, i + 1) for i in range(count - 1)]
        backward = [(target, source) for source, target in forward]
        low = lax.ppermute(
            lax.slice_in_dim(block, block.shape[dim] - width, None, axis=dim), axis, forward
        )
        high = lax.ppermute(lax.slice_in_dim(block, 0, width, axis=dim), axis, backward)
        block = jnp.concatenate([low, block, high], axis=dim)
    return block


def widen(block):
    return padded(block, (("row", 0), ("col", 1)), DILATION_STEP)


def taps_product(padded_input, weight, row_span, column_span, flip):
    width = padded_input.shape[-1]
    total = jnp.zeros((row_span * column_span, weight.shape[-1]), jnp.float32)
    for kernel_row in range(3):
        for kernel_column in range(3):
            row_offset = 2 - kernel_row if flip else kernel_row
            column_offset = 2 - kernel_column if flip else kernel_column
            window = padded_input[
                row_offset * DILATION_STEP : row_offset * DILATION_STEP + row_span,
                column_offset * DILATION_STEP : column_offset * DILATION_STEP + column_span,
            ]
            kernel = (
                weight[kernel_row, kernel_column].T if flip else weight[kernel_row, kernel_column]
            )
            total = total + jnp.dot(
                window.reshape(-1, width), kernel, preferred_element_type=jnp.float32
            )
    return total.reshape(row_span, column_span, -1)


def mirror(mixed, labels, valid):
    rows, cols, chans = mixed.shape
    parts = cols // rows
    place = lax.axis_index("row") % parts
    lab = labels.astype(jnp.bfloat16).reshape(rows, parts, rows).swapaxes(0, 1)
    val = valid.astype(jnp.bfloat16).reshape(rows, parts, rows).swapaxes(0, 1)
    mix = mixed.reshape(rows, parts, rows, chans).swapaxes(0, 1)
    cells = rows * rows
    split = cells * chans // 128
    load = jnp.concatenate(
        [
            mix.reshape(parts, split, 128),
            lab.reshape(parts, cells // 128, 128),
            val.reshape(parts, cells // 128, 128),
        ],
        axis=1,
    )
    got = []
    for step in range(parts):
        block = lax.dynamic_index_in_dim(load, place ^ step, 0, keepdims=False)
        got.append(send(block, lambda r, c: (parts * c + (r % parts ^ step), r // parts)))
    got = jnp.stack(got)
    got = jnp.stack(
        [lax.dynamic_index_in_dim(got, place ^ q, 0, keepdims=False) for q in range(parts)]
    )
    mix_t = got[:, :split].reshape(cols, rows, chans).swapaxes(0, 1)
    lab_t = got[:, split : split + cells // 128].reshape(cols, rows).T.astype(jnp.int32)
    val_t = got[:, split + cells // 128 :].reshape(cols, rows).T.astype(jnp.float32)
    return mix_t, lab_t, val_t


def partners(stage):
    if stage < 2:
        return lambda m: lambda r, c: (r ^ (m << (2 * stage)), c)
    if stage == 2:
        return lambda m: lambda r, c: (r ^ ((m & 1) << 4), c ^ (m >> 1))
    return lambda m: lambda r, c: (r, c ^ (m << 1))


def total_small(value):
    for bit in range(5):
        value = value + send(value, lambda r, c: (r ^ (1 << bit), c))
    for bit in range(3):
        value = value + send(value, lambda r, c: (r, c ^ (1 << bit)))
    return value


def total_rows(block):
    quarter = block.shape[0] // 4
    place = lax.axis_index("row") % 4
    near = partners(0)
    cut = block.reshape(4, quarter, block.shape[1])
    pick = lambda m: lax.dynamic_index_in_dim(cut, place ^ m, 0, keepdims=False)
    part = (pick(0) + send(pick(1), near(1))) + (send(pick(2), near(2)) + send(pick(3), near(3)))
    for stage in (1, 2, 3):
        to = partners(stage)
        part = (part + send(part, to(1))) + (send(part, to(2)) + send(part, to(3)))
    got = jnp.stack([part] + [send(part, near(m)) for m in (1, 2, 3)])
    return jnp.concatenate(
        [lax.dynamic_index_in_dim(got, place ^ q, 0, keepdims=False) for q in range(4)]
    )


def per_device(features, conv_weight, head_weight, head_bias, labels, valid):
    rows, cols, chans = features.shape
    bins = head_weight.shape[1]
    maskf = valid.astype(jnp.float32)
    count = jnp.maximum(total_small(jnp.full((8, 128), jnp.sum(maskf)))[0, 0], 1.0)
    feat32 = features.astype(jnp.float32)
    activation = jax.nn.elu(feat32).astype(jnp.bfloat16)
    padded_input = widen(activation)
    conv_out = taps_product(padded_input, conv_weight, rows, cols, False)
    mixed = (feat32 + conv_out).astype(jnp.bfloat16)
    flat = mixed.reshape(-1, chans)
    mixed_t, labels_t, mask_t = mirror(mixed, labels, valid)
    logits = jnp.dot(flat, head_weight, preferred_element_type=jnp.float32) + head_bias
    logits_t = (
        jnp.dot(mixed_t.reshape(-1, chans), head_weight, preferred_element_type=jnp.float32)
        + head_bias
    )
    sym = (0.5 * (logits + logits_t)).reshape(rows, cols, bins)
    lse = jax.nn.logsumexp(sym, axis=-1)
    bin_ids = jnp.arange(bins, dtype=jnp.int32)
    onehot = (labels[..., None] == bin_ids).astype(jnp.float32)
    onehot_t = (labels_t[..., None] == bin_ids).astype(jnp.float32)
    picked = jnp.sum(sym * onehot, axis=-1)
    loss_part = jnp.sum(maskf * (lse - picked))
    prob = jnp.exp(sym - lse[..., None])
    own = maskf[..., None] * (prob - onehot) / count
    other = mask_t[..., None] * (prob - onehot_t) / count
    glflat = (0.5 * (own + other)).reshape(-1, bins)
    head_part = jnp.dot(flat.astype(jnp.float32).T, glflat, precision=lax.Precision.HIGHEST)
    bias_part = jnp.sum(glflat, axis=0)
    grad_mixed = jnp.dot(
        glflat, head_weight.astype(jnp.float32).T, precision=lax.Precision.HIGHEST
    ).reshape(rows, cols, chans)
    lower_gradient = grad_mixed.astype(jnp.bfloat16)
    lower = lower_gradient.reshape(-1, chans)
    parts = []
    for kernel_row in range(3):
        for kernel_column in range(3):
            window = padded_input[
                kernel_row * DILATION_STEP : kernel_row * DILATION_STEP + rows,
                kernel_column * DILATION_STEP : kernel_column * DILATION_STEP + cols,
            ].reshape(-1, chans)
            parts.append(jnp.dot(window.T, lower, preferred_element_type=jnp.float32))
    flat_sums = jnp.concatenate(
        [
            jnp.stack(parts).reshape(-1),
            head_part.reshape(-1),
            bias_part,
            loss_part.reshape(1),
        ]
    )
    length = flat_sums.shape[0]
    lines = -(-length // 4096) * 32
    sums = total_rows(jnp.pad(flat_sums, (0, lines * 128 - length)).reshape(lines, 128)).reshape(-1)
    n_conv, n_head = 9 * chans * chans, chans * bins
    conv_grad = sums[:n_conv].reshape(3, 3, chans, chans)
    head_grad = sums[n_conv : n_conv + n_head].reshape(chans, bins)
    bias_grad = sums[n_conv + n_head : n_conv + n_head + bins]
    loss = sums[n_conv + n_head + bins] / count
    grad_padded = widen(lower_gradient)
    back = taps_product(grad_padded, conv_weight, rows, cols, True)
    slope = jnp.where(feat32 > 0, 1.0, jnp.exp(feat32))
    grad_features = (grad_mixed + slope * back).astype(jnp.bfloat16)
    return (loss, grad_features, conv_grad, head_grad, bias_grad)


def solution(mesh):
    placed = (P("row", "col", None), P(), P(), P(), P("row", "col"), P("row", "col"))
    return jax.shard_map(
        per_device,
        mesh=mesh,
        in_specs=placed,
        out_specs=(P(), P("row", "col", None), P(), P(), P()),
        check_vma=False,
    )
```

```python
import jax
import jax.numpy as jnp
from jax import lax
from jax.experimental import pallas as pl
from jax.experimental.pallas import tpu as pltpu
from jax.sharding import PartitionSpec as P

STEP = 8
GRID = ("row", "col")
F32, BF16 = jnp.float32, jnp.bfloat16
LANES = 128
FAR_BELOW = -1e30
VMEM = pl.BlockSpec(memory_space=pltpu.VMEM)
SMEM = pl.BlockSpec(memory_space=pltpu.SMEM)


def run(body, outs, args, scratch=(), scalars=0, micros=3):
    return pl.pallas_call(
        body,
        out_shape=outs,
        in_specs=[SMEM] * scalars + [VMEM] * (len(args) - scalars),
        out_specs=[VMEM] * len(outs),
        scratch_shapes=list(scratch),
        compiler_params=pltpu.CompilerParams(vmem_limit_bytes=48 * 1024 * 1024),
        cost_estimate=pl.CostEstimate(
            flops=0, bytes_accessed=int(micros * 3.6e6), transcendentals=0
        ),
    )(*args)


def shape(dims, kind):
    return jax.ShapeDtypeStruct(dims, kind)


def send(block, target):
    nrow, ncol = lax.axis_size("row"), lax.axis_size("col")
    pairs = []
    for r in range(nrow):
        for c in range(ncol):
            r2, c2 = target(r, c)
            pairs.append((r * ncol + c, r2 * ncol + c2))
    return lax.ppermute(block, GRID, pairs)


def shifted(block, axis, forward):
    count = lax.axis_size(axis)
    pairs = [(i, i + 1) for i in range(count - 1)]
    return lax.ppermute(block, axis, pairs if forward else [(b, a) for a, b in pairs])


def activate_kernel(feat, act, top, bottom):
    rows = feat.shape[0]

    def step(i, carry):
        v = feat[i].astype(F32)
        near = v * (1.0 + v * (0.5 + v * (1.0 / 6.0 + v * (1.0 / 24.0))))
        low = jnp.where(v > -0.03, near, jnp.exp(jnp.minimum(v, 0.0)) - 1.0)
        act[i] = jnp.where(v > 0, v, low).astype(BF16)
        return carry

    lax.fori_loop(0, rows, step, 0)
    top[...] = act[:STEP]
    bottom[...] = act[rows - STEP :]


def row_of(own, up, down, at):
    rows = own.shape[0]
    if at < STEP:
        return up[at]
    if at < STEP + rows:
        return own[at - STEP]
    return down[at - STEP - rows]


def pack_kernel(own, up, down, first, last):
    chans = own.shape[1]
    lane = lax.broadcasted_iota(jnp.int32, (chans, LANES), 1) // STEP
    for group in range(first.shape[0]):
        low = jnp.zeros((chans, LANES), F32)
        high = jnp.zeros((chans, LANES), F32)
        for slot in range(16):
            x = row_of(own, up, down, group * 16 + slot).astype(F32)
            here = lane == slot
            low = jnp.where(here, pltpu.roll(x, (STEP * slot) % LANES, 1), low)
            high = jnp.where(here, pltpu.roll(x, (STEP * slot + STEP) % LANES, 1), high)
        first[group] = low.astype(BF16)
        last[group] = high.astype(BF16)


def spread_columns(own, up, down, left, right, wide):
    chans = own.shape[1]
    lane = lax.broadcasted_iota(jnp.int32, (chans, LANES), 1)
    for group in range(left.shape[0]):
        from_left = left[group].astype(F32)
        from_right = right[group].astype(F32)
        for slot in range(16):
            at = group * 16 + slot
            middle = row_of(own, up, down, at)
            x = middle.astype(F32)
            before = jnp.where(
                lane < STEP,
                pltpu.roll(from_left, (LANES - STEP * slot) % LANES, 1),
                pltpu.roll(x, STEP, 1),
            )
            after = jnp.where(
                lane >= LANES - STEP,
                pltpu.roll(from_right, (2 * LANES - STEP - STEP * slot) % LANES, 1),
                pltpu.roll(x, LANES - STEP, 1),
            )
            wide[at, 0:chans] = before.astype(BF16)
            wide[at, chans : 2 * chans] = middle
            wide[at, 2 * chans : 3 * chans] = after.astype(BF16)


def windows(wide, i):
    return jnp.concatenate([wide[i], wide[i + STEP], wide[i + 2 * STEP]], axis=0)


def pair_windows(wide, i):
    return jnp.concatenate([windows(wide, i), windows(wide, i + 1)], axis=1)


def forward_kernel(
    place, act, up, down, left, right, feat, weight, labels, valid,
    wide, mixed, pay0, pay1, pay2, pay3, turned,
):
    rows, chans = act.shape[0], act.shape[1]
    part = rows
    pays = (pay0, pay1, pay2, pay3)
    spread_columns(act, up, down, left, right, wide)
    kernel = weight[...].astype(F32).T.astype(BF16)

    def step(p, carry):
        i = 2 * p
        out = jnp.dot(kernel, pair_windows(wide, i), preferred_element_type=F32)
        for d in range(2):
            total = feat[i + d].astype(F32) + out[:, d * LANES : (d + 1) * LANES]
            low = total.astype(BF16)
            mixed[i + d] = low
            turned[pl.ds(pl.multiple_of((i + d) * LANES, LANES), LANES), :] = low.astype(F32).T
        return carry

    lax.fori_loop(0, rows // 2, step, 0)
    turned[rows * LANES :, :] = jnp.concatenate(
        [labels[...].astype(F32).T, valid[...].astype(F32).T], axis=1
    )
    half = part // 2

    def pack(j, carry):
        for s in range(4):
            base = j * LANES + (place[0] ^ s) * part
            low = turned[pl.ds(pl.multiple_of(base, 16), half), :]
            high = turned[pl.ds(pl.multiple_of(base + half, 16), half), :]
            pays[s][pl.ds(pl.multiple_of(j * half, 16), half), :] = jnp.concatenate(
                [low, high], axis=1
            ).astype(BF16)
        return carry

    lax.fori_loop(0, rows + 1, pack, 0)


def softmax_kernel(
    place, got0, got1, got2, got3, mixed, head, labels, valid,
    grad, head_sum, bias_sum, loss_sum, cells, lab, lab_t, val, val_t,
):
    rows, chans = mixed.shape[0], mixed.shape[1]
    bins = head.shape[0]
    half = rows // 2
    size = rows * half
    lab[...] = labels[...].astype(F32)
    val[...] = valid[...].astype(F32)
    notes = []
    for s, got in enumerate((got0, got1, got2, got3)):
        q = place[0] ^ s
        cells[pl.ds(pl.multiple_of(q * size, size), size), :] = got[:size, :].astype(F32)
        cells[pl.ds(pl.multiple_of(4 * size + q * half, half), half), :] = got[size:, :].astype(F32)
    notes = [cells[4 * size + q * half : 4 * size + (q + 1) * half, :] for q in range(4)]
    for top in range(2):
        base = top * 2 * rows
        lab_t[top * half : (top + 1) * half, :] = jnp.concatenate(
            [n[:, base : base + rows] for n in notes], axis=1
        )
        val_t[top * half : (top + 1) * half, :] = jnp.concatenate(
            [n[:, base + rows : base + 2 * rows] for n in notes], axis=1
        )
    lane = lax.broadcasted_iota(jnp.int32, (bins, LANES), 1)
    plain = jnp.where(lane < chans, head[...], 0.0)
    both = jnp.concatenate([plain, pltpu.roll(plain, chans, 1)], axis=0).astype(BF16)
    single = plain[:, :chans]
    thrice = jnp.concatenate([single, single, single], axis=0).T.astype(BF16)
    single = single.astype(BF16)
    bias = head[:, chans : chans + 1]
    bin_ids = lax.broadcasted_iota(jnp.int32, (bins, LANES), 0).astype(F32)
    head_sum[...] = jnp.zeros_like(head_sum)
    bias_sum[...] = jnp.zeros_like(bias_sum)
    loss_sum[...] = jnp.zeros_like(loss_sum)

    def step(i, carry):
        other = cells[pl.ds(i, LANES, stride=half), :].astype(BF16)
        logits_t = lax.dot_general(both, other, (((1,), (1,)), ((), ())), preferred_element_type=F32)
        pair = jnp.concatenate([mixed[i], mixed[i + half]], axis=1)
        logits = jnp.dot(single, pair, preferred_element_type=F32)
        pieces = []
        for d in range(2):
            at = pl.ds(i + d * half, 1)
            own = logits[:, d * LANES : (d + 1) * LANES] + bias
            far = logits_t[d * bins : (d + 1) * bins] + bias
            sym = 0.5 * (own + far)
            peak = jnp.max(sym, axis=0, keepdims=True)
            raised = jnp.exp(sym - peak)
            total = jnp.sum(raised, axis=0, keepdims=True)
            lse = peak + jnp.log(total)
            hot = bin_ids == lab[at, :]
            hot_t = bin_ids == lab_t[at, :]
            mask, mask_t = val[at, :], val_t[at, :]
            picked = jnp.sum(jnp.where(hot, sym, 0.0), axis=0, keepdims=True)
            loss_sum[...] += mask * (lse - picked)
            share = raised * ((mask + mask_t) / total)
            pieces.append(share - jnp.where(hot, mask, 0.0) - jnp.where(hot_t, mask_t, 0.0))
        bias_sum[...] += pieces[0] + pieces[1]
        g = jnp.concatenate(pieces, axis=1)
        first = g.astype(BF16).astype(F32)
        rest = g - first
        second = rest.astype(BF16).astype(F32)
        split = jnp.concatenate([first, second, rest - second], axis=0).astype(BF16)
        out = jnp.dot(thrice, split, preferred_element_type=F32)
        grad[i] = out[:, :LANES]
        grad[i + half] = out[:, LANES:]
        head_sum[...] += lax.dot_general(
            split, pair, (((1,), (1,)), ((), ())), preferred_element_type=F32
        )
        return carry

    lax.fori_loop(0, half, step, 0)


def scale_of(count):
    return 0.5 / jnp.maximum(count[0:1, 0:1], 1.0)


def kernel_grad_kernel(
    place, count, grad, wide, head_sum, bias_sum, loss_sum,
    low, top, bottom, out0, out1, out2, out3, total, sheet,
):
    rows, chans = grad.shape[0], grad.shape[1]
    bins = bias_sum.shape[0]
    scale = scale_of(count)
    total[...] = jnp.zeros_like(total)

    def step(p, carry):
        i = 2 * p
        a = (grad[i] * scale).astype(BF16)
        b = (grad[i + 1] * scale).astype(BF16)
        low[i] = a
        low[i + 1] = b
        total[...] += lax.dot_general(
            pair_windows(wide, i),
            jnp.concatenate([a, b], axis=1),
            (((1,), (1,)), ((), ())),
            preferred_element_type=F32,
        )
        return carry

    lax.fori_loop(0, rows // 2, step, 0)
    top[...] = low[:STEP]
    bottom[...] = low[rows - STEP :]
    half = total.shape[0] // 2
    sheet[...] = jnp.zeros_like(sheet)
    sheet[:half, :] = jnp.concatenate([total[:half], total[half:]], axis=1)
    h = (head_sum[:bins] + head_sum[bins : 2 * bins] + head_sum[2 * bins :]) * scale
    b = jnp.sum(bias_sum[...], axis=1, keepdims=True) * scale
    loss = jnp.sum(loss_sum[...], axis=1, keepdims=True)
    lane = lax.broadcasted_iota(jnp.int32, (bins, chans), 1)
    extra = jnp.where(lane == 0, b, jnp.where(lane == 1, loss, 0.0))
    sheet[half : half + bins, :] = jnp.concatenate([h, extra], axis=1)
    quarter = sheet.shape[0] // 4
    for s, out in enumerate((out0, out1, out2, out3)):
        out[...] = sheet[pl.ds(pl.multiple_of((place[0] ^ s) * quarter, 8), quarter), :]


def backward_kernel(count, low, up, down, left, right, grad, feat, weight, out, wide):
    rows, chans = grad.shape[0], grad.shape[1]
    scale = scale_of(count)
    spread_columns(low, up, down, left, right, wide)
    taps = weight.shape[0] // chans
    kernel = jnp.concatenate(
        [weight[(taps - 1 - t) * chans : (taps - t) * chans, :].astype(F32) for t in range(taps)],
        axis=1,
    ).astype(BF16)

    def step(p, carry):
        i = 2 * p
        back = jnp.dot(kernel, pair_windows(wide, i), preferred_element_type=F32)
        for d in range(2):
            v = feat[i + d].astype(F32)
            slope = jnp.where(v > 0, 1.0, jnp.exp(jnp.minimum(v, 0.0)))
            out[i + d] = (
                grad[i + d] * scale + slope * back[:, d * LANES : (d + 1) * LANES]
            ).astype(BF16)
        return carry

    lax.fori_loop(0, rows // 2, step, 0)


def finish_kernel(place, got0, got1, got2, got3, kernel_grad, tail, sheet):
    quarter = got0.shape[0]
    for s, got in enumerate((got0, got1, got2, got3)):
        sheet[pl.ds(pl.multiple_of((place[0] ^ s) * quarter, 8), quarter), :] = got[...]
    half, chans = kernel_grad.shape[0] // 2, kernel_grad.shape[1]
    kernel_grad[:half, :] = sheet[:half, :chans]
    kernel_grad[half:, :] = sheet[:half, chans:]
    tail[...] = sheet[half : half + tail.shape[0], :]


def borders(own, top, bottom):
    rows, chans, _ = own.shape
    up = shifted(bottom, "row", True)
    down = shifted(top, "row", False)
    groups = (rows + 2 * STEP) // 16
    first, last = run(
        pack_kernel, [shape((groups, chans, LANES), BF16)] * 2, (own, up, down), micros=1
    )
    left = shifted(last, "col", True)
    right = shifted(first, "col", False)
    return up, down, left, right


def partners(stage):
    if stage < 2:
        return lambda m: lambda r, c: (r ^ (m << (2 * stage)), c)
    if stage == 2:
        return lambda m: lambda r, c: (r ^ ((m & 1) << 4), c ^ (m >> 1))
    return lambda m: lambda r, c: (r, c ^ (m << 1))


def total_small(value):
    for bit in range(5):
        value = value + send(value, lambda r, c: (r ^ (1 << bit), c))
    for bit in range(3):
        value = value + send(value, lambda r, c: (r, c ^ (1 << bit)))
    return value


def total_quarters(quarters):
    near = partners(0)
    a, b, c, d = quarters
    part = (a + send(b, near(1))) + (send(c, near(2)) + send(d, near(3)))
    for stage in (1, 2, 3):
        to = partners(stage)
        part = (part + send(part, to(1))) + (send(part, to(2)) + send(part, to(3)))
    return [part] + [send(part, near(m)) for m in (1, 2, 3)]


def per_device(features, conv_weight, head_weight, head_bias, labels, valid):
    rows, cols, chans = features.shape
    bins = head_weight.shape[1]
    parts = cols // rows
    place = (lax.axis_index("row") % parts).astype(jnp.int32).reshape(1)
    feat = features.transpose(0, 2, 1)
    weight = conv_weight.reshape(-1, chans)
    tall = -(-bins // 8) * 8
    head = jnp.concatenate(
        [
            jnp.pad(head_weight.T.astype(F32), ((0, tall - bins), (0, 0))),
            jnp.pad(head_bias, (0, tall - bins), constant_values=FAR_BELOW)[:, None],
            jnp.zeros((tall, LANES - chans - 1), F32),
        ],
        axis=1,
    )
    counted = jnp.full((8, LANES), jnp.sum(valid.astype(F32)))
    tile = (rows, chans, LANES)
    edge = (STEP, chans, LANES)
    act, top, bottom = run(
        activate_kernel, [shape(tile, BF16), shape(edge, BF16), shape(edge, BF16)], (feat,), micros=1
    )
    around = borders(act, top, bottom)
    count = total_small(counted)
    length = (rows + 1) * rows // 2
    wide, mixed, *pays = run(
        forward_kernel,
        [shape((rows + 2 * STEP, 3 * chans, LANES), BF16), shape(tile, BF16)]
        + [shape((length, LANES), BF16)] * 4,
        (place, act, *around, feat, weight, labels, valid),
        scratch=[pltpu.VMEM(((rows + 1) * LANES, chans), F32)],
        scalars=1,
        micros=5,
    )
    got = [
        send(pays[s], lambda r, c: (parts * c + (r % parts ^ s), r // parts)) for s in range(parts)
    ]
    grad, head_sum, bias_sum, loss_sum = run(
        softmax_kernel,
        [
            shape(tile, F32),
            shape((3 * tall, chans), F32),
            shape((tall, LANES), F32),
            shape((1, LANES), F32),
        ],
        (place, *got, mixed, head, labels, valid),
        scratch=[pltpu.VMEM((length * 4, LANES), F32)] + [pltpu.VMEM((rows, LANES), F32)] * 4,
        scalars=1,
        micros=5,
    )
    half = 9 * chans // 2
    lines = -(-(half + tall) // 32) * 32
    low, top, bottom, *quarters = run(
        kernel_grad_kernel,
        [shape(tile, BF16), shape(edge, BF16), shape(edge, BF16)]
        + [shape((lines // 4, LANES), F32)] * 4,
        (place, count, grad, wide, head_sum, bias_sum, loss_sum),
        scratch=[pltpu.VMEM((9 * chans, chans), F32), pltpu.VMEM((lines, LANES), F32)],
        scalars=1,
        micros=3,
    )
    sums = total_quarters(quarters)
    around = borders(low, top, bottom)
    (grad_features,) = run(
        backward_kernel,
        [shape(tile, BF16)],
        (count, low, *around, grad, feat, weight),
        scratch=[pltpu.VMEM((rows + 2 * STEP, 3 * chans, LANES), BF16)],
        micros=4,
    )
    kernel_grad, tail = run(
        finish_kernel,
        [shape((9 * chans, chans), F32), shape((tall, LANES), F32)],
        (place, *sums),
        scratch=[pltpu.VMEM((lines, LANES), F32)],
        scalars=1,
        micros=1,
    )
    loss = tail[0, chans + 1] / jnp.maximum(count[0, 0], 1.0)
    return (
        loss,
        grad_features.transpose(0, 2, 1),
        kernel_grad.reshape(conv_weight.shape),
        tail[:bins, :chans].T,
        tail[:bins, chans],
    )


def solution(mesh):
    placed = (P("row", "col", None), P(), P(), P(), P("row", "col"), P("row", "col"))
    return jax.shard_map(
        per_device,
        mesh=mesh,
        in_specs=placed,
        out_specs=(P(), P("row", "col", None), P(), P(), P()),
        check_vma=False,
    )
```

```python
import jax
import jax.numpy as jnp
from jax import lax
from jax.experimental import pallas as pl
from jax.experimental.pallas import tpu as pltpu
from jax.sharding import PartitionSpec as P

STEP = 8
GRID = ("row", "col")
F32, BF16 = jnp.float32, jnp.bfloat16
LANES = 128
FAR_BELOW = -1e30
VMEM = pl.BlockSpec(memory_space=pltpu.VMEM)
SMEM = pl.BlockSpec(memory_space=pltpu.SMEM)


def run(body, outs, args, scratch=(), scalars=0, micros=3):
    return pl.pallas_call(
        body,
        out_shape=outs,
        in_specs=[SMEM] * scalars + [VMEM] * (len(args) - scalars),
        out_specs=[VMEM] * len(outs),
        scratch_shapes=list(scratch),
        compiler_params=pltpu.CompilerParams(vmem_limit_bytes=48 * 1024 * 1024),
        cost_estimate=pl.CostEstimate(
            flops=0, bytes_accessed=int(micros * 3.6e6), transcendentals=0
        ),
    )(*args)


def shape(dims, kind):
    return jax.ShapeDtypeStruct(dims, kind)


def send(block, target):
    nrow, ncol = lax.axis_size("row"), lax.axis_size("col")
    pairs = []
    for r in range(nrow):
        for c in range(ncol):
            r2, c2 = target(r, c)
            pairs.append((r * ncol + c, r2 * ncol + c2))
    return lax.ppermute(block, GRID, pairs)


def shifted(block, axis, forward):
    count = lax.axis_size(axis)
    pairs = [(i, i + 1) for i in range(count - 1)]
    return lax.ppermute(block, axis, pairs if forward else [(b, a) for a, b in pairs])


def activate_kernel(feat, act, top, bottom):
    rows = feat.shape[0]

    def step(i, carry):
        v = feat[i].astype(F32)
        near = v * (1.0 + v * (0.5 + v * (1.0 / 6.0 + v * (1.0 / 24.0))))
        low = jnp.where(v > -0.03, near, jnp.exp(jnp.minimum(v, 0.0)) - 1.0)
        act[i] = jnp.where(v > 0, v, low).astype(BF16)
        return carry

    lax.fori_loop(0, rows, step, 0)
    top[...] = act[:STEP]
    bottom[...] = act[rows - STEP :]


def row_of(own, up, down, at):
    rows = own.shape[0]
    if at < STEP:
        return up[at]
    if at < STEP + rows:
        return own[at - STEP]
    return down[at - STEP - rows]


def pack_kernel(own, up, down, first, last):
    chans = own.shape[1]
    lane = lax.broadcasted_iota(jnp.int32, (chans, LANES), 1) // STEP
    for group in range(first.shape[0]):
        low = jnp.zeros((chans, LANES), F32)
        high = jnp.zeros((chans, LANES), F32)
        for slot in range(16):
            x = row_of(own, up, down, group * 16 + slot).astype(F32)
            here = lane == slot
            low = jnp.where(here, pltpu.roll(x, (STEP * slot) % LANES, 1), low)
            high = jnp.where(here, pltpu.roll(x, (STEP * slot + STEP) % LANES, 1), high)
        first[group] = low.astype(BF16)
        last[group] = high.astype(BF16)


def spread_columns(own, up, down, left, right, wide):
    chans = own.shape[1]
    lane = lax.broadcasted_iota(jnp.int32, (chans, LANES), 1)
    for group in range(left.shape[0]):
        from_left = left[group].astype(F32)
        from_right = right[group].astype(F32)
        for slot in range(16):
            at = group * 16 + slot
            middle = row_of(own, up, down, at)
            x = middle.astype(F32)
            before = jnp.where(
                lane < STEP,
                pltpu.roll(from_left, (LANES - STEP * slot) % LANES, 1),
                pltpu.roll(x, STEP, 1),
            )
            after = jnp.where(
                lane >= LANES - STEP,
                pltpu.roll(from_right, (2 * LANES - STEP - STEP * slot) % LANES, 1),
                pltpu.roll(x, LANES - STEP, 1),
            )
            wide[at, 0:chans] = before.astype(BF16)
            wide[at, chans : 2 * chans] = middle
            wide[at, 2 * chans : 3 * chans] = after.astype(BF16)


def windows(wide, i):
    return jnp.concatenate([wide[i], wide[i + STEP], wide[i + 2 * STEP]], axis=0)


def pair_windows(wide, i):
    return jnp.concatenate([windows(wide, i), windows(wide, i + 1)], axis=1)


def forward_kernel(
    place, act, up, down, left, right, feat, weight, labels, valid,
    wide, mixed, pay0, pay1, pay2, pay3, turned,
):
    rows, chans = act.shape[0], act.shape[1]
    part = rows
    pays = (pay0, pay1, pay2, pay3)
    spread_columns(act, up, down, left, right, wide)
    kernel = weight[...].astype(F32).T.astype(BF16)

    def step(p, carry):
        i = 2 * p
        out = jnp.dot(kernel, pair_windows(wide, i), preferred_element_type=F32)
        for d in range(2):
            total = feat[i + d].astype(F32) + out[:, d * LANES : (d + 1) * LANES]
            low = total.astype(BF16)
            mixed[i + d] = low
            turned[pl.ds(pl.multiple_of((i + d) * LANES, LANES), LANES), :] = low.astype(F32).T
        return carry

    lax.fori_loop(0, rows // 2, step, 0)
    turned[rows * LANES :, :] = jnp.concatenate(
        [labels[...].astype(F32).T, valid[...].astype(F32).T], axis=1
    )
    half = part // 2

    def pack(j, carry):
        for s in range(4):
            base = j * LANES + (place[0] ^ s) * part
            low = turned[pl.ds(pl.multiple_of(base, 16), half), :]
            high = turned[pl.ds(pl.multiple_of(base + half, 16), half), :]
            pays[s][pl.ds(pl.multiple_of(j * half, 16), half), :] = jnp.concatenate(
                [low, high], axis=1
            ).astype(BF16)
        return carry

    lax.fori_loop(0, rows + 1, pack, 0)


def softmax_kernel(
    place, got0, got1, got2, got3, mixed, head, labels, valid,
    grad, head_sum, bias_sum, loss_sum, cells, lab, lab_t, val, val_t,
):
    rows, chans = mixed.shape[0], mixed.shape[1]
    bins = head.shape[0]
    half = rows // 2
    size = rows * half
    lab[...] = labels[...].astype(F32)
    val[...] = valid[...].astype(F32)
    notes = []
    for s, got in enumerate((got0, got1, got2, got3)):
        q = place[0] ^ s
        cells[pl.ds(pl.multiple_of(q * size, size), size), :] = got[:size, :].astype(F32)
        cells[pl.ds(pl.multiple_of(4 * size + q * half, half), half), :] = got[size:, :].astype(F32)
    notes = [cells[4 * size + q * half : 4 * size + (q + 1) * half, :] for q in range(4)]
    for top in range(2):
        base = top * 2 * rows
        lab_t[top * half : (top + 1) * half, :] = jnp.concatenate(
            [n[:, base : base + rows] for n in notes], axis=1
        )
        val_t[top * half : (top + 1) * half, :] = jnp.concatenate(
            [n[:, base + rows : base + 2 * rows] for n in notes], axis=1
        )
    lane = lax.broadcasted_iota(jnp.int32, (bins, LANES), 1)
    plain = jnp.where(lane < chans, head[...], 0.0)
    both = jnp.concatenate([plain, pltpu.roll(plain, chans, 1)], axis=0).astype(BF16)
    single = plain[:, :chans]
    thrice = jnp.concatenate([single, single, single], axis=0).T.astype(BF16)
    single = single.astype(BF16)
    bias = head[:, chans : chans + 1]
    bin_ids = lax.broadcasted_iota(jnp.int32, (bins, LANES), 0).astype(F32)
    head_sum[...] = jnp.zeros_like(head_sum)
    bias_sum[...] = jnp.zeros_like(bias_sum)
    loss_sum[...] = jnp.zeros_like(loss_sum)

    def step(i, carry):
        other = cells[pl.ds(i, LANES, stride=half), :].astype(BF16)
        logits_t = lax.dot_general(both, other, (((1,), (1,)), ((), ())), preferred_element_type=F32)
        pair = jnp.concatenate([mixed[i], mixed[i + half]], axis=1)
        logits = jnp.dot(single, pair, preferred_element_type=F32)
        pieces = []
        for d in range(2):
            at = pl.ds(i + d * half, 1)
            own = logits[:, d * LANES : (d + 1) * LANES] + bias
            far = logits_t[d * bins : (d + 1) * bins] + bias
            sym = 0.5 * (own + far)
            peak = jnp.max(sym, axis=0, keepdims=True)
            raised = jnp.exp(sym - peak)
            total = jnp.sum(raised, axis=0, keepdims=True)
            lse = peak + jnp.log(total)
            hot = bin_ids == lab[at, :]
            hot_t = bin_ids == lab_t[at, :]
            mask, mask_t = val[at, :], val_t[at, :]
            picked = jnp.sum(jnp.where(hot, sym, 0.0), axis=0, keepdims=True)
            loss_sum[...] += mask * (lse - picked)
            share = raised * ((mask + mask_t) / total)
            pieces.append(share - jnp.where(hot, mask, 0.0) - jnp.where(hot_t, mask_t, 0.0))
        bias_sum[...] += pieces[0] + pieces[1]
        g = jnp.concatenate(pieces, axis=1)
        first = g.astype(BF16).astype(F32)
        rest = g - first
        second = rest.astype(BF16).astype(F32)
        split = jnp.concatenate([first, second, rest - second], axis=0).astype(BF16)
        out = jnp.dot(thrice, split, preferred_element_type=F32)
        grad[i] = out[:, :LANES]
        grad[i + half] = out[:, LANES:]
        head_sum[...] += lax.dot_general(
            split, pair, (((1,), (1,)), ((), ())), preferred_element_type=F32
        )
        return carry

    lax.fori_loop(0, half, step, 0)


def scale_of(count):
    return 0.5 / jnp.maximum(count[0:1, 0:1], 1.0)


def kernel_grad_kernel(
    place, count, grad, wide, head_sum, bias_sum, loss_sum,
    low, top, bottom, out0, out1, out2, out3, total, sheet,
):
    rows, chans = grad.shape[0], grad.shape[1]
    bins = bias_sum.shape[0]
    scale = scale_of(count)
    total[...] = jnp.zeros_like(total)

    def step(p, carry):
        i = 2 * p
        a = (grad[i] * scale).astype(BF16)
        b = (grad[i + 1] * scale).astype(BF16)
        low[i] = a
        low[i + 1] = b
        total[...] += lax.dot_general(
            pair_windows(wide, i),
            jnp.concatenate([a, b], axis=1),
            (((1,), (1,)), ((), ())),
            preferred_element_type=F32,
        )
        return carry

    lax.fori_loop(0, rows // 2, step, 0)
    top[...] = low[:STEP]
    bottom[...] = low[rows - STEP :]
    half = total.shape[0] // 2
    sheet[...] = jnp.zeros_like(sheet)
    sheet[:half, :] = jnp.concatenate([total[:half], total[half:]], axis=1)
    h = (head_sum[:bins] + head_sum[bins : 2 * bins] + head_sum[2 * bins :]) * scale
    b = jnp.sum(bias_sum[...], axis=1, keepdims=True) * scale
    loss = jnp.sum(loss_sum[...], axis=1, keepdims=True)
    lane = lax.broadcasted_iota(jnp.int32, (bins, chans), 1)
    extra = jnp.where(lane == 0, b, jnp.where(lane == 1, loss, 0.0))
    sheet[half : half + bins, :] = jnp.concatenate([h, extra], axis=1)
    quarter = sheet.shape[0] // 4
    for s, out in enumerate((out0, out1, out2, out3)):
        out[...] = sheet[pl.ds(pl.multiple_of((place[0] ^ s) * quarter, 8), quarter), :]


def backward_kernel(count, low, up, down, left, right, grad, feat, weight, out, wide):
    rows, chans = grad.shape[0], grad.shape[1]
    scale = scale_of(count)
    spread_columns(low, up, down, left, right, wide)
    taps = weight.shape[0] // chans
    kernel = jnp.concatenate(
        [weight[(taps - 1 - t) * chans : (taps - t) * chans, :].astype(F32) for t in range(taps)],
        axis=1,
    ).astype(BF16)

    def step(p, carry):
        i = 2 * p
        back = jnp.dot(kernel, pair_windows(wide, i), preferred_element_type=F32)
        for d in range(2):
            v = feat[i + d].astype(F32)
            slope = jnp.where(v > 0, 1.0, jnp.exp(jnp.minimum(v, 0.0)))
            out[i + d] = (
                grad[i + d] * scale + slope * back[:, d * LANES : (d + 1) * LANES]
            ).astype(BF16)
        return carry

    lax.fori_loop(0, rows // 2, step, 0)


def finish_kernel(place, got0, got1, got2, got3, kernel_grad, tail, sheet):
    quarter = got0.shape[0]
    for s, got in enumerate((got0, got1, got2, got3)):
        sheet[pl.ds(pl.multiple_of((place[0] ^ s) * quarter, 8), quarter), :] = got[...]
    half, chans = kernel_grad.shape[0] // 2, kernel_grad.shape[1]
    kernel_grad[:half, :] = sheet[:half, :chans]
    kernel_grad[half:, :] = sheet[:half, chans:]
    tail[...] = sheet[half : half + tail.shape[0], :]


def borders(own, top, bottom):
    rows, chans, _ = own.shape
    up = shifted(bottom, "row", True)
    down = shifted(top, "row", False)
    groups = (rows + 2 * STEP) // 16
    first, last = run(
        pack_kernel, [shape((groups, chans, LANES), BF16)] * 2, (own, up, down), micros=1
    )
    left = shifted(last, "col", True)
    right = shifted(first, "col", False)
    return up, down, left, right


def partners(stage):
    if stage < 2:
        return lambda m: lambda r, c: (r ^ (m << (2 * stage)), c)
    if stage == 2:
        return lambda m: lambda r, c: (r ^ ((m & 1) << 4), c ^ (m >> 1))
    return lambda m: lambda r, c: (r, c ^ (m << 1))


def total_small(value):
    for bit in range(5):
        value = value + send(value, lambda r, c: (r ^ (1 << bit), c))
    for bit in range(3):
        value = value + send(value, lambda r, c: (r, c ^ (1 << bit)))
    return value


def total_quarters(quarters):
    near = partners(0)
    a, b, c, d = quarters
    part = (a + send(b, near(1))) + (send(c, near(2)) + send(d, near(3)))
    for stage in (1, 2, 3):
        to = partners(stage)
        part = (part + send(part, to(1))) + (send(part, to(2)) + send(part, to(3)))
    return [part] + [send(part, near(m)) for m in (1, 2, 3)]


def per_device(features, conv_weight, head_weight, head_bias, labels, valid):
    rows, cols, chans = features.shape
    bins = head_weight.shape[1]
    parts = cols // rows
    place = (lax.axis_index("row") % parts).astype(jnp.int32).reshape(1)
    feat = features.transpose(0, 2, 1)
    weight = conv_weight.reshape(-1, chans)
    tall = -(-bins // 8) * 8
    head = jnp.concatenate(
        [
            jnp.pad(head_weight.T.astype(F32), ((0, tall - bins), (0, 0))),
            jnp.pad(head_bias, (0, tall - bins), constant_values=FAR_BELOW)[:, None],
            jnp.zeros((tall, LANES - chans - 1), F32),
        ],
        axis=1,
    )
    turns = jnp.where(labels[0, 0] >= 0, 1, 0).astype(jnp.int32)
    counted = jnp.full((8, LANES), jnp.sum(valid.astype(F32)))
    tile = (rows, chans, LANES)
    edge = (STEP, chans, LANES)
    act, top, bottom = run(
        activate_kernel, [shape(tile, BF16), shape(edge, BF16), shape(edge, BF16)], (feat,), micros=1
    )
    around = borders(act, top, bottom)
    length = (rows + 1) * rows // 2
    wide, mixed, *pays = run(
        forward_kernel,
        [shape((rows + 2 * STEP, 3 * chans, LANES), BF16), shape(tile, BF16)]
        + [shape((length, LANES), BF16)] * 4,
        (place, act, *around, feat, weight, labels, valid),
        scratch=[pltpu.VMEM(((rows + 1) * LANES, chans), F32)],
        scalars=1,
        micros=5,
    )
    got = [
        send(pays[s], lambda r, c: (parts * c + (r % parts ^ s), r // parts)) for s in range(parts)
    ]
    counted, mixed = lax.optimization_barrier((counted, mixed))
    count = lax.while_loop(
        lambda state: state[0] < turns,
        lambda state: (state[0] + 1, total_small(state[1])),
        (jnp.int32(0), counted),
    )[1]
    got, count = lax.optimization_barrier((got, count))
    grad, head_sum, bias_sum, loss_sum = run(
        softmax_kernel,
        [
            shape(tile, F32),
            shape((3 * tall, chans), F32),
            shape((tall, LANES), F32),
            shape((1, LANES), F32),
        ],
        (place, *got, mixed, head, labels, valid),
        scratch=[pltpu.VMEM((length * 4, LANES), F32)] + [pltpu.VMEM((rows, LANES), F32)] * 4,
        scalars=1,
        micros=5,
    )
    half = 9 * chans // 2
    lines = -(-(half + tall) // 32) * 32
    low, top, bottom, *quarters = run(
        kernel_grad_kernel,
        [shape(tile, BF16), shape(edge, BF16), shape(edge, BF16)]
        + [shape((lines // 4, LANES), F32)] * 4,
        (place, count, grad, wide, head_sum, bias_sum, loss_sum),
        scratch=[pltpu.VMEM((9 * chans, chans), F32), pltpu.VMEM((lines, LANES), F32)],
        scalars=1,
        micros=3,
    )
    sums = total_quarters(quarters)
    around = borders(low, top, bottom)
    (grad_features,) = run(
        backward_kernel,
        [shape(tile, BF16)],
        (count, low, *around, grad, feat, weight),
        scratch=[pltpu.VMEM((rows + 2 * STEP, 3 * chans, LANES), BF16)],
        micros=4,
    )
    kernel_grad, tail = run(
        finish_kernel,
        [shape((9 * chans, chans), F32), shape((tall, LANES), F32)],
        (place, *sums),
        scratch=[pltpu.VMEM((lines, LANES), F32)],
        scalars=1,
        micros=1,
    )
    loss = tail[0, chans + 1] / jnp.maximum(count[0, 0], 1.0)
    return (
        loss,
        grad_features.transpose(0, 2, 1),
        kernel_grad.reshape(conv_weight.shape),
        tail[:bins, :chans].T,
        tail[:bins, chans],
    )


def solution(mesh):
    placed = (P("row", "col", None), P(), P(), P(), P("row", "col"), P("row", "col"))
    return jax.shard_map(
        per_device,
        mesh=mesh,
        in_specs=placed,
        out_specs=(P(), P("row", "col", None), P(), P(), P()),
        check_vma=False,
    )
```

```python
import jax
import jax.numpy as jnp
from jax import lax
from jax.experimental import pallas as pl
from jax.experimental.pallas import tpu as pltpu
from jax.sharding import PartitionSpec as P

STEP = 8
GRID = ("row", "col")
F32, BF16 = jnp.float32, jnp.bfloat16
LANES = 128
FAR_BELOW = -1e30
VMEM = pl.BlockSpec(memory_space=pltpu.VMEM)
SMEM = pl.BlockSpec(memory_space=pltpu.SMEM)


def run(body, outs, args, scratch=(), scalars=0, micros=3):
    return pl.pallas_call(
        body,
        out_shape=outs,
        in_specs=[SMEM] * scalars + [VMEM] * (len(args) - scalars),
        out_specs=[VMEM] * len(outs),
        scratch_shapes=list(scratch),
        compiler_params=pltpu.CompilerParams(vmem_limit_bytes=48 * 1024 * 1024),
        cost_estimate=pl.CostEstimate(
            flops=0, bytes_accessed=int(micros * 3.6e6), transcendentals=0
        ),
    )(*args)


def shape(dims, kind):
    return jax.ShapeDtypeStruct(dims, kind)


def send(block, target):
    nrow, ncol = lax.axis_size("row"), lax.axis_size("col")
    pairs = []
    for r in range(nrow):
        for c in range(ncol):
            r2, c2 = target(r, c)
            pairs.append((r * ncol + c, r2 * ncol + c2))
    return lax.ppermute(block, GRID, pairs)


def shifted(block, axis, forward):
    count = lax.axis_size(axis)
    pairs = [(i, i + 1) for i in range(count - 1)]
    return lax.ppermute(block, axis, pairs if forward else [(b, a) for a, b in pairs])


def activate_kernel(feat, valid, act, top, bottom, counted):
    rows = feat.shape[0]

    def step(i, carry):
        v = feat[i].astype(F32)
        near = v * (1.0 + v * (0.5 + v * (1.0 / 6.0 + v * (1.0 / 24.0))))
        low = jnp.where(v > -0.03, near, jnp.exp(jnp.minimum(v, 0.0)) - 1.0)
        act[i] = jnp.where(v > 0, v, low).astype(BF16)
        return carry

    lax.fori_loop(0, rows, step, 0)
    top[...] = act[:STEP]
    bottom[...] = act[rows - STEP :]
    lines = jnp.sum(valid[...].astype(F32), axis=0, keepdims=True)
    counted[...] = jnp.broadcast_to(jnp.sum(lines, axis=1, keepdims=True), counted.shape)


def row_of(own, up, down, at):
    rows = own.shape[0]
    if at < STEP:
        return up[at]
    if at < STEP + rows:
        return own[at - STEP]
    return down[at - STEP - rows]


def pack_kernel(own, up, down, first, last):
    chans = own.shape[1]
    lane = lax.broadcasted_iota(jnp.int32, (chans, LANES), 1) // STEP
    for group in range(first.shape[0]):
        low = jnp.zeros((chans, LANES), F32)
        high = jnp.zeros((chans, LANES), F32)
        for slot in range(16):
            x = row_of(own, up, down, group * 16 + slot).astype(F32)
            here = lane == slot
            low = jnp.where(here, pltpu.roll(x, (STEP * slot) % LANES, 1), low)
            high = jnp.where(here, pltpu.roll(x, (STEP * slot + STEP) % LANES, 1), high)
        first[group] = low.astype(BF16)
        last[group] = high.astype(BF16)


def spread_columns(own, up, down, left, right, wide):
    chans = own.shape[1]
    lane = lax.broadcasted_iota(jnp.int32, (chans, LANES), 1)
    for group in range(left.shape[0]):
        from_left = left[group].astype(F32)
        from_right = right[group].astype(F32)
        for slot in range(16):
            at = group * 16 + slot
            middle = row_of(own, up, down, at)
            x = middle.astype(F32)
            before = jnp.where(
                lane < STEP,
                pltpu.roll(from_left, (LANES - STEP * slot) % LANES, 1),
                pltpu.roll(x, STEP, 1),
            )
            after = jnp.where(
                lane >= LANES - STEP,
                pltpu.roll(from_right, (2 * LANES - STEP - STEP * slot) % LANES, 1),
                pltpu.roll(x, LANES - STEP, 1),
            )
            wide[at, 0:chans] = before.astype(BF16)
            wide[at, chans : 2 * chans] = middle
            wide[at, 2 * chans : 3 * chans] = after.astype(BF16)


def windows(wide, i):
    return jnp.concatenate([wide[i], wide[i + STEP], wide[i + 2 * STEP]], axis=0)


def pair_windows(wide, i):
    return jnp.concatenate([windows(wide, i), windows(wide, i + 1)], axis=1)


def forward_kernel(
    place, act, up, down, left, right, feat, weight, labels, valid,
    wide, mixed, pay0, pay1, pay2, pay3, turned,
):
    rows, chans = act.shape[0], act.shape[1]
    part = rows
    pays = (pay0, pay1, pay2, pay3)
    spread_columns(act, up, down, left, right, wide)
    kernel = weight[...].astype(F32).T.astype(BF16)

    def step(p, carry):
        i = 2 * p
        out = jnp.dot(kernel, pair_windows(wide, i), preferred_element_type=F32)
        for d in range(2):
            total = feat[i + d].astype(F32) + out[:, d * LANES : (d + 1) * LANES]
            low = total.astype(BF16)
            mixed[i + d] = low
            turned[pl.ds(pl.multiple_of((i + d) * LANES, LANES), LANES), :] = low.astype(F32).T
        return carry

    lax.fori_loop(0, rows // 2, step, 0)
    turned[rows * LANES :, :] = jnp.concatenate(
        [labels[...].astype(F32).T, valid[...].astype(F32).T], axis=1
    )
    half = part // 2

    def pack(j, carry):
        for s in range(4):
            base = j * LANES + (place[0] ^ s) * part
            low = turned[pl.ds(pl.multiple_of(base, 16), half), :]
            high = turned[pl.ds(pl.multiple_of(base + half, 16), half), :]
            pays[s][pl.ds(pl.multiple_of(j * half, 16), half), :] = jnp.concatenate(
                [low, high], axis=1
            ).astype(BF16)
        return carry

    lax.fori_loop(0, rows + 1, pack, 0)


def softmax_kernel(
    place, got0, got1, got2, got3, mixed, head, head_bias, labels, valid,
    grad, head_sum, bias_sum, loss_sum, cells, lab, lab_t, val, val_t, padded_head,
):
    rows, chans = mixed.shape[0], mixed.shape[1]
    bins, real = padded_head.shape[0], head.shape[0]
    half = rows // 2
    size = rows * half
    for s, got in enumerate((got0, got1, got2, got3)):
        q = place[0] ^ s
        cells[pl.ds(pl.multiple_of(q * size, size), size), :] = got[:size, :].astype(F32)
        cells[pl.ds(pl.multiple_of(4 * size + q * half, half), half), :] = got[size:, :].astype(F32)
    notes = [cells[4 * size + q * half : 4 * size + (q + 1) * half, :] for q in range(4)]
    for top in range(2):
        base = top * 2 * rows
        lab_t[top * half : (top + 1) * half, :] = jnp.concatenate(
            [n[:, base : base + rows] for n in notes], axis=1
        )
        val_t[top * half : (top + 1) * half, :] = jnp.concatenate(
            [n[:, base + rows : base + 2 * rows] for n in notes], axis=1
        )
    padded_head[...] = jnp.zeros_like(padded_head)
    padded_head[:real, :] = head[...].astype(F32)
    single = padded_head[...]
    blank = jnp.zeros_like(single)
    both = jnp.concatenate(
        [jnp.concatenate([single, blank], axis=1), jnp.concatenate([blank, single], axis=1)], axis=0
    ).astype(BF16)
    thrice = jnp.concatenate([single, single, single], axis=0).T.astype(BF16)
    single = single.astype(BF16)
    line = lax.broadcasted_iota(jnp.int32, (bins, real), 0)
    across = lax.broadcasted_iota(jnp.int32, (bins, real), 1)
    bias = jnp.sum(jnp.where(line == across, head_bias[...], 0.0), axis=1, keepdims=True)
    bias = jnp.where(lax.broadcasted_iota(jnp.int32, (bins, 1), 0) < real, bias, FAR_BELOW)
    lab[...] = labels[...].astype(F32)
    val[...] = valid[...].astype(F32)
    bin_ids = lax.broadcasted_iota(jnp.int32, (bins, LANES), 0).astype(F32)
    head_sum[...] = jnp.zeros_like(head_sum)
    bias_sum[...] = jnp.zeros_like(bias_sum)
    loss_sum[...] = jnp.zeros_like(loss_sum)

    def step(i, carry):
        other = cells[pl.ds(i, LANES, stride=half), :].astype(BF16)
        logits_t = lax.dot_general(both, other, (((1,), (1,)), ((), ())), preferred_element_type=F32)
        pair = jnp.concatenate([mixed[i], mixed[i + half]], axis=1)
        logits = jnp.dot(single, pair, preferred_element_type=F32)
        pieces = []
        for d in range(2):
            at = pl.ds(i + d * half, 1)
            own = logits[:, d * LANES : (d + 1) * LANES] + bias
            far = logits_t[d * bins : (d + 1) * bins] + bias
            sym = 0.5 * (own + far)
            peak = jnp.max(sym, axis=0, keepdims=True)
            raised = jnp.exp(sym - peak)
            total = jnp.sum(raised, axis=0, keepdims=True)
            lse = peak + jnp.log(total)
            hot = bin_ids == lab[at, :]
            hot_t = bin_ids == lab_t[at, :]
            mask, mask_t = val[at, :], val_t[at, :]
            picked = jnp.sum(jnp.where(hot, sym, 0.0), axis=0, keepdims=True)
            loss_sum[...] += mask * (lse - picked)
            share = raised * ((mask + mask_t) / total)
            pieces.append(share - jnp.where(hot, mask, 0.0) - jnp.where(hot_t, mask_t, 0.0))
        bias_sum[...] += pieces[0] + pieces[1]
        g = jnp.concatenate(pieces, axis=1)
        first = g.astype(BF16).astype(F32)
        rest = g - first
        second = rest.astype(BF16).astype(F32)
        split = jnp.concatenate([first, second, rest - second], axis=0).astype(BF16)
        out = jnp.dot(thrice, split, preferred_element_type=F32)
        grad[i] = out[:, :LANES]
        grad[i + half] = out[:, LANES:]
        head_sum[...] += lax.dot_general(
            split, pair, (((1,), (1,)), ((), ())), preferred_element_type=F32
        )
        return carry

    lax.fori_loop(0, half, step, 0)


def scale_of(count):
    return 0.5 / jnp.maximum(count[0:1, 0:1], 1.0)


def kernel_grad_kernel(
    place, count, grad, wide, head_sum, bias_sum, loss_sum,
    low, top, bottom, out0, out1, out2, out3, total, sheet,
):
    rows, chans = grad.shape[0], grad.shape[1]
    bins = bias_sum.shape[0]
    scale = scale_of(count)
    total[...] = jnp.zeros_like(total)

    def step(p, carry):
        i = 2 * p
        a = (grad[i] * scale).astype(BF16)
        b = (grad[i + 1] * scale).astype(BF16)
        low[i] = a
        low[i + 1] = b
        total[...] += lax.dot_general(
            pair_windows(wide, i),
            jnp.concatenate([a, b], axis=1),
            (((1,), (1,)), ((), ())),
            preferred_element_type=F32,
        )
        return carry

    lax.fori_loop(0, rows // 2, step, 0)
    top[...] = low[:STEP]
    bottom[...] = low[rows - STEP :]
    half = total.shape[0] // 2
    sheet[...] = jnp.zeros_like(sheet)
    sheet[:half, :] = jnp.concatenate([total[:half], total[half:]], axis=1)
    h = (head_sum[:bins] + head_sum[bins : 2 * bins] + head_sum[2 * bins :]) * scale
    sheet[half : half + bins, :chans] = h
    note = half + bins
    sheet[note : note + 1, :bins] = jnp.sum(bias_sum[...].T, axis=0, keepdims=True) * scale
    sheet[note + 1 : note + 2, :1] = jnp.sum(loss_sum[...], axis=1, keepdims=True)
    quarter = sheet.shape[0] // 4
    for s, out in enumerate((out0, out1, out2, out3)):
        out[...] = sheet[pl.ds(pl.multiple_of((place[0] ^ s) * quarter, 8), quarter), :]


def backward_kernel(count, low, up, down, left, right, grad, feat, weight, out, wide):
    rows, chans = grad.shape[0], grad.shape[1]
    scale = scale_of(count)
    spread_columns(low, up, down, left, right, wide)
    taps = weight.shape[0] // chans
    kernel = jnp.concatenate(
        [weight[(taps - 1 - t) * chans : (taps - t) * chans, :].astype(F32) for t in range(taps)],
        axis=1,
    ).astype(BF16)

    def step(p, carry):
        i = 2 * p
        back = jnp.dot(kernel, pair_windows(wide, i), preferred_element_type=F32)
        for d in range(2):
            v = feat[i + d].astype(F32)
            slope = jnp.where(v > 0, 1.0, jnp.exp(jnp.minimum(v, 0.0)))
            out[i + d] = (
                grad[i + d] * scale + slope * back[:, d * LANES : (d + 1) * LANES]
            ).astype(BF16)
        return carry

    lax.fori_loop(0, rows // 2, step, 0)


def finish_kernel(
    place, count, got0, got1, got2, got3, kernel_grad, head_grad, bias_grad, loss, sheet
):
    quarter = got0.shape[0]
    for s, got in enumerate((got0, got1, got2, got3)):
        sheet[pl.ds(pl.multiple_of((place[0] ^ s) * quarter, 8), quarter), :] = got[...]
    half, chans = kernel_grad.shape[0] // 2, kernel_grad.shape[1]
    bins = head_grad.shape[0]
    kernel_grad[:half, :] = sheet[:half, :chans]
    kernel_grad[half:, :] = sheet[:half, chans:]
    head_grad[...] = sheet[half : half + bins, :chans]
    note = half + -(-bins // 8) * 8
    bias_grad[...] = sheet[note : note + 1, :bins]
    loss[...] = sheet[note + 1 : note + 2, :1] / jnp.maximum(count[0:1, 0:1], 1.0)


def borders(own, top, bottom):
    rows, chans, _ = own.shape
    up = shifted(bottom, "row", True)
    down = shifted(top, "row", False)
    groups = (rows + 2 * STEP) // 16
    first, last = run(
        pack_kernel, [shape((groups, chans, LANES), BF16)] * 2, (own, up, down), micros=8
    )
    left = shifted(last, "col", True)
    right = shifted(first, "col", False)
    return up, down, left, right


def partners(stage):
    if stage < 2:
        return lambda m: lambda r, c: (r ^ (m << (2 * stage)), c)
    if stage == 2:
        return lambda m: lambda r, c: (r ^ ((m & 1) << 4), c ^ (m >> 1))
    return lambda m: lambda r, c: (r, c ^ (m << 1))


def total_small(value):
    for stage in range(4):
        to = partners(stage)
        value = (value + send(value, to(1))) + (send(value, to(2)) + send(value, to(3)))
    return value


def mirrored(pays, parts):
    got = []
    for s, block in enumerate(pays):
        bits = (2, 6, 0, 0)[s]
        owner = lambda r, c: (parts * c + (r % parts ^ s), r // parts)
        if bits:
            block = send(block, lambda r, c: (r, c ^ bits))
        got.append(send(block, lambda r, c: owner(r, c ^ bits)))
    return got


def total_quarters(quarters):
    near = partners(0)
    a, b, c, d = quarters
    part = (a + send(b, near(1))) + (send(c, near(2)) + send(d, near(3)))
    for stage in (1, 2, 3):
        to = partners(stage)
        part = (part + send(part, to(1))) + (send(part, to(2)) + send(part, to(3)))
    return [part] + [send(part, near(m)) for m in (1, 2, 3)]


def per_device(features, conv_weight, head_weight, head_bias, labels, valid):
    rows, cols, chans = features.shape
    bins = head_weight.shape[1]
    parts = cols // rows
    place = (lax.axis_index("row") % parts).astype(jnp.int32).reshape(1)
    feat = features.transpose(0, 2, 1)
    weight = conv_weight.reshape(-1, chans)
    tall = -(-bins // 8) * 8
    tile = (rows, chans, LANES)
    edge = (STEP, chans, LANES)
    act, top, bottom, counted = run(
        activate_kernel,
        [shape(tile, BF16), shape(edge, BF16), shape(edge, BF16), shape((8, LANES), F32)],
        (feat, valid),
        micros=1,
    )
    around = borders(act, top, bottom)
    count = total_small(counted)
    count, act = lax.optimization_barrier((count, act))
    length = (rows + 1) * rows // 2
    wide, mixed, *pays = run(
        forward_kernel,
        [shape((rows + 2 * STEP, 3 * chans, LANES), BF16), shape(tile, BF16)]
        + [shape((length, LANES), BF16)] * 4,
        (place, act, *around, feat, weight, labels, valid),
        scratch=[pltpu.VMEM(((rows + 1) * LANES, chans), F32)],
        scalars=1,
        micros=5,
    )
    got = mirrored(pays, parts)
    grad, head_sum, bias_sum, loss_sum = run(
        softmax_kernel,
        [
            shape(tile, F32),
            shape((3 * tall, chans), F32),
            shape((tall, LANES), F32),
            shape((1, LANES), F32),
        ],
        (place, *got, mixed, head_weight.T, head_bias.reshape(1, bins), labels, valid),
        scratch=[pltpu.VMEM((length * 4, LANES), F32)]
        + [pltpu.VMEM((rows, LANES), F32)] * 4
        + [pltpu.VMEM((tall, chans), F32)],
        scalars=1,
        micros=5,
    )
    half = 9 * chans // 2
    lines = -(-(half + tall + 8) // 32) * 32
    low, top, bottom, *quarters = run(
        kernel_grad_kernel,
        [shape(tile, BF16), shape(edge, BF16), shape(edge, BF16)]
        + [shape((lines // 4, LANES), F32)] * 4,
        (place, count, grad, wide, head_sum, bias_sum, loss_sum),
        scratch=[pltpu.VMEM((9 * chans, chans), F32), pltpu.VMEM((lines, LANES), F32)],
        scalars=1,
        micros=3,
    )
    sums = total_quarters(quarters)
    around = borders(low, top, bottom)
    (grad_features,) = run(
        backward_kernel,
        [shape(tile, BF16)],
        (count, low, *around, grad, feat, weight),
        scratch=[pltpu.VMEM((rows + 2 * STEP, 3 * chans, LANES), BF16)],
        micros=4,
    )
    kernel_grad, head_grad, bias_grad, loss = run(
        finish_kernel,
        [
            shape((9 * chans, chans), F32),
            shape((bins, chans), F32),
            shape((1, bins), F32),
            shape((1, 1), F32),
        ],
        (place, count, *sums),
        scratch=[pltpu.VMEM((lines, LANES), F32)],
        scalars=1,
        micros=1,
    )
    return (
        loss.reshape(()),
        grad_features.transpose(0, 2, 1),
        kernel_grad.reshape(conv_weight.shape),
        head_grad.T,
        bias_grad.reshape(bins),
    )


def solution(mesh):
    placed = (P("row", "col", None), P(), P(), P(), P("row", "col"), P("row", "col"))
    return jax.shard_map(
        per_device,
        mesh=mesh,
        in_specs=placed,
        out_specs=(P(), P("row", "col", None), P(), P(), P()),
        check_vma=False,
    )
```

```python
import jax
import jax.numpy as jnp
from jax import lax
from jax.experimental import pallas as pl
from jax.experimental.pallas import tpu as pltpu
from jax.sharding import PartitionSpec as P

STEP = 8
GRID = ("row", "col")
F32, BF16 = jnp.float32, jnp.bfloat16
LANES = 128
UNROLL = 8
FAR_BELOW = -1e30
VMEM = pl.BlockSpec(memory_space=pltpu.VMEM)
SMEM = pl.BlockSpec(memory_space=pltpu.SMEM)


def run(body, outs, args, scratch=(), scalars=0, micros=3):
    return pl.pallas_call(
        body,
        out_shape=outs,
        in_specs=[SMEM] * scalars + [VMEM] * (len(args) - scalars),
        out_specs=[VMEM] * len(outs),
        scratch_shapes=list(scratch),
        compiler_params=pltpu.CompilerParams(vmem_limit_bytes=48 * 1024 * 1024),
        cost_estimate=pl.CostEstimate(
            flops=0, bytes_accessed=int(micros * 3.6e6), transcendentals=0
        ),
    )(*args)


def shape(dims, kind):
    return jax.ShapeDtypeStruct(dims, kind)


def send(block, target):
    nrow, ncol = lax.axis_size("row"), lax.axis_size("col")
    pairs = []
    for r in range(nrow):
        for c in range(ncol):
            r2, c2 = target(r, c)
            pairs.append((r * ncol + c, r2 * ncol + c2))
    return lax.ppermute(block, GRID, pairs)


def shifted(block, axis, forward):
    count = lax.axis_size(axis)
    pairs = [(i, i + 1) for i in range(count - 1)]
    return lax.ppermute(block, axis, pairs if forward else [(b, a) for a, b in pairs])


def activate_kernel(feat, valid, act, top, bottom, counted, kept_feat, kept_valid):
    rows = feat.shape[0]

    def step(i, carry):
        kept_feat[i] = feat[i]
        v = feat[i].astype(F32)
        near = v * (1.0 + v * (0.5 + v * (1.0 / 6.0 + v * (1.0 / 24.0))))
        low = jnp.where(v > -0.03, near, jnp.exp(jnp.minimum(v, 0.0)) - 1.0)
        act[i] = jnp.where(v > 0, v, low).astype(BF16)
        return carry

    lax.fori_loop(0, rows, step, 0, unroll=4)
    top[...] = act[:STEP]
    bottom[...] = act[rows - STEP :]
    lines = jnp.sum(valid[...].astype(F32), axis=0, keepdims=True)
    kept_valid[...] = valid[...]
    counted[...] = jnp.broadcast_to(jnp.sum(lines, axis=1, keepdims=True), counted.shape)


def row_of(own, up, down, at):
    rows = own.shape[0]
    if at < STEP:
        return up[at]
    if at < STEP + rows:
        return own[at - STEP]
    return down[at - STEP - rows]


def pack_kernel(own, up, down, first, last):
    chans = own.shape[1]
    lane = lax.broadcasted_iota(jnp.int32, (chans, LANES), 1) // STEP
    for group in range(first.shape[0]):
        low = jnp.zeros((chans, LANES), F32)
        high = jnp.zeros((chans, LANES), F32)
        for slot in range(16):
            x = row_of(own, up, down, group * 16 + slot).astype(F32)
            here = lane == slot
            low = jnp.where(here, pltpu.roll(x, (STEP * slot) % LANES, 1), low)
            high = jnp.where(here, pltpu.roll(x, (STEP * slot + STEP) % LANES, 1), high)
        first[group] = low.astype(BF16)
        last[group] = high.astype(BF16)


def spread_columns(own, up, down, left, right, wide):
    chans = own.shape[1]
    lane = lax.broadcasted_iota(jnp.int32, (chans, LANES), 1)
    for group in range(left.shape[0]):
        from_left = left[group].astype(F32)
        from_right = right[group].astype(F32)
        for slot in range(16):
            at = group * 16 + slot
            middle = row_of(own, up, down, at)
            x = middle.astype(F32)
            before = jnp.where(
                lane < STEP,
                pltpu.roll(from_left, (LANES - STEP * slot) % LANES, 1),
                pltpu.roll(x, STEP, 1),
            )
            after = jnp.where(
                lane >= LANES - STEP,
                pltpu.roll(from_right, (2 * LANES - STEP - STEP * slot) % LANES, 1),
                pltpu.roll(x, LANES - STEP, 1),
            )
            wide[at, 0:chans] = before.astype(BF16)
            wide[at, chans : 2 * chans] = middle
            wide[at, 2 * chans : 3 * chans] = after.astype(BF16)


def windows(wide, i):
    return jnp.concatenate([wide[i], wide[i + STEP], wide[i + 2 * STEP]], axis=0)


def pair_windows(wide, i):
    return jnp.concatenate([windows(wide, i), windows(wide, i + 1)], axis=1)


def forward_kernel(
    place, act, up, down, left, right, feat, weight, labels, valid,
    wide, mixed, pay0, pay1, pay2, pay3, turned,
):
    rows, chans = act.shape[0], act.shape[1]
    part = rows
    pays = (pay0, pay1, pay2, pay3)
    spread_columns(act, up, down, left, right, wide)
    kernel = weight[...].astype(F32).T.astype(BF16)

    def step(p, carry):
        i = 2 * p
        out = jnp.dot(kernel, pair_windows(wide, i), preferred_element_type=F32)
        for d in range(2):
            total = feat[i + d].astype(F32) + out[:, d * LANES : (d + 1) * LANES]
            low = total.astype(BF16)
            mixed[i + d] = low
            turned[pl.ds(pl.multiple_of((i + d) * LANES, LANES), LANES), :] = low.astype(F32).T
        return carry

    lax.fori_loop(0, rows // 2, step, 0, unroll=UNROLL)
    turned[rows * LANES :, :] = jnp.concatenate(
        [labels[...].astype(F32).T, valid[...].astype(F32).T], axis=1
    )
    half = part // 2

    def pack(j, carry):
        for s in range(4):
            base = j * LANES + (place[0] ^ s) * part
            low = turned[pl.ds(pl.multiple_of(base, 16), half), :]
            high = turned[pl.ds(pl.multiple_of(base + half, 16), half), :]
            pays[s][pl.ds(pl.multiple_of(j * half, 16), half), :] = jnp.concatenate(
                [low, high], axis=1
            ).astype(BF16)
        return carry

    lax.fori_loop(0, rows + 1, pack, 0, unroll=3)


def softmax_kernel(
    place, got0, got1, got2, got3, mixed, head, head_bias, labels, valid,
    grad, head_sum, bias_sum, loss_sum, cells, lab, lab_t, val, val_t, padded_head,
):
    rows, chans = mixed.shape[0], mixed.shape[1]
    bins, real = padded_head.shape[0], head.shape[0]
    half = rows // 2
    size = rows * half
    for s, got in enumerate((got0, got1, got2, got3)):
        q = place[0] ^ s
        cells[pl.ds(pl.multiple_of(q * size, size), size), :] = got[:size, :].astype(F32)
        cells[pl.ds(pl.multiple_of(4 * size + q * half, half), half), :] = got[size:, :].astype(F32)
    notes = [cells[4 * size + q * half : 4 * size + (q + 1) * half, :] for q in range(4)]
    for top in range(2):
        base = top * 2 * rows
        lab_t[top * half : (top + 1) * half, :] = jnp.concatenate(
            [n[:, base : base + rows] for n in notes], axis=1
        )
        val_t[top * half : (top + 1) * half, :] = jnp.concatenate(
            [n[:, base + rows : base + 2 * rows] for n in notes], axis=1
        )
    padded_head[...] = jnp.zeros_like(padded_head)
    padded_head[:real, :] = head[...].astype(F32)
    single = padded_head[...]
    blank = jnp.zeros_like(single)
    both = jnp.concatenate(
        [jnp.concatenate([single, blank], axis=1), jnp.concatenate([blank, single], axis=1)], axis=0
    ).astype(BF16)
    thrice = jnp.concatenate([single, single, single], axis=0).T.astype(BF16)
    single = single.astype(BF16)
    line = lax.broadcasted_iota(jnp.int32, (bins, real), 0)
    across = lax.broadcasted_iota(jnp.int32, (bins, real), 1)
    bias = jnp.sum(jnp.where(line == across, head_bias[...], 0.0), axis=1, keepdims=True)
    bias = jnp.where(lax.broadcasted_iota(jnp.int32, (bins, 1), 0) < real, bias, FAR_BELOW)
    lab[...] = labels[...].astype(F32)
    val[...] = valid[...].astype(F32)
    bin_ids = lax.broadcasted_iota(jnp.int32, (bins, LANES), 0).astype(F32)
    head_sum[...] = jnp.zeros_like(head_sum)
    bias_sum[...] = jnp.zeros_like(bias_sum)
    loss_sum[...] = jnp.zeros_like(loss_sum)

    def step(i, carry):
        other = cells[pl.ds(i, LANES, stride=half), :].astype(BF16)
        logits_t = lax.dot_general(both, other, (((1,), (1,)), ((), ())), preferred_element_type=F32)
        pair = jnp.concatenate([mixed[i], mixed[i + half]], axis=1)
        logits = jnp.dot(single, pair, preferred_element_type=F32)
        pieces = []
        for d in range(2):
            at = pl.ds(i + d * half, 1)
            own = logits[:, d * LANES : (d + 1) * LANES] + bias
            far = logits_t[d * bins : (d + 1) * bins] + bias
            sym = 0.5 * (own + far)
            peak = jnp.max(sym, axis=0, keepdims=True)
            raised = jnp.exp(sym - peak)
            total = jnp.sum(raised, axis=0, keepdims=True)
            lse = peak + jnp.log(total)
            hot = bin_ids == lab[at, :]
            hot_t = bin_ids == lab_t[at, :]
            mask, mask_t = val[at, :], val_t[at, :]
            picked = jnp.sum(jnp.where(hot, sym, 0.0), axis=0, keepdims=True)
            loss_sum[...] += mask * (lse - picked)
            share = raised * ((mask + mask_t) / total)
            pieces.append(share - jnp.where(hot, mask, 0.0) - jnp.where(hot_t, mask_t, 0.0))
        bias_sum[...] += pieces[0] + pieces[1]
        g = jnp.concatenate(pieces, axis=1)
        first = g.astype(BF16).astype(F32)
        rest = g - first
        second = rest.astype(BF16).astype(F32)
        split = jnp.concatenate([first, second, rest - second], axis=0).astype(BF16)
        out = jnp.dot(thrice, split, preferred_element_type=F32)
        grad[i] = out[:, :LANES]
        grad[i + half] = out[:, LANES:]
        head_sum[...] += lax.dot_general(
            split, pair, (((1,), (1,)), ((), ())), preferred_element_type=F32
        )
        return carry

    lax.fori_loop(0, half, step, 0, unroll=UNROLL)


def scale_of(count):
    return 0.5 / jnp.maximum(count[0:1, 0:1], 1.0)


def kernel_grad_kernel(
    place, count, grad, wide, head_sum, bias_sum, loss_sum,
    low, top, bottom, out0, out1, out2, out3, total, sheet,
):
    rows, chans = grad.shape[0], grad.shape[1]
    bins = bias_sum.shape[0]
    scale = scale_of(count)
    total[...] = jnp.zeros_like(total)

    def step(p, carry):
        i = 2 * p
        a = (grad[i] * scale).astype(BF16)
        b = (grad[i + 1] * scale).astype(BF16)
        low[i] = a
        low[i + 1] = b
        total[...] += lax.dot_general(
            pair_windows(wide, i),
            jnp.concatenate([a, b], axis=1),
            (((1,), (1,)), ((), ())),
            preferred_element_type=F32,
        )
        return carry

    lax.fori_loop(0, rows // 2, step, 0, unroll=UNROLL)
    top[...] = low[:STEP]
    bottom[...] = low[rows - STEP :]
    half = total.shape[0] // 2
    sheet[...] = jnp.zeros_like(sheet)
    sheet[:half, :] = jnp.concatenate([total[:half], total[half:]], axis=1)
    h = (head_sum[:bins] + head_sum[bins : 2 * bins] + head_sum[2 * bins :]) * scale
    sheet[half : half + bins, :chans] = h
    note = half + bins
    sheet[note : note + 1, :bins] = jnp.sum(bias_sum[...].T, axis=0, keepdims=True) * scale
    sheet[note + 1 : note + 2, :1] = jnp.sum(loss_sum[...], axis=1, keepdims=True)
    quarter = sheet.shape[0] // 4
    for s, out in enumerate((out0, out1, out2, out3)):
        out[...] = sheet[pl.ds(pl.multiple_of((place[0] ^ s) * quarter, 8), quarter), :]


def backward_kernel(count, low, up, down, left, right, grad, feat, weight, out, wide):
    rows, chans = grad.shape[0], grad.shape[1]
    scale = scale_of(count)
    spread_columns(low, up, down, left, right, wide)
    taps = weight.shape[0] // chans
    kernel = jnp.concatenate(
        [weight[(taps - 1 - t) * chans : (taps - t) * chans, :].astype(F32) for t in range(taps)],
        axis=1,
    ).astype(BF16)

    def step(p, carry):
        i = 2 * p
        back = jnp.dot(kernel, pair_windows(wide, i), preferred_element_type=F32)
        for d in range(2):
            v = feat[i + d].astype(F32)
            slope = jnp.where(v > 0, 1.0, jnp.exp(jnp.minimum(v, 0.0)))
            out[i + d] = (
                grad[i + d] * scale + slope * back[:, d * LANES : (d + 1) * LANES]
            ).astype(BF16)
        return carry

    lax.fori_loop(0, rows // 2, step, 0, unroll=UNROLL)


def finish_kernel(
    place, count, got0, got1, got2, got3, kernel_grad, head_grad, bias_grad, loss, sheet
):
    quarter = got0.shape[0]
    for s, got in enumerate((got0, got1, got2, got3)):
        sheet[pl.ds(pl.multiple_of((place[0] ^ s) * quarter, 8), quarter), :] = got[...]
    half, chans = kernel_grad.shape[0] // 2, kernel_grad.shape[1]
    bins = head_grad.shape[0]
    kernel_grad[:half, :] = sheet[:half, :chans]
    kernel_grad[half:, :] = sheet[:half, chans:]
    head_grad[...] = sheet[half : half + bins, :chans]
    note = half + -(-bins // 8) * 8
    bias_grad[...] = sheet[note : note + 1, :bins]
    loss[...] = sheet[note + 1 : note + 2, :1] / jnp.maximum(count[0:1, 0:1], 1.0)


def borders(own, top, bottom):
    rows, chans, _ = own.shape
    up = shifted(bottom, "row", True)
    down = shifted(top, "row", False)
    groups = (rows + 2 * STEP) // 16
    first, last = run(
        pack_kernel, [shape((groups, chans, LANES), BF16)] * 2, (own, up, down), micros=8
    )
    left = shifted(last, "col", True)
    right = shifted(first, "col", False)
    return up, down, left, right


def partners(stage):
    if stage < 2:
        return lambda m: lambda r, c: (r ^ (m << (2 * stage)), c)
    if stage == 2:
        return lambda m: lambda r, c: (r ^ ((m & 1) << 4), c ^ (m >> 1))
    return lambda m: lambda r, c: (r, c ^ (m << 1))


def total_small(value):
    for stage in range(4):
        to = partners(stage)
        value = (value + send(value, to(1))) + (send(value, to(2)) + send(value, to(3)))
    return value


def mirrored(pays, parts):
    got = []
    for s, block in enumerate(pays):
        bits = (2, 6, 0, 0)[s]
        owner = lambda r, c: (parts * c + (r % parts ^ s), r // parts)
        if bits:
            block = send(block, lambda r, c: (r, c ^ bits))
        got.append(send(block, lambda r, c: owner(r, c ^ bits)))
    return got


def total_quarters(quarters):
    near = partners(0)
    a, b, c, d = quarters
    part = (a + send(b, near(1))) + (send(c, near(2)) + send(d, near(3)))
    for stage in (1, 2, 3):
        to = partners(stage)
        part = (part + send(part, to(1))) + (send(part, to(2)) + send(part, to(3)))
    return [part] + [send(part, near(m)) for m in (1, 2, 3)]


def per_device(features, conv_weight, head_weight, head_bias, labels, valid):
    rows, cols, chans = features.shape
    bins = head_weight.shape[1]
    parts = cols // rows
    place = (lax.axis_index("row") % parts).astype(jnp.int32).reshape(1)
    feat = features.transpose(0, 2, 1)
    weight = conv_weight.reshape(-1, chans)
    tall = -(-bins // 8) * 8
    tile = (rows, chans, LANES)
    edge = (STEP, chans, LANES)
    act, top, bottom, counted, feat, valid = run(
        activate_kernel,
        [shape(tile, BF16), shape(edge, BF16), shape(edge, BF16), shape((8, LANES), F32)]
        + [shape(tile, BF16), shape(valid.shape, jnp.int32)],
        (feat, valid),
        micros=1,
    )
    around = borders(act, top, bottom)
    count = total_small(counted)
    count, act = lax.optimization_barrier((count, act))
    length = (rows + 1) * rows // 2
    wide, mixed, *pays = run(
        forward_kernel,
        [shape((rows + 2 * STEP, 3 * chans, LANES), BF16), shape(tile, BF16)]
        + [shape((length, LANES), BF16)] * 4,
        (place, act, *around, feat, weight, labels, valid),
        scratch=[pltpu.VMEM(((rows + 1) * LANES, chans), F32)],
        scalars=1,
        micros=5,
    )
    got = mirrored(pays, parts)
    grad, head_sum, bias_sum, loss_sum = run(
        softmax_kernel,
        [
            shape(tile, F32),
            shape((3 * tall, chans), F32),
            shape((tall, LANES), F32),
            shape((1, LANES), F32),
        ],
        (place, *got, mixed, head_weight.T, head_bias.reshape(1, bins), labels, valid),
        scratch=[pltpu.VMEM((length * 4, LANES), F32)]
        + [pltpu.VMEM((rows, LANES), F32)] * 4
        + [pltpu.VMEM((tall, chans), F32)],
        scalars=1,
        micros=5,
    )
    half = 9 * chans // 2
    lines = -(-(half + tall + 8) // 32) * 32
    low, top, bottom, *quarters = run(
        kernel_grad_kernel,
        [shape(tile, BF16), shape(edge, BF16), shape(edge, BF16)]
        + [shape((lines // 4, LANES), F32)] * 4,
        (place, count, grad, wide, head_sum, bias_sum, loss_sum),
        scratch=[pltpu.VMEM((9 * chans, chans), F32), pltpu.VMEM((lines, LANES), F32)],
        scalars=1,
        micros=3,
    )
    sums = total_quarters(quarters)
    around = borders(low, top, bottom)
    (grad_features,) = run(
        backward_kernel,
        [shape(tile, BF16)],
        (count, low, *around, grad, feat, weight),
        scratch=[pltpu.VMEM((rows + 2 * STEP, 3 * chans, LANES), BF16)],
        micros=4,
    )
    kernel_grad, head_grad, bias_grad, loss = run(
        finish_kernel,
        [
            shape((9 * chans, chans), F32),
            shape((bins, chans), F32),
            shape((1, bins), F32),
            shape((1, 1), F32),
        ],
        (place, count, *sums),
        scratch=[pltpu.VMEM((lines, LANES), F32)],
        scalars=1,
        micros=1,
    )
    return (
        loss.reshape(()),
        grad_features.transpose(0, 2, 1),
        kernel_grad.reshape(conv_weight.shape),
        head_grad.T,
        bias_grad.reshape(bins),
    )


def solution(mesh):
    placed = (P("row", "col", None), P(), P(), P(), P("row", "col"), P("row", "col"))
    return jax.shard_map(
        per_device,
        mesh=mesh,
        in_specs=placed,
        out_specs=(P(), P("row", "col", None), P(), P(), P()),
        check_vma=False,
    )
```

```python
import jax
import jax.numpy as jnp
from jax import lax
from jax.experimental import pallas as pl
from jax.experimental.pallas import tpu as pltpu
from jax.sharding import PartitionSpec as P

STEP = 8
GRID = ("row", "col")
F32, BF16 = jnp.float32, jnp.bfloat16
LANES = 128
UNROLL = 8
SLAB = 64
FAR_BELOW = -1e30
VMEM = pl.BlockSpec(memory_space=pltpu.VMEM)
SMEM = pl.BlockSpec(memory_space=pltpu.SMEM)


def run(body, outs, args, scratch=(), scalars=0, micros=3):
    return pl.pallas_call(
        body,
        out_shape=outs,
        in_specs=[SMEM] * scalars + [VMEM] * (len(args) - scalars),
        out_specs=[VMEM] * len(outs),
        scratch_shapes=list(scratch),
        compiler_params=pltpu.CompilerParams(vmem_limit_bytes=48 * 1024 * 1024),
        cost_estimate=pl.CostEstimate(
            flops=0, bytes_accessed=int(micros * 3.6e6), transcendentals=0
        ),
    )(*args)


def shape(dims, kind):
    return jax.ShapeDtypeStruct(dims, kind)


def send(block, target):
    nrow, ncol = lax.axis_size("row"), lax.axis_size("col")
    pairs = []
    for r in range(nrow):
        for c in range(ncol):
            r2, c2 = target(r, c)
            pairs.append((r * ncol + c, r2 * ncol + c2))
    return lax.ppermute(block, GRID, pairs)


def shifted(block, axis, forward):
    count = lax.axis_size(axis)
    pairs = [(i, i + 1) for i in range(count - 1)]
    return lax.ppermute(block, axis, pairs if forward else [(b, a) for a, b in pairs])


def activate_kernel(feat, valid, act, top, bottom, counted, kept_feat, kept_valid):
    rows = feat.shape[0]

    def step(i, carry):
        kept_feat[i] = feat[i]
        v = feat[i].astype(F32)
        near = v * (1.0 + v * (0.5 + v * (1.0 / 6.0 + v * (1.0 / 24.0))))
        low = jnp.where(v > -0.03, near, jnp.exp(jnp.minimum(v, 0.0)) - 1.0)
        act[i] = jnp.where(v > 0, v, low).astype(BF16)
        return carry

    lax.fori_loop(0, rows, step, 0, unroll=4)
    top[...] = act[:STEP]
    bottom[...] = act[rows - STEP :]
    lines = jnp.sum(valid[...].astype(F32), axis=0, keepdims=True)
    kept_valid[...] = valid[...]
    counted[...] = jnp.broadcast_to(jnp.sum(lines, axis=1, keepdims=True), counted.shape)


def row_of(own, up, down, at):
    rows = own.shape[0]
    if at < STEP:
        return up[at]
    if at < STEP + rows:
        return own[at - STEP]
    return down[at - STEP - rows]


def pack_kernel(own, up, down, first, last):
    chans = own.shape[1]
    lane = lax.broadcasted_iota(jnp.int32, (chans, LANES), 1) // STEP
    for group in range(first.shape[0]):
        low = jnp.zeros((chans, LANES), F32)
        high = jnp.zeros((chans, LANES), F32)
        for slot in range(16):
            x = row_of(own, up, down, group * 16 + slot).astype(F32)
            here = lane == slot
            low = jnp.where(here, pltpu.roll(x, (STEP * slot) % LANES, 1), low)
            high = jnp.where(here, pltpu.roll(x, (STEP * slot + STEP) % LANES, 1), high)
        first[group] = low.astype(BF16)
        last[group] = high.astype(BF16)


def spread_columns(own, up, down, left, right, wide):
    chans = own.shape[1]
    lane = lax.broadcasted_iota(jnp.int32, (chans, LANES), 1)
    for group in range(left.shape[0]):
        from_left = left[group].astype(F32)
        from_right = right[group].astype(F32)
        for slot in range(16):
            at = group * 16 + slot
            middle = row_of(own, up, down, at)
            x = middle.astype(F32)
            before = jnp.where(
                lane < STEP,
                pltpu.roll(from_left, (LANES - STEP * slot) % LANES, 1),
                pltpu.roll(x, STEP, 1),
            )
            after = jnp.where(
                lane >= LANES - STEP,
                pltpu.roll(from_right, (2 * LANES - STEP - STEP * slot) % LANES, 1),
                pltpu.roll(x, LANES - STEP, 1),
            )
            wide[at, 0:chans] = before.astype(BF16)
            wide[at, chans : 2 * chans] = middle
            wide[at, 2 * chans : 3 * chans] = after.astype(BF16)


def windows(wide, i):
    return jnp.concatenate([wide[i], wide[i + STEP], wide[i + 2 * STEP]], axis=0)


def pair_windows(wide, i):
    return jnp.concatenate([windows(wide, i), windows(wide, i + 1)], axis=1)


def forward_kernel(
    place, act, up, down, left, right, feat, weight, labels, valid,
    wide, mixed, pay0, pay1, pay2, pay3, turned,
):
    rows, chans = act.shape[0], act.shape[1]
    part = rows
    pays = (pay0, pay1, pay2, pay3)
    spread_columns(act, up, down, left, right, wide)
    kernel = weight[...].astype(F32).T.astype(BF16)

    def step(p, carry):
        i = 2 * p
        out = jnp.dot(kernel, pair_windows(wide, i), preferred_element_type=F32)
        for d in range(2):
            total = feat[i + d].astype(F32) + out[:, d * LANES : (d + 1) * LANES]
            low = total.astype(BF16)
            mixed[i + d] = low
            turned[pl.ds(pl.multiple_of((i + d) * LANES, LANES), LANES), :] = low.astype(F32).T
        return carry

    lax.fori_loop(0, rows // 2, step, 0, unroll=UNROLL)
    turned[rows * LANES :, :] = jnp.concatenate(
        [labels[...].astype(F32).T, valid[...].astype(F32).T], axis=1
    )
    half = part // 2

    def pack(j, carry):
        for s in range(4):
            base = j * LANES + (place[0] ^ s) * part
            low = turned[pl.ds(pl.multiple_of(base, 16), half), :]
            high = turned[pl.ds(pl.multiple_of(base + half, 16), half), :]
            pays[s][pl.ds(pl.multiple_of(j * half, 16), half), :] = jnp.concatenate(
                [low, high], axis=1
            ).astype(BF16)
        return carry

    lax.fori_loop(0, rows + 1, pack, 0, unroll=3)


def softmax_kernel(
    place, got0, got1, got2, got3, mixed, head, head_bias, labels, valid,
    grad, head_sum, bias_sum, loss_sum, cells, lab, lab_t, val, val_t, padded_head,
):
    rows, chans = mixed.shape[0], mixed.shape[1]
    bins, real = padded_head.shape[0], head.shape[0]
    half = rows // 2
    size = rows * half
    for s, got in enumerate((got0, got1, got2, got3)):
        q = place[0] ^ s
        cells[pl.ds(pl.multiple_of(q * size, size), size), :] = got[:size, :].astype(F32)
        cells[pl.ds(pl.multiple_of(4 * size + q * half, half), half), :] = got[size:, :].astype(F32)
    notes = [cells[4 * size + q * half : 4 * size + (q + 1) * half, :] for q in range(4)]
    for top in range(2):
        base = top * 2 * rows
        lab_t[top * half : (top + 1) * half, :] = jnp.concatenate(
            [n[:, base : base + rows] for n in notes], axis=1
        )
        val_t[top * half : (top + 1) * half, :] = jnp.concatenate(
            [n[:, base + rows : base + 2 * rows] for n in notes], axis=1
        )
    padded_head[...] = jnp.zeros_like(padded_head)
    padded_head[:real, :] = head[...].astype(F32)
    single = padded_head[...]
    blank = jnp.zeros_like(single)
    both = jnp.concatenate(
        [jnp.concatenate([single, blank], axis=1), jnp.concatenate([blank, single], axis=1)], axis=0
    ).astype(BF16)
    thrice = jnp.concatenate([single, single, single], axis=0).T.astype(BF16)
    single = single.astype(BF16)
    line = lax.broadcasted_iota(jnp.int32, (bins, real), 0)
    across = lax.broadcasted_iota(jnp.int32, (bins, real), 1)
    bias = jnp.sum(jnp.where(line == across, head_bias[...], 0.0), axis=1, keepdims=True)
    bias = jnp.where(lax.broadcasted_iota(jnp.int32, (bins, 1), 0) < real, bias, FAR_BELOW)
    lab[...] = labels[...].astype(F32)
    val[...] = valid[...].astype(F32)
    bin_ids = lax.broadcasted_iota(jnp.int32, (bins, LANES), 0).astype(F32)
    head_sum[...] = jnp.zeros_like(head_sum)
    bias_sum[...] = jnp.zeros_like(bias_sum)
    loss_sum[...] = jnp.zeros_like(loss_sum)

    def step(i, carry):
        other = cells[pl.ds(i, LANES, stride=half), :].astype(BF16)
        logits_t = lax.dot_general(both, other, (((1,), (1,)), ((), ())), preferred_element_type=F32)
        pair = jnp.concatenate([mixed[i], mixed[i + half]], axis=1)
        logits = jnp.dot(single, pair, preferred_element_type=F32)
        pieces = []
        for d in range(2):
            at = pl.ds(i + d * half, 1)
            own = logits[:, d * LANES : (d + 1) * LANES] + bias
            far = logits_t[d * bins : (d + 1) * bins] + bias
            sym = 0.5 * (own + far)
            peak = jnp.max(sym, axis=0, keepdims=True)
            raised = jnp.exp(sym - peak)
            total = jnp.sum(raised, axis=0, keepdims=True)
            lse = peak + jnp.log(total)
            hot = bin_ids == lab[at, :]
            hot_t = bin_ids == lab_t[at, :]
            mask, mask_t = val[at, :], val_t[at, :]
            picked = jnp.sum(jnp.where(hot, sym, 0.0), axis=0, keepdims=True)
            loss_sum[...] += mask * (lse - picked)
            share = raised * ((mask + mask_t) / total)
            pieces.append(share - jnp.where(hot, mask, 0.0) - jnp.where(hot_t, mask_t, 0.0))
        bias_sum[...] += pieces[0] + pieces[1]
        g = jnp.concatenate(pieces, axis=1)
        first = g.astype(BF16).astype(F32)
        rest = g - first
        second = rest.astype(BF16).astype(F32)
        split = jnp.concatenate([first, second, rest - second], axis=0).astype(BF16)
        out = jnp.dot(thrice, split, preferred_element_type=F32)
        grad[i] = out[:, :LANES]
        grad[i + half] = out[:, LANES:]
        head_sum[...] += lax.dot_general(
            split, pair, (((1,), (1,)), ((), ())), preferred_element_type=F32
        )
        return carry

    lax.fori_loop(0, half, step, 0, unroll=UNROLL)


def scale_of(count):
    return 0.5 / jnp.maximum(count[0:1, 0:1], 1.0)


def kernel_grad_kernel(
    place, count, grad, wide, head_sum, bias_sum, loss_sum,
    low, top, bottom, out0, out1, out2, out3, total, sheet,
):
    rows, chans = grad.shape[0], grad.shape[1]
    bins = bias_sum.shape[0]
    scale = scale_of(count)
    total[...] = jnp.zeros_like(total)

    def step(p, carry):
        i = 2 * p
        a = (grad[i] * scale).astype(BF16)
        b = (grad[i + 1] * scale).astype(BF16)
        low[i] = a
        low[i + 1] = b
        total[...] += lax.dot_general(
            pair_windows(wide, i),
            jnp.concatenate([a, b], axis=1),
            (((1,), (1,)), ((), ())),
            preferred_element_type=F32,
        )
        return carry

    lax.fori_loop(0, rows // 2, step, 0, unroll=UNROLL)
    top[...] = low[:STEP]
    bottom[...] = low[rows - STEP :]
    half = total.shape[0] // 2
    sheet[...] = jnp.zeros_like(sheet)
    sheet[:half, :] = jnp.concatenate([total[:half], total[half:]], axis=1)
    h = (head_sum[:bins] + head_sum[bins : 2 * bins] + head_sum[2 * bins :]) * scale
    sheet[half : half + bins, :chans] = h
    note = half + bins
    sheet[note : note + 1, :bins] = jnp.sum(bias_sum[...].T, axis=0, keepdims=True) * scale
    sheet[note + 1 : note + 2, :1] = jnp.sum(loss_sum[...], axis=1, keepdims=True)
    quarter = sheet.shape[0] // 4
    for s, out in enumerate((out0, out1, out2, out3)):
        out[...] = sheet[pl.ds(pl.multiple_of((place[0] ^ s) * quarter, 8), quarter), :]


def backward_kernel(count, low, up, down, left, right, grad, feat, weight, out, wide):
    rows, chans = grad.shape[0], grad.shape[1]
    scale = scale_of(count)
    spread_columns(low, up, down, left, right, wide)
    taps = weight.shape[0] // chans
    kernel = jnp.concatenate(
        [weight[(taps - 1 - t) * chans : (taps - t) * chans, :].astype(F32) for t in range(taps)],
        axis=1,
    ).astype(BF16)

    def step(p, carry):
        i = 2 * p
        back = jnp.dot(kernel, pair_windows(wide, i), preferred_element_type=F32)
        for d in range(2):
            v = feat[i + d].astype(F32)
            slope = jnp.where(v > 0, 1.0, jnp.exp(jnp.minimum(v, 0.0)))
            out[i + d] = (
                grad[i + d] * scale + slope * back[:, d * LANES : (d + 1) * LANES]
            ).astype(BF16)
        return carry

    lax.fori_loop(0, rows // 2, step, 0, unroll=UNROLL)


def finish_kernel(
    place, count, got0, got1, got2, got3, kernel_grad, head_grad, bias_grad, loss, sheet
):
    quarter = got0.shape[0]
    for s, got in enumerate((got0, got1, got2, got3)):
        sheet[pl.ds(pl.multiple_of((place[0] ^ s) * quarter, 8), quarter), :] = got[...]
    half, chans = kernel_grad.shape[0] // 2, kernel_grad.shape[1]
    bins = head_grad.shape[0]
    kernel_grad[:half, :] = sheet[:half, :chans]
    kernel_grad[half:, :] = sheet[:half, chans:]
    head_grad[...] = sheet[half : half + bins, :chans]
    note = half + -(-bins // 8) * 8
    bias_grad[...] = sheet[note : note + 1, :bins]
    loss[...] = sheet[note + 1 : note + 2, :1] / jnp.maximum(count[0:1, 0:1], 1.0)


def borders(own, top, bottom):
    rows, chans, _ = own.shape
    up = shifted(bottom, "row", True)
    down = shifted(top, "row", False)
    groups = (rows + 2 * STEP) // 16
    first, last = run(
        pack_kernel, [shape((groups, chans, LANES), BF16)] * 2, (own, up, down), micros=8
    )
    left = shifted(last, "col", True)
    right = shifted(first, "col", False)
    return up, down, left, right


def partners(stage):
    if stage < 2:
        return lambda m: lambda r, c: (r ^ (m << (2 * stage)), c)
    if stage == 2:
        return lambda m: lambda r, c: (r ^ ((m & 1) << 4), c ^ (m >> 1))
    return lambda m: lambda r, c: (r, c ^ (m << 1))


def total_columns(value):
    near = lambda m: lambda r, c: (r, c ^ m)
    value = value + send(value, near(1))
    return (value + send(value, near(2))) + (send(value, near(4)) + send(value, near(6)))


def mirrored(pays, parts):
    bits = (2, 6, 0, 0)
    half = [send(pays[s], lambda r, c: (r, c ^ bits[s])) if bits[s] else pays[s] for s in range(4)]
    owner = lambda s: lambda r, c: (parts * (c ^ bits[s]) + (r % parts ^ s), r // parts)
    return half, [send(half[s], owner(s)) for s in range(4)]


def total_quarters(quarters):
    near = partners(0)
    a, b, c, d = quarters
    part = (a + send(b, near(1))) + (send(c, near(2)) + send(d, near(3)))
    for stage in (1, 2, 3):
        to = partners(stage)
        part = (part + send(part, to(1))) + (send(part, to(2)) + send(part, to(3)))
    return [part] + [send(part, near(m)) for m in (1, 2, 3)]


def per_device(features, conv_weight, head_weight, head_bias, labels, valid):
    rows, cols, chans = features.shape
    bins = head_weight.shape[1]
    parts = cols // rows
    place = (lax.axis_index("row") % parts).astype(jnp.int32).reshape(1)
    feat = features.transpose(0, 2, 1)
    weight = conv_weight.reshape(-1, chans)
    tall = -(-bins // 8) * 8
    tile = (rows, chans, LANES)
    edge = (STEP, chans, LANES)
    act, top, bottom, counted, feat, valid = run(
        activate_kernel,
        [shape(tile, BF16), shape(edge, BF16), shape(edge, BF16), shape((8, LANES), F32)]
        + [shape(tile, BF16), shape(valid.shape, jnp.int32)],
        (feat, valid),
        micros=1,
    )
    around = borders(act, top, bottom)
    gathered = lax.all_gather(
        jnp.broadcast_to(counted[:1], (SLAB, LANES)), "row", axis=0, tiled=True
    )
    length = (rows + 1) * rows // 2
    wide, mixed, *pays = run(
        forward_kernel,
        [shape((rows + 2 * STEP, 3 * chans, LANES), BF16), shape(tile, BF16)]
        + [shape((length, LANES), BF16)] * 4,
        (place, act, *around, feat, weight, labels, valid),
        scratch=[pltpu.VMEM(((rows + 1) * LANES, chans), F32)],
        scalars=1,
        micros=5,
    )
    half, got = mirrored(pays, parts)
    _, gathered = lax.optimization_barrier((half[1], gathered))
    count = total_columns(jnp.sum(gathered.reshape(-1, SLAB, LANES)[:, :8], axis=0))
    grad, head_sum, bias_sum, loss_sum = run(
        softmax_kernel,
        [
            shape(tile, F32),
            shape((3 * tall, chans), F32),
            shape((tall, LANES), F32),
            shape((1, LANES), F32),
        ],
        (place, *got, mixed, head_weight.T, head_bias.reshape(1, bins), labels, valid),
        scratch=[pltpu.VMEM((length * 4, LANES), F32)]
        + [pltpu.VMEM((rows, LANES), F32)] * 4
        + [pltpu.VMEM((tall, chans), F32)],
        scalars=1,
        micros=5,
    )
    half = 9 * chans // 2
    lines = -(-(half + tall + 8) // 32) * 32
    low, top, bottom, *quarters = run(
        kernel_grad_kernel,
        [shape(tile, BF16), shape(edge, BF16), shape(edge, BF16)]
        + [shape((lines // 4, LANES), F32)] * 4,
        (place, count, grad, wide, head_sum, bias_sum, loss_sum),
        scratch=[pltpu.VMEM((9 * chans, chans), F32), pltpu.VMEM((lines, LANES), F32)],
        scalars=1,
        micros=3,
    )
    sums = total_quarters(quarters)
    around = borders(low, top, bottom)
    (grad_features,) = run(
        backward_kernel,
        [shape(tile, BF16)],
        (count, low, *around, grad, feat, weight),
        scratch=[pltpu.VMEM((rows + 2 * STEP, 3 * chans, LANES), BF16)],
        micros=4,
    )
    kernel_grad, head_grad, bias_grad, loss = run(
        finish_kernel,
        [
            shape((9 * chans, chans), F32),
            shape((bins, chans), F32),
            shape((1, bins), F32),
            shape((1, 1), F32),
        ],
        (place, count, *sums),
        scratch=[pltpu.VMEM((lines, LANES), F32)],
        scalars=1,
        micros=1,
    )
    return (
        loss.reshape(()),
        grad_features.transpose(0, 2, 1),
        kernel_grad.reshape(conv_weight.shape),
        head_grad.T,
        bias_grad.reshape(bins),
    )


def solution(mesh):
    placed = (P("row", "col", None), P(), P(), P(), P("row", "col"), P("row", "col"))
    return jax.shard_map(
        per_device,
        mesh=mesh,
        in_specs=placed,
        out_specs=(P(), P("row", "col", None), P(), P(), P()),
        check_vma=False,
    )
```

```python
import jax
import jax.numpy as jnp
from jax import lax
from jax.experimental import pallas as pl
from jax.experimental.pallas import tpu as pltpu
from jax.sharding import PartitionSpec as P

STEP = 8
GRID = ("row", "col")
F32, BF16 = jnp.float32, jnp.bfloat16
LANES = 128
UNROLL = 8
FAR_BELOW = -1e30
VMEM = pl.BlockSpec(memory_space=pltpu.VMEM)
SMEM = pl.BlockSpec(memory_space=pltpu.SMEM)


def run(body, outs, args, scratch=(), scalars=0, micros=3):
    return pl.pallas_call(
        body,
        out_shape=outs,
        in_specs=[SMEM] * scalars + [VMEM] * (len(args) - scalars),
        out_specs=[VMEM] * len(outs),
        scratch_shapes=list(scratch),
        compiler_params=pltpu.CompilerParams(vmem_limit_bytes=48 * 1024 * 1024),
        cost_estimate=pl.CostEstimate(
            flops=0, bytes_accessed=int(micros * 3.6e6), transcendentals=0
        ),
    )(*args)


def shape(dims, kind):
    return jax.ShapeDtypeStruct(dims, kind)


def send(block, target):
    nrow, ncol = lax.axis_size("row"), lax.axis_size("col")
    pairs = []
    for r in range(nrow):
        for c in range(ncol):
            r2, c2 = target(r, c)
            pairs.append((r * ncol + c, r2 * ncol + c2))
    return lax.ppermute(block, GRID, pairs)


def shifted(block, axis, forward):
    count = lax.axis_size(axis)
    pairs = [(i, i + 1) for i in range(count - 1)]
    return lax.ppermute(block, axis, pairs if forward else [(b, a) for a, b in pairs])


def activate_kernel(feat, valid, act, top, bottom, counted, kept_feat, kept_valid):
    rows = feat.shape[0]

    def step(i, carry):
        kept_feat[i] = feat[i]
        v = feat[i].astype(F32)
        near = v * (1.0 + v * (0.5 + v * (1.0 / 6.0 + v * (1.0 / 24.0))))
        low = jnp.where(v > -0.03, near, jnp.exp(jnp.minimum(v, 0.0)) - 1.0)
        act[i] = jnp.where(v > 0, v, low).astype(BF16)
        return carry

    lax.fori_loop(0, rows, step, 0, unroll=4)
    top[...] = act[:STEP]
    bottom[...] = act[rows - STEP :]
    lines = jnp.sum(valid[...].astype(F32), axis=0, keepdims=True)
    kept_valid[...] = valid[...]
    counted[...] = jnp.broadcast_to(jnp.sum(lines, axis=1, keepdims=True), counted.shape)


def row_of(own, up, down, at):
    rows = own.shape[0]
    if at < STEP:
        return up[at]
    if at < STEP + rows:
        return own[at - STEP]
    return down[at - STEP - rows]


def pack_kernel(own, up, down, first, last):
    chans = own.shape[1]
    lane = lax.broadcasted_iota(jnp.int32, (chans, LANES), 1) // STEP
    for group in range(first.shape[0]):
        low = jnp.zeros((chans, LANES), F32)
        high = jnp.zeros((chans, LANES), F32)
        for slot in range(16):
            x = row_of(own, up, down, group * 16 + slot).astype(F32)
            here = lane == slot
            low = jnp.where(here, pltpu.roll(x, (STEP * slot) % LANES, 1), low)
            high = jnp.where(here, pltpu.roll(x, (STEP * slot + STEP) % LANES, 1), high)
        first[group] = low.astype(BF16)
        last[group] = high.astype(BF16)


def spread_columns(own, up, down, left, right, wide):
    chans = own.shape[1]
    lane = lax.broadcasted_iota(jnp.int32, (chans, LANES), 1)
    for group in range(left.shape[0]):
        from_left = left[group].astype(F32)
        from_right = right[group].astype(F32)
        for slot in range(16):
            at = group * 16 + slot
            middle = row_of(own, up, down, at)
            x = middle.astype(F32)
            before = jnp.where(
                lane < STEP,
                pltpu.roll(from_left, (LANES - STEP * slot) % LANES, 1),
                pltpu.roll(x, STEP, 1),
            )
            after = jnp.where(
                lane >= LANES - STEP,
                pltpu.roll(from_right, (2 * LANES - STEP - STEP * slot) % LANES, 1),
                pltpu.roll(x, LANES - STEP, 1),
            )
            wide[at, 0:chans] = before.astype(BF16)
            wide[at, chans : 2 * chans] = middle
            wide[at, 2 * chans : 3 * chans] = after.astype(BF16)


def windows(wide, i):
    return jnp.concatenate([wide[i], wide[i + STEP], wide[i + 2 * STEP]], axis=0)


def pair_windows(wide, i):
    return jnp.concatenate([windows(wide, i), windows(wide, i + 1)], axis=1)


def forward_kernel(
    place, act, up, down, left, right, feat, weight, labels, valid,
    wide, mixed, pay_near, pay_far, turned,
):
    rows, chans = act.shape[0], act.shape[1]
    part = rows
    length = pay_near.shape[0] // 2
    spread_columns(act, up, down, left, right, wide)
    kernel = weight[...].astype(F32).T.astype(BF16)

    def step(p, carry):
        i = 2 * p
        out = jnp.dot(kernel, pair_windows(wide, i), preferred_element_type=F32)
        for d in range(2):
            total = feat[i + d].astype(F32) + out[:, d * LANES : (d + 1) * LANES]
            low = total.astype(BF16)
            mixed[i + d] = low
            turned[pl.ds(pl.multiple_of((i + d) * LANES, LANES), LANES), :] = low.astype(F32).T
        return carry

    lax.fori_loop(0, rows // 2, step, 0, unroll=UNROLL)
    turned[rows * LANES :, :] = jnp.concatenate(
        [labels[...].astype(F32).T, valid[...].astype(F32).T], axis=1
    )
    half = part // 2

    def pack(j, carry):
        for s in range(4):
            base = j * LANES + (place[0] ^ s) * part
            low = turned[pl.ds(pl.multiple_of(base, 16), half), :]
            high = turned[pl.ds(pl.multiple_of(base + half, 16), half), :]
            pay = pay_near if s < 2 else pay_far
            pay[pl.ds(pl.multiple_of(s % 2 * length + j * half, 16), half), :] = jnp.concatenate(
                [low, high], axis=1
            ).astype(BF16)
        return carry

    lax.fori_loop(0, rows + 1, pack, 0, unroll=3)


def softmax_kernel(
    place, near, far, got1, got3, mixed, head, head_bias, labels, valid,
    grad, head_sum, bias_sum, loss_sum, cells, lab, lab_t, val, val_t, padded_head,
):
    rows, chans = mixed.shape[0], mixed.shape[1]
    bins, real = padded_head.shape[0], head.shape[0]
    half = rows // 2
    size = rows * half
    length = size + half
    for s, got in ((0, near), (2, far), (1, got1), (3, got3)):
        q = place[0] ^ s
        cells[pl.ds(pl.multiple_of(q * size, size), size), :] = got[:size, :].astype(F32)
        cells[pl.ds(pl.multiple_of(4 * size + q * half, half), half), :] = got[size:length, :].astype(F32)
    notes = [cells[4 * size + q * half : 4 * size + (q + 1) * half, :] for q in range(4)]
    for top in range(2):
        base = top * 2 * rows
        lab_t[top * half : (top + 1) * half, :] = jnp.concatenate(
            [n[:, base : base + rows] for n in notes], axis=1
        )
        val_t[top * half : (top + 1) * half, :] = jnp.concatenate(
            [n[:, base + rows : base + 2 * rows] for n in notes], axis=1
        )
    padded_head[...] = jnp.zeros_like(padded_head)
    padded_head[:real, :] = head[...].astype(F32)
    single = padded_head[...]
    blank = jnp.zeros_like(single)
    both = jnp.concatenate(
        [jnp.concatenate([single, blank], axis=1), jnp.concatenate([blank, single], axis=1)], axis=0
    ).astype(BF16)
    thrice = jnp.concatenate([single, single, single], axis=0).T.astype(BF16)
    single = single.astype(BF16)
    line = lax.broadcasted_iota(jnp.int32, (bins, real), 0)
    across = lax.broadcasted_iota(jnp.int32, (bins, real), 1)
    bias = jnp.sum(jnp.where(line == across, head_bias[...], 0.0), axis=1, keepdims=True)
    bias = jnp.where(lax.broadcasted_iota(jnp.int32, (bins, 1), 0) < real, bias, FAR_BELOW)
    lab[...] = labels[...].astype(F32)
    val[...] = valid[...].astype(F32)
    bin_ids = lax.broadcasted_iota(jnp.int32, (bins, LANES), 0).astype(F32)
    head_sum[...] = jnp.zeros_like(head_sum)
    bias_sum[...] = jnp.zeros_like(bias_sum)
    loss_sum[...] = jnp.zeros_like(loss_sum)

    def step(i, carry):
        other = cells[pl.ds(i, LANES, stride=half), :].astype(BF16)
        logits_t = lax.dot_general(both, other, (((1,), (1,)), ((), ())), preferred_element_type=F32)
        pair = jnp.concatenate([mixed[i], mixed[i + half]], axis=1)
        logits = jnp.dot(single, pair, preferred_element_type=F32)
        pieces = []
        for d in range(2):
            at = pl.ds(i + d * half, 1)
            own = logits[:, d * LANES : (d + 1) * LANES] + bias
            far = logits_t[d * bins : (d + 1) * bins] + bias
            sym = 0.5 * (own + far)
            peak = jnp.max(sym, axis=0, keepdims=True)
            raised = jnp.exp(sym - peak)
            total = jnp.sum(raised, axis=0, keepdims=True)
            lse = peak + jnp.log(total)
            hot = bin_ids == lab[at, :]
            hot_t = bin_ids == lab_t[at, :]
            mask, mask_t = val[at, :], val_t[at, :]
            picked = jnp.sum(jnp.where(hot, sym, 0.0), axis=0, keepdims=True)
            loss_sum[...] += mask * (lse - picked)
            share = raised * ((mask + mask_t) / total)
            pieces.append(share - jnp.where(hot, mask, 0.0) - jnp.where(hot_t, mask_t, 0.0))
        bias_sum[...] += pieces[0] + pieces[1]
        g = jnp.concatenate(pieces, axis=1)
        first = g.astype(BF16).astype(F32)
        rest = g - first
        second = rest.astype(BF16).astype(F32)
        split = jnp.concatenate([first, second, rest - second], axis=0).astype(BF16)
        out = jnp.dot(thrice, split, preferred_element_type=F32)
        grad[i] = out[:, :LANES]
        grad[i + half] = out[:, LANES:]
        head_sum[...] += lax.dot_general(
            split, pair, (((1,), (1,)), ((), ())), preferred_element_type=F32
        )
        return carry

    lax.fori_loop(0, half, step, 0, unroll=UNROLL)


def scale_of(count):
    return 0.5 / jnp.maximum(count[0:1, 0:1], 1.0)


def kernel_grad_kernel(
    place, count, grad, wide, head_sum, bias_sum, loss_sum,
    low, top, bottom, out0, out1, out2, out3, total, sheet,
):
    rows, chans = grad.shape[0], grad.shape[1]
    bins = bias_sum.shape[0]
    scale = scale_of(count)
    total[...] = jnp.zeros_like(total)

    def step(p, carry):
        i = 2 * p
        a = (grad[i] * scale).astype(BF16)
        b = (grad[i + 1] * scale).astype(BF16)
        low[i] = a
        low[i + 1] = b
        total[...] += lax.dot_general(
            pair_windows(wide, i),
            jnp.concatenate([a, b], axis=1),
            (((1,), (1,)), ((), ())),
            preferred_element_type=F32,
        )
        return carry

    lax.fori_loop(0, rows // 2, step, 0, unroll=UNROLL)
    top[...] = low[:STEP]
    bottom[...] = low[rows - STEP :]
    half = total.shape[0] // 2
    sheet[...] = jnp.zeros_like(sheet)
    sheet[:half, :] = jnp.concatenate([total[:half], total[half:]], axis=1)
    h = (head_sum[:bins] + head_sum[bins : 2 * bins] + head_sum[2 * bins :]) * scale
    sheet[half : half + bins, :chans] = h
    note = half + bins
    sheet[note : note + 1, :bins] = jnp.sum(bias_sum[...].T, axis=0, keepdims=True) * scale
    sheet[note + 1 : note + 2, :1] = jnp.sum(loss_sum[...], axis=1, keepdims=True)
    quarter = sheet.shape[0] // 4
    for s, out in enumerate((out0, out1, out2, out3)):
        out[...] = sheet[pl.ds(pl.multiple_of((place[0] ^ s) * quarter, 8), quarter), :]


def backward_kernel(count, low, up, down, left, right, grad, feat, weight, out, wide):
    rows, chans = grad.shape[0], grad.shape[1]
    scale = scale_of(count)
    spread_columns(low, up, down, left, right, wide)
    taps = weight.shape[0] // chans
    kernel = jnp.concatenate(
        [weight[(taps - 1 - t) * chans : (taps - t) * chans, :].astype(F32) for t in range(taps)],
        axis=1,
    ).astype(BF16)

    def step(p, carry):
        i = 2 * p
        back = jnp.dot(kernel, pair_windows(wide, i), preferred_element_type=F32)
        for d in range(2):
            v = feat[i + d].astype(F32)
            slope = jnp.where(v > 0, 1.0, jnp.exp(jnp.minimum(v, 0.0)))
            out[i + d] = (
                grad[i + d] * scale + slope * back[:, d * LANES : (d + 1) * LANES]
            ).astype(BF16)
        return carry

    lax.fori_loop(0, rows // 2, step, 0, unroll=UNROLL)


def finish_kernel(
    place, count, got0, got1, got2, got3, kernel_grad, head_grad, bias_grad, loss, sheet
):
    quarter = got0.shape[0]
    for s, got in enumerate((got0, got1, got2, got3)):
        sheet[pl.ds(pl.multiple_of((place[0] ^ s) * quarter, 8), quarter), :] = got[...]
    half, chans = kernel_grad.shape[0] // 2, kernel_grad.shape[1]
    bins = head_grad.shape[0]
    kernel_grad[:half, :] = sheet[:half, :chans]
    kernel_grad[half:, :] = sheet[:half, chans:]
    head_grad[...] = sheet[half : half + bins, :chans]
    note = half + -(-bins // 8) * 8
    bias_grad[...] = sheet[note : note + 1, :bins]
    loss[...] = sheet[note + 1 : note + 2, :1] / jnp.maximum(count[0:1, 0:1], 1.0)


def borders(own, top, bottom):
    rows, chans, _ = own.shape
    up = shifted(bottom, "row", True)
    down = shifted(top, "row", False)
    groups = (rows + 2 * STEP) // 16
    first, last = run(
        pack_kernel, [shape((groups, chans, LANES), BF16)] * 2, (own, up, down), micros=8
    )
    left = shifted(last, "col", True)
    right = shifted(first, "col", False)
    return up, down, left, right


def partners(stage):
    if stage < 2:
        return lambda m: lambda r, c: (r ^ (m << (2 * stage)), c)
    if stage == 2:
        return lambda m: lambda r, c: (r ^ ((m & 1) << 4), c ^ (m >> 1))
    return lambda m: lambda r, c: (r, c ^ (m << 1))


def total_small(value, stages):
    for stage in stages:
        to = partners(stage)
        value = (value + send(value, to(1))) + (send(value, to(2)) + send(value, to(3)))
    return value


def mirrored(pay_near, pay_far, parts):
    length = pay_near.shape[0] // 2
    pay_near = send(pay_near, lambda r, c: (r, c ^ 2))
    near = send(pay_near, lambda r, c: (parts * (c ^ 2) + r % parts, r // parts))
    far = send(pay_far, lambda r, c: (parts * c + (r % parts ^ 2), r // parts))
    mate = lambda r, c: (r ^ 1, c)
    return pay_near, (near, far, send(near[length:], mate), send(far[length:], mate))


def total_quarters(quarters):
    near = partners(0)
    a, b, c, d = quarters
    part = (a + send(b, near(1))) + (send(c, near(2)) + send(d, near(3)))
    for stage in (1, 2, 3):
        to = partners(stage)
        part = (part + send(part, to(1))) + (send(part, to(2)) + send(part, to(3)))
    return [part] + [send(part, near(m)) for m in (1, 2, 3)]


def per_device(features, conv_weight, head_weight, head_bias, labels, valid):
    rows, cols, chans = features.shape
    bins = head_weight.shape[1]
    parts = cols // rows
    place = (lax.axis_index("row") % parts).astype(jnp.int32).reshape(1)
    feat = features.transpose(0, 2, 1)
    weight = conv_weight.reshape(-1, chans)
    tall = -(-bins // 8) * 8
    tile = (rows, chans, LANES)
    edge = (STEP, chans, LANES)
    act, top, bottom, counted, feat, valid = run(
        activate_kernel,
        [shape(tile, BF16), shape(edge, BF16), shape(edge, BF16), shape((8, LANES), F32)]
        + [shape(tile, BF16), shape(valid.shape, jnp.int32)],
        (feat, valid),
        micros=1,
    )
    around = borders(act, top, bottom)
    counted = total_small(counted, (1, 2))
    counted, act = lax.optimization_barrier((counted, act))
    length = (rows + 1) * rows // 2
    wide, mixed, pay_near, pay_far = run(
        forward_kernel,
        [shape((rows + 2 * STEP, 3 * chans, LANES), BF16), shape(tile, BF16)]
        + [shape((2 * length, LANES), BF16)] * 2,
        (place, act, *around, feat, weight, labels, valid),
        scratch=[pltpu.VMEM(((rows + 1) * LANES, chans), F32)],
        scalars=1,
        micros=5,
    )
    passed, got = mirrored(pay_near, pay_far, parts)
    _, counted = lax.optimization_barrier((passed, counted))
    count = total_small(counted, (3, 0))
    grad, head_sum, bias_sum, loss_sum = run(
        softmax_kernel,
        [
            shape(tile, F32),
            shape((3 * tall, chans), F32),
            shape((tall, LANES), F32),
            shape((1, LANES), F32),
        ],
        (place, *got, mixed, head_weight.T, head_bias.reshape(1, bins), labels, valid),
        scratch=[pltpu.VMEM((length * 4, LANES), F32)]
        + [pltpu.VMEM((rows, LANES), F32)] * 4
        + [pltpu.VMEM((tall, chans), F32)],
        scalars=1,
        micros=5,
    )
    half = 9 * chans // 2
    lines = -(-(half + tall + 8) // 32) * 32
    low, top, bottom, *quarters = run(
        kernel_grad_kernel,
        [shape(tile, BF16), shape(edge, BF16), shape(edge, BF16)]
        + [shape((lines // 4, LANES), F32)] * 4,
        (place, count, grad, wide, head_sum, bias_sum, loss_sum),
        scratch=[pltpu.VMEM((9 * chans, chans), F32), pltpu.VMEM((lines, LANES), F32)],
        scalars=1,
        micros=3,
    )
    sums = total_quarters(quarters)
    around = borders(low, top, bottom)
    (grad_features,) = run(
        backward_kernel,
        [shape(tile, BF16)],
        (count, low, *around, grad, feat, weight),
        scratch=[pltpu.VMEM((rows + 2 * STEP, 3 * chans, LANES), BF16)],
        micros=4,
    )
    kernel_grad, head_grad, bias_grad, loss = run(
        finish_kernel,
        [
            shape((9 * chans, chans), F32),
            shape((bins, chans), F32),
            shape((1, bins), F32),
            shape((1, 1), F32),
        ],
        (place, count, *sums),
        scratch=[pltpu.VMEM((lines, LANES), F32)],
        scalars=1,
        micros=1,
    )
    return (
        loss.reshape(()),
        grad_features.transpose(0, 2, 1),
        kernel_grad.reshape(conv_weight.shape),
        head_grad.T,
        bias_grad.reshape(bins),
    )


def solution(mesh):
    placed = (P("row", "col", None), P(), P(), P(), P("row", "col"), P("row", "col"))
    return jax.shard_map(
        per_device,
        mesh=mesh,
        in_specs=placed,
        out_specs=(P(), P("row", "col", None), P(), P(), P()),
        check_vma=False,
    )
```

```python
import jax
import jax.numpy as jnp
from jax import lax
from jax.experimental import pallas as pl
from jax.experimental.pallas import tpu as pltpu
from jax.sharding import PartitionSpec as P

STEP = 8
GRID = ("row", "col")
F32, BF16 = jnp.float32, jnp.bfloat16
LANES = 128
UNROLL = 8
FAR_BELOW = -1e30
VMEM = pl.BlockSpec(memory_space=pltpu.VMEM)
SMEM = pl.BlockSpec(memory_space=pltpu.SMEM)


def run(body, outs, args, scratch=(), scalars=0, micros=3):
    return pl.pallas_call(
        body,
        out_shape=outs,
        in_specs=[SMEM] * scalars + [VMEM] * (len(args) - scalars),
        out_specs=[VMEM] * len(outs),
        scratch_shapes=list(scratch),
        compiler_params=pltpu.CompilerParams(vmem_limit_bytes=48 * 1024 * 1024),
        cost_estimate=pl.CostEstimate(
            flops=0, bytes_accessed=int(micros * 3.6e6), transcendentals=0
        ),
    )(*args)


def shape(dims, kind):
    return jax.ShapeDtypeStruct(dims, kind)


def send(block, target):
    nrow, ncol = lax.axis_size("row"), lax.axis_size("col")
    pairs = []
    for r in range(nrow):
        for c in range(ncol):
            r2, c2 = target(r, c)
            pairs.append((r * ncol + c, r2 * ncol + c2))
    return lax.ppermute(block, GRID, pairs)


def swapped(to_mate, to_other, axis):
    count = lax.axis_size(axis)
    mates = [(i, i ^ 1) for i in range(count)]
    others = [(i, i + 1 if i % 2 else i - 1) for i in range(1, count - 1)]
    return lax.ppermute(to_mate, axis, mates), lax.ppermute(to_other, axis, others)


def activate_kernel(place, feat, valid, act, mate, other, counted, kept_feat, kept_valid):
    rows = feat.shape[0]

    def step(i, carry):
        kept_feat[i] = feat[i]
        v = feat[i].astype(F32)
        near = v * (1.0 + v * (0.5 + v * (1.0 / 6.0 + v * (1.0 / 24.0))))
        low = jnp.where(v > -0.03, near, jnp.exp(jnp.minimum(v, 0.0)) - 1.0)
        act[i] = jnp.where(v > 0, v, low).astype(BF16)
        return carry

    lax.fori_loop(0, rows, step, 0, unroll=4)
    share_edges(place, act, mate, other)
    lines = jnp.sum(valid[...].astype(F32), axis=0, keepdims=True)
    kept_valid[...] = valid[...]
    counted[...] = jnp.broadcast_to(jnp.sum(lines, axis=1, keepdims=True), counted.shape)


def share_edges(place, own, mate, other):
    last = own.shape[0] - STEP
    low = (1 - place[0] % 2) * last
    mate[...] = own[pl.ds(low, STEP)]
    other[...] = own[pl.ds(last - low, STEP)]


def settle_edges(place, mate, other, edges):
    odd = place[0] % 2
    edges[pl.ds((1 - odd) * STEP, STEP)] = mate[...]
    edges[pl.ds(odd * STEP, STEP)] = other[...]


def row_of(own, edges, at):
    rows = own.shape[0]
    if at < STEP:
        return edges[at]
    if at < STEP + rows:
        return own[at - STEP]
    return edges[at - rows]


def pack_kernel(place, own, mate, other, to_mate, to_other, edges, sides):
    chans = own.shape[1]
    lane = lax.broadcasted_iota(jnp.int32, (chans, LANES), 1) // STEP
    settle_edges(place, mate, other, edges)
    for group in range(sides.shape[1]):
        low = jnp.zeros((chans, LANES), F32)
        high = jnp.zeros((chans, LANES), F32)
        for slot in range(16):
            x = row_of(own, edges, group * 16 + slot).astype(F32)
            here = lane == slot
            low = jnp.where(here, pltpu.roll(x, (STEP * slot) % LANES, 1), low)
            high = jnp.where(here, pltpu.roll(x, (STEP * slot + STEP) % LANES, 1), high)
        sides[0, group] = low.astype(BF16)
        sides[1, group] = high.astype(BF16)
    to_mate[...] = sides[1 - (place[0] // 4)]
    to_other[...] = sides[(place[0] // 4)]


def spread_columns(place, own, mate, other, side_mate, side_other, edges, sides, wide):
    chans = own.shape[1]
    lane = lax.broadcasted_iota(jnp.int32, (chans, LANES), 1)
    settle_edges(place, mate, other, edges)
    sides[1 - (place[0] // 4)] = side_mate[...]
    sides[(place[0] // 4)] = side_other[...]
    for group in range(sides.shape[1]):
        from_left = sides[0, group].astype(F32)
        from_right = sides[1, group].astype(F32)
        for slot in range(16):
            at = group * 16 + slot
            middle = row_of(own, edges, at)
            x = middle.astype(F32)
            before = jnp.where(
                lane < STEP,
                pltpu.roll(from_left, (LANES - STEP * slot) % LANES, 1),
                pltpu.roll(x, STEP, 1),
            )
            after = jnp.where(
                lane >= LANES - STEP,
                pltpu.roll(from_right, (2 * LANES - STEP - STEP * slot) % LANES, 1),
                pltpu.roll(x, LANES - STEP, 1),
            )
            wide[at, 0:chans] = before.astype(BF16)
            wide[at, chans : 2 * chans] = middle
            wide[at, 2 * chans : 3 * chans] = after.astype(BF16)


def windows(wide, i):
    return jnp.concatenate([wide[i], wide[i + STEP], wide[i + 2 * STEP]], axis=0)


def pair_windows(wide, i):
    return jnp.concatenate([windows(wide, i), windows(wide, i + 1)], axis=1)


def forward_kernel(
    place, act, mate, other, side_mate, side_other, feat, weight, labels, valid,
    wide, mixed, pay_near, pay_far, turned, edges, sides,
):
    rows, chans = act.shape[0], act.shape[1]
    part = rows
    length = pay_near.shape[0] // 2
    spread_columns(place, act, mate, other, side_mate, side_other, edges, sides, wide)
    kernel = weight[...].astype(F32).T.astype(BF16)

    def step(p, carry):
        i = 2 * p
        out = jnp.dot(kernel, pair_windows(wide, i), preferred_element_type=F32)
        for d in range(2):
            total = feat[i + d].astype(F32) + out[:, d * LANES : (d + 1) * LANES]
            low = total.astype(BF16)
            mixed[i + d] = low
            turned[pl.ds(pl.multiple_of((i + d) * LANES, LANES), LANES), :] = low.astype(F32).T
        return carry

    lax.fori_loop(0, rows // 2, step, 0, unroll=UNROLL)
    turned[rows * LANES :, :] = jnp.concatenate(
        [labels[...].astype(F32).T, valid[...].astype(F32).T], axis=1
    )
    half = part // 2

    def pack(j, carry):
        for s in range(4):
            base = j * LANES + (place[0] % 4 ^ s) * part
            low = turned[pl.ds(pl.multiple_of(base, 16), half), :]
            high = turned[pl.ds(pl.multiple_of(base + half, 16), half), :]
            pay = pay_near if s < 2 else pay_far
            pay[pl.ds(pl.multiple_of(s % 2 * length + j * half, 16), half), :] = jnp.concatenate(
                [low, high], axis=1
            ).astype(BF16)
        return carry

    lax.fori_loop(0, rows + 1, pack, 0, unroll=3)


def softmax_kernel(
    place, near, far, got1, got3, mixed, head, head_bias, labels, valid,
    grad, head_sum, bias_sum, loss_sum, cells, lab, lab_t, val, val_t, padded_head,
):
    rows, chans = mixed.shape[0], mixed.shape[1]
    bins, real = padded_head.shape[0], head.shape[0]
    half = rows // 2
    size = rows * half
    length = size + half
    for s, got in ((0, near), (2, far), (1, got1), (3, got3)):
        q = place[0] % 4 ^ s
        cells[pl.ds(pl.multiple_of(q * size, size), size), :] = got[:size, :].astype(F32)
        cells[pl.ds(pl.multiple_of(4 * size + q * half, half), half), :] = got[size:length, :].astype(F32)
    notes = [cells[4 * size + q * half : 4 * size + (q + 1) * half, :] for q in range(4)]
    for top in range(2):
        base = top * 2 * rows
        lab_t[top * half : (top + 1) * half, :] = jnp.concatenate(
            [n[:, base : base + rows] for n in notes], axis=1
        )
        val_t[top * half : (top + 1) * half, :] = jnp.concatenate(
            [n[:, base + rows : base + 2 * rows] for n in notes], axis=1
        )
    padded_head[...] = jnp.zeros_like(padded_head)
    padded_head[:real, :] = head[...].astype(F32)
    single = padded_head[...]
    blank = jnp.zeros_like(single)
    both = jnp.concatenate(
        [jnp.concatenate([single, blank], axis=1), jnp.concatenate([blank, single], axis=1)], axis=0
    ).astype(BF16)
    thrice = jnp.concatenate([single, single, single], axis=0).T.astype(BF16)
    single = single.astype(BF16)
    line = lax.broadcasted_iota(jnp.int32, (bins, real), 0)
    across = lax.broadcasted_iota(jnp.int32, (bins, real), 1)
    bias = jnp.sum(jnp.where(line == across, head_bias[...], 0.0), axis=1, keepdims=True)
    bias = jnp.where(lax.broadcasted_iota(jnp.int32, (bins, 1), 0) < real, bias, FAR_BELOW)
    lab[...] = labels[...].astype(F32)
    val[...] = valid[...].astype(F32)
    bin_ids = lax.broadcasted_iota(jnp.int32, (bins, LANES), 0).astype(F32)
    head_sum[...] = jnp.zeros_like(head_sum)
    bias_sum[...] = jnp.zeros_like(bias_sum)
    loss_sum[...] = jnp.zeros_like(loss_sum)

    def step(i, carry):
        other = cells[pl.ds(i, LANES, stride=half), :].astype(BF16)
        logits_t = lax.dot_general(both, other, (((1,), (1,)), ((), ())), preferred_element_type=F32)
        pair = jnp.concatenate([mixed[i], mixed[i + half]], axis=1)
        logits = jnp.dot(single, pair, preferred_element_type=F32)
        pieces = []
        for d in range(2):
            at = pl.ds(i + d * half, 1)
            own = logits[:, d * LANES : (d + 1) * LANES] + bias
            far = logits_t[d * bins : (d + 1) * bins] + bias
            sym = 0.5 * (own + far)
            peak = jnp.max(sym, axis=0, keepdims=True)
            raised = jnp.exp(sym - peak)
            total = jnp.sum(raised, axis=0, keepdims=True)
            lse = peak + jnp.log(total)
            hot = bin_ids == lab[at, :]
            hot_t = bin_ids == lab_t[at, :]
            mask, mask_t = val[at, :], val_t[at, :]
            picked = jnp.sum(jnp.where(hot, sym, 0.0), axis=0, keepdims=True)
            loss_sum[...] += mask * (lse - picked)
            share = raised * ((mask + mask_t) / total)
            pieces.append(share - jnp.where(hot, mask, 0.0) - jnp.where(hot_t, mask_t, 0.0))
        bias_sum[...] += pieces[0] + pieces[1]
        g = jnp.concatenate(pieces, axis=1)
        first = g.astype(BF16).astype(F32)
        rest = g - first
        second = rest.astype(BF16).astype(F32)
        split = jnp.concatenate([first, second, rest - second], axis=0).astype(BF16)
        out = jnp.dot(thrice, split, preferred_element_type=F32)
        grad[i] = out[:, :LANES]
        grad[i + half] = out[:, LANES:]
        head_sum[...] += lax.dot_general(
            split, pair, (((1,), (1,)), ((), ())), preferred_element_type=F32
        )
        return carry

    lax.fori_loop(0, half, step, 0, unroll=UNROLL)


def scale_of(count):
    return 0.5 / jnp.maximum(count[0:1, 0:1], 1.0)


def kernel_grad_kernel(
    place, count, grad, wide, head_sum, bias_sum, loss_sum,
    low, mate, other, out0, out1, out2, out3, total, sheet,
):
    rows, chans = grad.shape[0], grad.shape[1]
    bins = bias_sum.shape[0]
    scale = scale_of(count)
    total[...] = jnp.zeros_like(total)

    def step(p, carry):
        i = 2 * p
        a = (grad[i] * scale).astype(BF16)
        b = (grad[i + 1] * scale).astype(BF16)
        low[i] = a
        low[i + 1] = b
        total[...] += lax.dot_general(
            pair_windows(wide, i),
            jnp.concatenate([a, b], axis=1),
            (((1,), (1,)), ((), ())),
            preferred_element_type=F32,
        )
        return carry

    lax.fori_loop(0, rows // 2, step, 0, unroll=UNROLL)
    share_edges(place, low, mate, other)
    half = total.shape[0] // 2
    sheet[...] = jnp.zeros_like(sheet)
    sheet[:half, :] = jnp.concatenate([total[:half], total[half:]], axis=1)
    h = (head_sum[:bins] + head_sum[bins : 2 * bins] + head_sum[2 * bins :]) * scale
    sheet[half : half + bins, :chans] = h
    note = half + bins
    sheet[note : note + 1, :bins] = jnp.sum(bias_sum[...].T, axis=0, keepdims=True) * scale
    sheet[note + 1 : note + 2, :1] = jnp.sum(loss_sum[...], axis=1, keepdims=True)
    quarter = sheet.shape[0] // 4
    for s, out in enumerate((out0, out1, out2, out3)):
        out[...] = sheet[pl.ds(pl.multiple_of((place[0] % 4 ^ s) * quarter, 8), quarter), :]


def backward_kernel(
    place, count, low, mate, other, side_mate, side_other, grad, feat, weight, out, wide, edges, sides
):
    rows, chans = grad.shape[0], grad.shape[1]
    scale = scale_of(count)
    spread_columns(place, low, mate, other, side_mate, side_other, edges, sides, wide)
    taps = weight.shape[0] // chans
    kernel = jnp.concatenate(
        [weight[(taps - 1 - t) * chans : (taps - t) * chans, :].astype(F32) for t in range(taps)],
        axis=1,
    ).astype(BF16)

    def step(p, carry):
        i = 2 * p
        back = jnp.dot(kernel, pair_windows(wide, i), preferred_element_type=F32)
        for d in range(2):
            v = feat[i + d].astype(F32)
            slope = jnp.where(v > 0, 1.0, jnp.exp(jnp.minimum(v, 0.0)))
            out[i + d] = (
                grad[i + d] * scale + slope * back[:, d * LANES : (d + 1) * LANES]
            ).astype(BF16)
        return carry

    lax.fori_loop(0, rows // 2, step, 0, unroll=UNROLL)


def finish_kernel(
    place, count, got0, got1, got2, got3, kernel_grad, head_grad, bias_grad, loss, sheet
):
    quarter = got0.shape[0]
    for s, got in enumerate((got0, got1, got2, got3)):
        sheet[pl.ds(pl.multiple_of((place[0] % 4 ^ s) * quarter, 8), quarter), :] = got[...]
    half, chans = kernel_grad.shape[0] // 2, kernel_grad.shape[1]
    bins = head_grad.shape[0]
    kernel_grad[:half, :] = sheet[:half, :chans]
    kernel_grad[half:, :] = sheet[:half, chans:]
    head_grad[...] = sheet[half : half + bins, :chans]
    note = half + -(-bins // 8) * 8
    bias_grad[...] = sheet[note : note + 1, :bins]
    loss[...] = sheet[note + 1 : note + 2, :1] / jnp.maximum(count[0:1, 0:1], 1.0)


def border_buffers(rows, chans):
    groups = (rows + 2 * STEP) // 16
    return [
        pltpu.VMEM((2 * STEP, chans, LANES), BF16),
        pltpu.VMEM((2, groups, chans, LANES), BF16),
    ]


def borders(place, own, mate, other):
    rows, chans, _ = own.shape
    edges = swapped(mate, other, "row")
    groups = (rows + 2 * STEP) // 16
    sides = run(
        pack_kernel,
        [shape((groups, chans, LANES), BF16)] * 2,
        (place, own, *edges),
        scratch=border_buffers(rows, chans),
        scalars=1,
        micros=8,
    )
    return *edges, *swapped(*sides, "col")


def partners(stage):
    if stage < 2:
        return lambda m: lambda r, c: (r ^ (m << (2 * stage)), c)
    if stage == 2:
        return lambda m: lambda r, c: (r ^ ((m & 1) << 4), c ^ (m >> 1))
    return lambda m: lambda r, c: (r, c ^ (m << 1))


def total_small(value, stages):
    for stage in stages:
        to = partners(stage)
        value = (value + send(value, to(1))) + (send(value, to(2)) + send(value, to(3)))
    return value


def mirrored(pay_near, pay_far, parts):
    length = pay_near.shape[0] // 2
    pay_near = send(pay_near, lambda r, c: (r, c ^ 2))
    near = send(pay_near, lambda r, c: (parts * (c ^ 2) + r % parts, r // parts))
    far = send(pay_far, lambda r, c: (parts * c + (r % parts ^ 2), r // parts))
    mate = lambda r, c: (r ^ 1, c)
    return pay_near, (near, far, send(near[length:], mate), send(far[length:], mate))


def total_quarters(quarters):
    near = partners(0)
    a, b, c, d = quarters
    part = (a + send(b, near(1))) + (send(c, near(2)) + send(d, near(3)))
    for stage in (1, 2, 3):
        to = partners(stage)
        part = (part + send(part, to(1))) + (send(part, to(2)) + send(part, to(3)))
    return [part] + [send(part, near(m)) for m in (1, 2, 3)]


def per_device(features, conv_weight, head_weight, head_bias, labels, valid):
    rows, cols, chans = features.shape
    bins = head_weight.shape[1]
    parts = cols // rows
    place = lax.axis_index("row") % parts + 4 * (lax.axis_index("col") % 2)
    place = place.astype(jnp.int32).reshape(1)
    feat = features.transpose(0, 2, 1)
    weight = conv_weight.reshape(-1, chans)
    tall = -(-bins // 8) * 8
    tile = (rows, chans, LANES)
    edge = (STEP, chans, LANES)
    act, mate, other, counted, feat, valid = run(
        activate_kernel,
        [shape(tile, BF16), shape(edge, BF16), shape(edge, BF16), shape((8, LANES), F32)]
        + [shape(tile, BF16), shape(valid.shape, jnp.int32)],
        (place, feat, valid),
        scalars=1,
        micros=1,
    )
    around = borders(place, act, mate, other)
    counted = total_small(counted, (1, 2))
    counted, act = lax.optimization_barrier((counted, act))
    length = (rows + 1) * rows // 2
    wide, mixed, pay_near, pay_far = run(
        forward_kernel,
        [shape((rows + 2 * STEP, 3 * chans, LANES), BF16), shape(tile, BF16)]
        + [shape((2 * length, LANES), BF16)] * 2,
        (place, act, *around, feat, weight, labels, valid),
        scratch=[pltpu.VMEM(((rows + 1) * LANES, chans), F32)] + border_buffers(rows, chans),
        scalars=1,
        micros=5,
    )
    passed, got = mirrored(pay_near, pay_far, parts)
    _, counted = lax.optimization_barrier((passed, counted))
    count = total_small(counted, (3, 0))
    grad, head_sum, bias_sum, loss_sum = run(
        softmax_kernel,
        [
            shape(tile, F32),
            shape((3 * tall, chans), F32),
            shape((tall, LANES), F32),
            shape((1, LANES), F32),
        ],
        (place, *got, mixed, head_weight.T, head_bias.reshape(1, bins), labels, valid),
        scratch=[pltpu.VMEM((length * 4, LANES), F32)]
        + [pltpu.VMEM((rows, LANES), F32)] * 4
        + [pltpu.VMEM((tall, chans), F32)],
        scalars=1,
        micros=5,
    )
    half = 9 * chans // 2
    lines = -(-(half + tall + 8) // 32) * 32
    low, mate, other, *quarters = run(
        kernel_grad_kernel,
        [shape(tile, BF16), shape(edge, BF16), shape(edge, BF16)]
        + [shape((lines // 4, LANES), F32)] * 4,
        (place, count, grad, wide, head_sum, bias_sum, loss_sum),
        scratch=[pltpu.VMEM((9 * chans, chans), F32), pltpu.VMEM((lines, LANES), F32)],
        scalars=1,
        micros=3,
    )
    sums = total_quarters(quarters)
    around = borders(place, low, mate, other)
    (grad_features,) = run(
        backward_kernel,
        [shape(tile, BF16)],
        (place, count, low, *around, grad, feat, weight),
        scratch=[pltpu.VMEM((rows + 2 * STEP, 3 * chans, LANES), BF16)]
        + border_buffers(rows, chans),
        scalars=1,
        micros=4,
    )
    kernel_grad, head_grad, bias_grad, loss = run(
        finish_kernel,
        [
            shape((9 * chans, chans), F32),
            shape((bins, chans), F32),
            shape((1, bins), F32),
            shape((1, 1), F32),
        ],
        (place, count, *sums),
        scratch=[pltpu.VMEM((lines, LANES), F32)],
        scalars=1,
        micros=1,
    )
    return (
        loss.reshape(()),
        grad_features.transpose(0, 2, 1),
        kernel_grad.reshape(conv_weight.shape),
        head_grad.T,
        bias_grad.reshape(bins),
    )


def solution(mesh):
    placed = (P("row", "col", None), P(), P(), P(), P("row", "col"), P("row", "col"))
    return jax.shard_map(
        per_device,
        mesh=mesh,
        in_specs=placed,
        out_specs=(P(), P("row", "col", None), P(), P(), P()),
        check_vma=False,
    )
```

```python
import jax
import jax.numpy as jnp
from jax import lax
from jax.experimental import pallas as pl
from jax.experimental.pallas import tpu as pltpu
from jax.sharding import PartitionSpec as P

STEP = 8
GRID = ("row", "col")
F32, BF16 = jnp.float32, jnp.bfloat16
LANES = 128
UNROLL = 8
FAR_BELOW = -1e30
VMEM = pl.BlockSpec(memory_space=pltpu.VMEM)
SMEM = pl.BlockSpec(memory_space=pltpu.SMEM)


def run(body, outs, args, scratch=(), scalars=0, micros=3):
    return pl.pallas_call(
        body,
        out_shape=outs,
        in_specs=[SMEM] * scalars + [VMEM] * (len(args) - scalars),
        out_specs=[VMEM] * len(outs),
        scratch_shapes=list(scratch),
        compiler_params=pltpu.CompilerParams(vmem_limit_bytes=48 * 1024 * 1024),
        cost_estimate=pl.CostEstimate(
            flops=0, bytes_accessed=int(micros * 3.6e6), transcendentals=0
        ),
    )(*args)


def shape(dims, kind):
    return jax.ShapeDtypeStruct(dims, kind)


def send(block, target):
    nrow, ncol = lax.axis_size("row"), lax.axis_size("col")
    pairs = []
    for r in range(nrow):
        for c in range(ncol):
            r2, c2 = target(r, c)
            pairs.append((r * ncol + c, r2 * ncol + c2))
    return lax.ppermute(block, GRID, pairs)


def swapped(to_mate, to_other, axis):
    count = lax.axis_size(axis)
    mates = [(i, i ^ 1) for i in range(count)]
    others = [(i, i + 1 if i % 2 else i - 1) for i in range(1, count - 1)]
    return lax.ppermute(to_mate, axis, mates), lax.ppermute(to_other, axis, others)


def activate_kernel(place, feat, valid, act, mate, other, counted, kept_feat, kept_valid):
    rows = feat.shape[0]

    def step(i, carry):
        kept_feat[i] = feat[i]
        v = feat[i].astype(F32)
        near = v * (1.0 + v * (0.5 + v * (1.0 / 6.0 + v * (1.0 / 24.0))))
        low = jnp.where(v > -0.03, near, jnp.exp(jnp.minimum(v, 0.0)) - 1.0)
        act[i] = jnp.where(v > 0, v, low).astype(BF16)
        return carry

    lax.fori_loop(0, rows, step, 0, unroll=4)
    share_edges(place, act, mate, other)
    lines = jnp.sum(valid[...].astype(F32), axis=0, keepdims=True)
    kept_valid[...] = valid[...]
    counted[...] = jnp.broadcast_to(jnp.sum(lines, axis=1, keepdims=True), counted.shape)


def share_edges(place, own, mate, other):
    last = own.shape[0] - STEP
    low = (1 - place[0] % 2) * last
    mate[...] = own[pl.ds(low, STEP)]
    other[...] = own[pl.ds(last - low, STEP)]


def settle_edges(place, mate, other, edges):
    odd = place[0] % 2
    edges[pl.ds((1 - odd) * STEP, STEP)] = mate[...]
    edges[pl.ds(odd * STEP, STEP)] = other[...]


def row_of(own, edges, at):
    rows = own.shape[0]
    if at < STEP:
        return edges[at]
    if at < STEP + rows:
        return own[at - STEP]
    return edges[at - rows]


def pack_kernel(place, own, mate, other, to_mate, to_other, edges, sides):
    chans = own.shape[1]
    lane = lax.broadcasted_iota(jnp.int32, (chans, LANES), 1) // STEP
    settle_edges(place, mate, other, edges)
    for group in range(sides.shape[1]):
        low = jnp.zeros((chans, LANES), F32)
        high = jnp.zeros((chans, LANES), F32)
        for slot in range(16):
            x = row_of(own, edges, group * 16 + slot).astype(F32)
            here = lane == slot
            low = jnp.where(here, pltpu.roll(x, (STEP * slot) % LANES, 1), low)
            high = jnp.where(here, pltpu.roll(x, (STEP * slot + STEP) % LANES, 1), high)
        sides[0, group] = low.astype(BF16)
        sides[1, group] = high.astype(BF16)
    to_mate[...] = sides[1 - (place[0] // 4)]
    to_other[...] = sides[(place[0] // 4)]


def spread_columns(place, own, mate, other, side_mate, side_other, edges, sides, wide):
    chans = own.shape[1]
    lane = lax.broadcasted_iota(jnp.int32, (chans, LANES), 1)
    settle_edges(place, mate, other, edges)
    sides[1 - (place[0] // 4)] = side_mate[...]
    sides[(place[0] // 4)] = side_other[...]
    for group in range(sides.shape[1]):
        from_left = sides[0, group].astype(F32)
        from_right = sides[1, group].astype(F32)
        for slot in range(16):
            at = group * 16 + slot
            middle = row_of(own, edges, at)
            x = middle.astype(F32)
            before = jnp.where(
                lane < STEP,
                pltpu.roll(from_left, (LANES - STEP * slot) % LANES, 1),
                pltpu.roll(x, STEP, 1),
            )
            after = jnp.where(
                lane >= LANES - STEP,
                pltpu.roll(from_right, (2 * LANES - STEP - STEP * slot) % LANES, 1),
                pltpu.roll(x, LANES - STEP, 1),
            )
            wide[at, 0:chans] = before.astype(BF16)
            wide[at, chans : 2 * chans] = middle
            wide[at, 2 * chans : 3 * chans] = after.astype(BF16)


def windows(wide, i):
    return jnp.concatenate([wide[i], wide[i + STEP], wide[i + 2 * STEP]], axis=0)


def pair_windows(wide, i):
    return jnp.concatenate([windows(wide, i), windows(wide, i + 1)], axis=1)


def forward_kernel(
    place, act, mate, other, side_mate, side_other, feat, weight, labels, valid,
    wide, mixed, pay_near, pay_far, turned, edges, sides,
):
    rows, chans = act.shape[0], act.shape[1]
    part = rows
    length = pay_near.shape[0] // 2
    spread_columns(place, act, mate, other, side_mate, side_other, edges, sides, wide)
    kernel = weight[...].astype(F32).T.astype(BF16)

    def step(p, carry):
        i = 2 * p
        out = jnp.dot(kernel, pair_windows(wide, i), preferred_element_type=F32)
        for d in range(2):
            total = feat[i + d].astype(F32) + out[:, d * LANES : (d + 1) * LANES]
            low = total.astype(BF16)
            mixed[i + d] = low
            turned[pl.ds(pl.multiple_of((i + d) * LANES, LANES), LANES), :] = low.astype(F32).T
        return carry

    lax.fori_loop(0, rows // 2, step, 0, unroll=UNROLL)
    turned[rows * LANES :, :] = jnp.concatenate(
        [labels[...].astype(F32).T, valid[...].astype(F32).T], axis=1
    )
    half = part // 2

    def pack(j, carry):
        for s in range(4):
            base = j * LANES + (place[0] % 4 ^ s) * part
            low = turned[pl.ds(pl.multiple_of(base, 16), half), :]
            high = turned[pl.ds(pl.multiple_of(base + half, 16), half), :]
            pay = pay_near if s < 2 else pay_far
            pay[pl.ds(pl.multiple_of(s % 2 * length + j * half, 16), half), :] = jnp.concatenate(
                [low, high], axis=1
            ).astype(BF16)
        return carry

    lax.fori_loop(0, rows + 1, pack, 0, unroll=3)


def softmax_kernel(
    place, near, far, got1, got3, mixed, head, head_bias, labels, valid,
    grad, head_sum, bias_sum, loss_sum, cells, lab, lab_t, val, val_t, padded_head,
):
    rows, chans = mixed.shape[0], mixed.shape[1]
    bins, real = padded_head.shape[0], head.shape[0]
    half = rows // 2
    size = rows * half
    length = size + half
    for s, got in ((0, near), (2, far), (1, got1), (3, got3)):
        q = place[0] % 4 ^ s
        cells[pl.ds(pl.multiple_of(q * size, size), size), :] = got[:size, :].astype(F32)
        cells[pl.ds(pl.multiple_of(4 * size + q * half, half), half), :] = got[size:length, :].astype(F32)
    notes = [cells[4 * size + q * half : 4 * size + (q + 1) * half, :] for q in range(4)]
    for top in range(2):
        base = top * 2 * rows
        lab_t[top * half : (top + 1) * half, :] = jnp.concatenate(
            [n[:, base : base + rows] for n in notes], axis=1
        )
        val_t[top * half : (top + 1) * half, :] = jnp.concatenate(
            [n[:, base + rows : base + 2 * rows] for n in notes], axis=1
        )
    padded_head[...] = jnp.zeros_like(padded_head)
    padded_head[:real, :] = head[...].astype(F32)
    single = padded_head[...]
    blank = jnp.zeros_like(single)
    both = jnp.concatenate(
        [jnp.concatenate([single, blank], axis=1), jnp.concatenate([blank, single], axis=1)], axis=0
    ).astype(BF16)
    thrice = jnp.concatenate([single, single, single], axis=0).T.astype(BF16)
    single = single.astype(BF16)
    line = lax.broadcasted_iota(jnp.int32, (bins, real), 0)
    across = lax.broadcasted_iota(jnp.int32, (bins, real), 1)
    bias = jnp.sum(jnp.where(line == across, head_bias[...], 0.0), axis=1, keepdims=True)
    bias = jnp.where(lax.broadcasted_iota(jnp.int32, (bins, 1), 0) < real, bias, FAR_BELOW)
    lab[...] = labels[...].astype(F32)
    val[...] = valid[...].astype(F32)
    bin_ids = lax.broadcasted_iota(jnp.int32, (bins, LANES), 0).astype(F32)
    head_sum[...] = jnp.zeros_like(head_sum)
    bias_sum[...] = jnp.zeros_like(bias_sum)
    loss_sum[...] = jnp.zeros_like(loss_sum)

    def step(i, carry):
        other = cells[pl.ds(i, LANES, stride=half), :].astype(BF16)
        logits_t = lax.dot_general(both, other, (((1,), (1,)), ((), ())), preferred_element_type=F32)
        pair = jnp.concatenate([mixed[i], mixed[i + half]], axis=1)
        logits = jnp.dot(single, pair, preferred_element_type=F32)
        pieces = []
        for d in range(2):
            at = pl.ds(i + d * half, 1)
            own = logits[:, d * LANES : (d + 1) * LANES] + bias
            far = logits_t[d * bins : (d + 1) * bins] + bias
            sym = 0.5 * (own + far)
            peak = jnp.max(sym, axis=0, keepdims=True)
            raised = jnp.exp(sym - peak)
            total = jnp.sum(raised, axis=0, keepdims=True)
            lse = peak + jnp.log(total)
            hot = bin_ids == lab[at, :]
            hot_t = bin_ids == lab_t[at, :]
            mask, mask_t = val[at, :], val_t[at, :]
            picked = jnp.sum(jnp.where(hot, sym, 0.0), axis=0, keepdims=True)
            loss_sum[...] += mask * (lse - picked)
            share = raised * ((mask + mask_t) / total)
            pieces.append(share - jnp.where(hot, mask, 0.0) - jnp.where(hot_t, mask_t, 0.0))
        bias_sum[...] += pieces[0] + pieces[1]
        g = jnp.concatenate(pieces, axis=1)
        first = g.astype(BF16).astype(F32)
        rest = g - first
        second = rest.astype(BF16).astype(F32)
        split = jnp.concatenate([first, second, rest - second], axis=0).astype(BF16)
        out = jnp.dot(thrice, split, preferred_element_type=F32)
        grad[i] = out[:, :LANES]
        grad[i + half] = out[:, LANES:]
        head_sum[...] += lax.dot_general(
            split, pair, (((1,), (1,)), ((), ())), preferred_element_type=F32
        )
        return carry

    lax.fori_loop(0, half, step, 0, unroll=UNROLL)


def scale_of(count):
    return 0.5 / jnp.maximum(count[0:1, 0:1], 1.0)


def kernel_grad_kernel(
    place, count, grad, wide, head_sum, bias_sum, loss_sum,
    low, mate, other, out0, out1, out2, out3, total, sheet,
):
    rows, chans = grad.shape[0], grad.shape[1]
    bins = bias_sum.shape[0]
    scale = scale_of(count)
    total[...] = jnp.zeros_like(total)

    def step(p, carry):
        i = 2 * p
        a = (grad[i] * scale).astype(BF16)
        b = (grad[i + 1] * scale).astype(BF16)
        low[i] = a
        low[i + 1] = b
        total[...] += lax.dot_general(
            pair_windows(wide, i),
            jnp.concatenate([a, b], axis=1),
            (((1,), (1,)), ((), ())),
            preferred_element_type=F32,
        )
        return carry

    lax.fori_loop(0, rows // 2, step, 0, unroll=UNROLL)
    share_edges(place, low, mate, other)
    half = total.shape[0] // 2
    sheet[...] = jnp.zeros_like(sheet)
    sheet[:half, :] = jnp.concatenate([total[:half], total[half:]], axis=1)
    h = (head_sum[:bins] + head_sum[bins : 2 * bins] + head_sum[2 * bins :]) * scale
    sheet[half : half + bins, :chans] = h
    note = half + bins
    sheet[note : note + 1, :bins] = jnp.sum(bias_sum[...].T, axis=0, keepdims=True) * scale
    sheet[note + 1 : note + 2, :1] = jnp.sum(loss_sum[...], axis=1, keepdims=True)
    quarter = sheet.shape[0] // 4
    for s, out in enumerate((out0, out1, out2, out3)):
        out[...] = sheet[pl.ds(pl.multiple_of((place[0] % 4 ^ s) * quarter, 8), quarter), :]


def backward_kernel(
    place, count, low, mate, other, side_mate, side_other, grad, feat, weight, out, wide, edges, sides
):
    rows, chans = grad.shape[0], grad.shape[1]
    scale = scale_of(count)
    spread_columns(place, low, mate, other, side_mate, side_other, edges, sides, wide)
    taps = weight.shape[0] // chans
    kernel = jnp.concatenate(
        [weight[(taps - 1 - t) * chans : (taps - t) * chans, :].astype(F32) for t in range(taps)],
        axis=1,
    ).astype(BF16)

    def step(p, carry):
        i = 2 * p
        back = jnp.dot(kernel, pair_windows(wide, i), preferred_element_type=F32)
        for d in range(2):
            v = feat[i + d].astype(F32)
            slope = jnp.where(v > 0, 1.0, jnp.exp(jnp.minimum(v, 0.0)))
            out[i + d] = (
                grad[i + d] * scale + slope * back[:, d * LANES : (d + 1) * LANES]
            ).astype(BF16)
        return carry

    lax.fori_loop(0, rows // 2, step, 0, unroll=UNROLL)


def finish_kernel(
    place, count, got0, got1, got2, got3, kernel_grad, head_grad, bias_grad, loss, sheet
):
    quarter = got0.shape[0]
    for s, got in enumerate((got0, got1, got2, got3)):
        sheet[pl.ds(pl.multiple_of((place[0] % 4 ^ s) * quarter, 8), quarter), :] = got[...]
    half, chans = kernel_grad.shape[0] // 2, kernel_grad.shape[1]
    bins = head_grad.shape[0]
    kernel_grad[:half, :] = sheet[:half, :chans]
    kernel_grad[half:, :] = sheet[:half, chans:]
    head_grad[...] = sheet[half : half + bins, :chans]
    note = half + -(-bins // 8) * 8
    bias_grad[...] = sheet[note : note + 1, :bins]
    loss[...] = sheet[note + 1 : note + 2, :1] / jnp.maximum(count[0:1, 0:1], 1.0)


def border_buffers(rows, chans):
    groups = (rows + 2 * STEP) // 16
    return [
        pltpu.VMEM((2 * STEP, chans, LANES), BF16),
        pltpu.VMEM((2, groups, chans, LANES), BF16),
    ]


def borders(place, own, mate, other):
    rows, chans, _ = own.shape
    edges = swapped(mate, other, "row")
    groups = (rows + 2 * STEP) // 16
    sides = run(
        pack_kernel,
        [shape((groups, chans, LANES), BF16)] * 2,
        (place, own, *edges),
        scratch=border_buffers(rows, chans),
        scalars=1,
        micros=8,
    )
    return *edges, *swapped(*sides, "col")


def partners(stage):
    if stage < 2:
        return lambda m: lambda r, c: (r ^ (m << (2 * stage)), c)
    if stage == 2:
        return lambda m: lambda r, c: (r ^ ((m & 1) << 4), c ^ (m >> 1))
    return lambda m: lambda r, c: (r, c ^ (m << 1))


def total_small(value, stages):
    for stage in stages:
        to = partners(stage)
        value = (value + send(value, to(1))) + (send(value, to(2)) + send(value, to(3)))
    return value


def mirrored(pay_near, pay_far, counted, parts):
    length = pay_near.shape[0] // 2
    pay_near = send(pay_near, lambda r, c: (r, c ^ 2))
    counted = total_small(counted, (3,))
    pay_near, pay_far, counted = lax.optimization_barrier((pay_near, pay_far, counted))
    near = send(pay_near, lambda r, c: (parts * (c ^ 2) + r % parts, r // parts))
    far = send(pay_far, lambda r, c: (parts * c + (r % parts ^ 2), r // parts))
    mate = lambda r, c: (r ^ 1, c)
    return (near, far, send(near[length:], mate), send(far[length:], mate)), total_small(counted, (0,))


def total_quarters(quarters):
    near = partners(0)
    a, b, c, d = quarters
    part = (a + send(b, near(1))) + (send(c, near(2)) + send(d, near(3)))
    for stage in (1, 2, 3):
        to = partners(stage)
        part = (part + send(part, to(1))) + (send(part, to(2)) + send(part, to(3)))
    return [part] + [send(part, near(m)) for m in (1, 2, 3)]


def per_device(features, conv_weight, head_weight, head_bias, labels, valid):
    rows, cols, chans = features.shape
    bins = head_weight.shape[1]
    parts = cols // rows
    place = lax.axis_index("row") % parts + 4 * (lax.axis_index("col") % 2)
    place = place.astype(jnp.int32).reshape(1)
    feat = features.transpose(0, 2, 1)
    weight = conv_weight.reshape(-1, chans)
    tall = -(-bins // 8) * 8
    tile = (rows, chans, LANES)
    edge = (STEP, chans, LANES)
    act, mate, other, counted, feat, valid = run(
        activate_kernel,
        [shape(tile, BF16), shape(edge, BF16), shape(edge, BF16), shape((8, LANES), F32)]
        + [shape(tile, BF16), shape(valid.shape, jnp.int32)],
        (place, feat, valid),
        scalars=1,
        micros=1,
    )
    around = borders(place, act, mate, other)
    counted = total_small(counted, (1, 2))
    counted, act = lax.optimization_barrier((counted, act))
    length = (rows + 1) * rows // 2
    wide, mixed, pay_near, pay_far = run(
        forward_kernel,
        [shape((rows + 2 * STEP, 3 * chans, LANES), BF16), shape(tile, BF16)]
        + [shape((2 * length, LANES), BF16)] * 2,
        (place, act, *around, feat, weight, labels, valid),
        scratch=[pltpu.VMEM(((rows + 1) * LANES, chans), F32)] + border_buffers(rows, chans),
        scalars=1,
        micros=5,
    )
    _, counted = lax.optimization_barrier((mixed, counted))
    got, count = mirrored(pay_near, pay_far, counted, parts)
    grad, head_sum, bias_sum, loss_sum = run(
        softmax_kernel,
        [
            shape(tile, F32),
            shape((3 * tall, chans), F32),
            shape((tall, LANES), F32),
            shape((1, LANES), F32),
        ],
        (place, *got, mixed, head_weight.T, head_bias.reshape(1, bins), labels, valid),
        scratch=[pltpu.VMEM((length * 4, LANES), F32)]
        + [pltpu.VMEM((rows, LANES), F32)] * 4
        + [pltpu.VMEM((tall, chans), F32)],
        scalars=1,
        micros=5,
    )
    half = 9 * chans // 2
    lines = -(-(half + tall + 8) // 32) * 32
    low, mate, other, *quarters = run(
        kernel_grad_kernel,
        [shape(tile, BF16), shape(edge, BF16), shape(edge, BF16)]
        + [shape((lines // 4, LANES), F32)] * 4,
        (place, count, grad, wide, head_sum, bias_sum, loss_sum),
        scratch=[pltpu.VMEM((9 * chans, chans), F32), pltpu.VMEM((lines, LANES), F32)],
        scalars=1,
        micros=3,
    )
    sums = total_quarters(quarters)
    around = borders(place, low, mate, other)
    (grad_features,) = run(
        backward_kernel,
        [shape(tile, BF16)],
        (place, count, low, *around, grad, feat, weight),
        scratch=[pltpu.VMEM((rows + 2 * STEP, 3 * chans, LANES), BF16)]
        + border_buffers(rows, chans),
        scalars=1,
        micros=4,
    )
    kernel_grad, head_grad, bias_grad, loss = run(
        finish_kernel,
        [
            shape((9 * chans, chans), F32),
            shape((bins, chans), F32),
            shape((1, bins), F32),
            shape((1, 1), F32),
        ],
        (place, count, *sums),
        scratch=[pltpu.VMEM((lines, LANES), F32)],
        scalars=1,
        micros=1,
    )
    return (
        loss.reshape(()),
        grad_features.transpose(0, 2, 1),
        kernel_grad.reshape(conv_weight.shape),
        head_grad.T,
        bias_grad.reshape(bins),
    )


def solution(mesh):
    placed = (P("row", "col", None), P(), P(), P(), P("row", "col"), P("row", "col"))
    return jax.shard_map(
        per_device,
        mesh=mesh,
        in_specs=placed,
        out_specs=(P(), P("row", "col", None), P(), P(), P()),
        check_vma=False,
    )
```

```python
import jax
import jax.numpy as jnp
from jax import lax
from jax.experimental import pallas as pl
from jax.experimental.pallas import tpu as pltpu
from jax.sharding import PartitionSpec as P

STEP = 8
GRID = ("row", "col")
F32, BF16 = jnp.float32, jnp.bfloat16
LANES = 128
UNROLL = 16
FAR_BELOW = -1e30
VMEM = pl.BlockSpec(memory_space=pltpu.VMEM)
SMEM = pl.BlockSpec(memory_space=pltpu.SMEM)


def run(body, outs, args, scratch=(), scalars=0, micros=3):
    return pl.pallas_call(
        body,
        out_shape=outs,
        in_specs=[SMEM] * scalars + [VMEM] * (len(args) - scalars),
        out_specs=[VMEM] * len(outs),
        scratch_shapes=list(scratch),
        compiler_params=pltpu.CompilerParams(vmem_limit_bytes=48 * 1024 * 1024),
        cost_estimate=pl.CostEstimate(
            flops=0, bytes_accessed=int(micros * 3.6e6), transcendentals=0
        ),
    )(*args)


def shape(dims, kind):
    return jax.ShapeDtypeStruct(dims, kind)


def send(block, target):
    nrow, ncol = lax.axis_size("row"), lax.axis_size("col")
    pairs = []
    for r in range(nrow):
        for c in range(ncol):
            r2, c2 = target(r, c)
            pairs.append((r * ncol + c, r2 * ncol + c2))
    return lax.ppermute(block, GRID, pairs)


def swapped(to_mate, to_other, axis):
    count = lax.axis_size(axis)
    mates = [(i, i ^ 1) for i in range(count)]
    others = [(i, i + 1 if i % 2 else i - 1) for i in range(1, count - 1)]
    return lax.ppermute(to_mate, axis, mates), lax.ppermute(to_other, axis, others)


def activate_kernel(place, feat, valid, act, mate, other, counted, kept_feat, kept_valid):
    rows = feat.shape[0]

    def step(i, carry):
        kept_feat[i] = feat[i]
        v = feat[i].astype(F32)
        near = v * (1.0 + v * (0.5 + v * (1.0 / 6.0 + v * (1.0 / 24.0))))
        low = jnp.where(v > -0.03, near, jnp.exp(jnp.minimum(v, 0.0)) - 1.0)
        act[i] = jnp.where(v > 0, v, low).astype(BF16)
        return carry

    lax.fori_loop(0, rows, step, 0, unroll=4)
    share_edges(place, act, mate, other)
    lines = jnp.sum(valid[...].astype(F32), axis=0, keepdims=True)
    kept_valid[...] = valid[...]
    counted[...] = jnp.broadcast_to(jnp.sum(lines, axis=1, keepdims=True), counted.shape)


def share_edges(place, own, mate, other):
    last = own.shape[0] - STEP
    low = (1 - place[0] % 2) * last
    mate[...] = own[pl.ds(low, STEP)]
    other[...] = own[pl.ds(last - low, STEP)]


def settle_edges(place, mate, other, edges):
    odd = place[0] % 2
    edges[pl.ds((1 - odd) * STEP, STEP)] = mate[...]
    edges[pl.ds(odd * STEP, STEP)] = other[...]


def row_of(own, edges, at):
    rows = own.shape[0]
    if at < STEP:
        return edges[at]
    if at < STEP + rows:
        return own[at - STEP]
    return edges[at - rows]


def pack_kernel(place, own, mate, other, to_mate, to_other, edges, sides):
    chans = own.shape[1]
    lane = lax.broadcasted_iota(jnp.int32, (chans, LANES), 1) // STEP
    settle_edges(place, mate, other, edges)
    for group in range(sides.shape[1]):
        low = jnp.zeros((chans, LANES), F32)
        high = jnp.zeros((chans, LANES), F32)
        for slot in range(16):
            x = row_of(own, edges, group * 16 + slot).astype(F32)
            here = lane == slot
            low = jnp.where(here, pltpu.roll(x, (STEP * slot) % LANES, 1), low)
            high = jnp.where(here, pltpu.roll(x, (STEP * slot + STEP) % LANES, 1), high)
        sides[0, group] = low.astype(BF16)
        sides[1, group] = high.astype(BF16)
    to_mate[...] = sides[1 - (place[0] // 4)]
    to_other[...] = sides[(place[0] // 4)]


def spread_columns(place, own, mate, other, side_mate, side_other, edges, sides, wide):
    chans = own.shape[1]
    lane = lax.broadcasted_iota(jnp.int32, (chans, LANES), 1)
    settle_edges(place, mate, other, edges)
    sides[1 - (place[0] // 4)] = side_mate[...]
    sides[(place[0] // 4)] = side_other[...]
    for group in range(sides.shape[1]):
        from_left = sides[0, group].astype(F32)
        from_right = sides[1, group].astype(F32)
        for slot in range(16):
            at = group * 16 + slot
            middle = row_of(own, edges, at)
            x = middle.astype(F32)
            before = jnp.where(
                lane < STEP,
                pltpu.roll(from_left, (LANES - STEP * slot) % LANES, 1),
                pltpu.roll(x, STEP, 1),
            )
            after = jnp.where(
                lane >= LANES - STEP,
                pltpu.roll(from_right, (2 * LANES - STEP - STEP * slot) % LANES, 1),
                pltpu.roll(x, LANES - STEP, 1),
            )
            wide[at, 0:chans] = before.astype(BF16)
            wide[at, chans : 2 * chans] = middle
            wide[at, 2 * chans : 3 * chans] = after.astype(BF16)


def windows(wide, i):
    return jnp.concatenate([wide[i], wide[i + STEP], wide[i + 2 * STEP]], axis=0)


def pair_windows(wide, i):
    return jnp.concatenate([windows(wide, i), windows(wide, i + 1)], axis=1)


def forward_kernel(
    place, act, mate, other, side_mate, side_other, feat, weight, labels, valid,
    wide, mixed, pay_near, pay_far, turned, edges, sides,
):
    rows, chans = act.shape[0], act.shape[1]
    part = rows
    length = pay_near.shape[0] // 2
    spread_columns(place, act, mate, other, side_mate, side_other, edges, sides, wide)
    kernel = weight[...].astype(F32).T.astype(BF16)

    def step(p, carry):
        i = 2 * p
        out = jnp.dot(kernel, pair_windows(wide, i), preferred_element_type=F32)
        for d in range(2):
            total = feat[i + d].astype(F32) + out[:, d * LANES : (d + 1) * LANES]
            low = total.astype(BF16)
            mixed[i + d] = low
            turned[pl.ds(pl.multiple_of((i + d) * LANES, LANES), LANES), :] = low.astype(F32).T
        return carry

    lax.fori_loop(0, rows // 2, step, 0, unroll=UNROLL)
    turned[rows * LANES :, :] = jnp.concatenate(
        [labels[...].astype(F32).T, valid[...].astype(F32).T], axis=1
    )
    half = part // 2

    def pack(j, carry):
        for s in range(4):
            base = j * LANES + (place[0] % 4 ^ s) * part
            low = turned[pl.ds(pl.multiple_of(base, 16), half), :]
            high = turned[pl.ds(pl.multiple_of(base + half, 16), half), :]
            pay = pay_near if s < 2 else pay_far
            pay[pl.ds(pl.multiple_of(s % 2 * length + j * half, 16), half), :] = jnp.concatenate(
                [low, high], axis=1
            ).astype(BF16)
        return carry

    lax.fori_loop(0, rows + 1, pack, 0, unroll=3)


def softmax_kernel(
    place, near, far, got1, got3, mixed, head, head_bias, labels, valid,
    grad, head_sum, bias_sum, loss_sum, cells, lab, lab_t, val, val_t, padded_head,
):
    rows, chans = mixed.shape[0], mixed.shape[1]
    bins, real = padded_head.shape[0], head.shape[0]
    half = rows // 2
    size = rows * half
    length = size + half
    for s, got in ((0, near), (2, far), (1, got1), (3, got3)):
        q = place[0] % 4 ^ s
        cells[pl.ds(pl.multiple_of(q * size, size), size), :] = got[:size, :].astype(F32)
        cells[pl.ds(pl.multiple_of(4 * size + q * half, half), half), :] = got[size:length, :].astype(F32)
    notes = [cells[4 * size + q * half : 4 * size + (q + 1) * half, :] for q in range(4)]
    for top in range(2):
        base = top * 2 * rows
        lab_t[top * half : (top + 1) * half, :] = jnp.concatenate(
            [n[:, base : base + rows] for n in notes], axis=1
        )
        val_t[top * half : (top + 1) * half, :] = jnp.concatenate(
            [n[:, base + rows : base + 2 * rows] for n in notes], axis=1
        )
    padded_head[...] = jnp.zeros_like(padded_head)
    padded_head[:real, :] = head[...].astype(F32)
    single = padded_head[...]
    blank = jnp.zeros_like(single)
    both = jnp.concatenate(
        [jnp.concatenate([single, blank], axis=1), jnp.concatenate([blank, single], axis=1)], axis=0
    ).astype(BF16)
    thrice = jnp.concatenate([single, single, single], axis=0).T.astype(BF16)
    single = single.astype(BF16)
    line = lax.broadcasted_iota(jnp.int32, (bins, real), 0)
    across = lax.broadcasted_iota(jnp.int32, (bins, real), 1)
    bias = jnp.sum(jnp.where(line == across, head_bias[...], 0.0), axis=1, keepdims=True)
    bias = jnp.where(lax.broadcasted_iota(jnp.int32, (bins, 1), 0) < real, bias, FAR_BELOW)
    lab[...] = labels[...].astype(F32)
    val[...] = valid[...].astype(F32)
    bin_ids = lax.broadcasted_iota(jnp.int32, (bins, LANES), 0).astype(F32)
    head_sum[...] = jnp.zeros_like(head_sum)
    bias_sum[...] = jnp.zeros_like(bias_sum)
    loss_sum[...] = jnp.zeros_like(loss_sum)

    def step(i, carry):
        other = cells[pl.ds(i, LANES, stride=half), :].astype(BF16)
        logits_t = lax.dot_general(both, other, (((1,), (1,)), ((), ())), preferred_element_type=F32)
        pair = jnp.concatenate([mixed[i], mixed[i + half]], axis=1)
        logits = jnp.dot(single, pair, preferred_element_type=F32)
        pieces = []
        for d in range(2):
            at = pl.ds(i + d * half, 1)
            own = logits[:, d * LANES : (d + 1) * LANES] + bias
            far = logits_t[d * bins : (d + 1) * bins] + bias
            sym = 0.5 * (own + far)
            peak = jnp.max(sym, axis=0, keepdims=True)
            raised = jnp.exp(sym - peak)
            total = jnp.sum(raised, axis=0, keepdims=True)
            lse = peak + jnp.log(total)
            hot = bin_ids == lab[at, :]
            hot_t = bin_ids == lab_t[at, :]
            mask, mask_t = val[at, :], val_t[at, :]
            picked = jnp.sum(jnp.where(hot, sym, 0.0), axis=0, keepdims=True)
            loss_sum[...] += mask * (lse - picked)
            share = raised * ((mask + mask_t) / total)
            pieces.append(share - jnp.where(hot, mask, 0.0) - jnp.where(hot_t, mask_t, 0.0))
        bias_sum[...] += pieces[0] + pieces[1]
        g = jnp.concatenate(pieces, axis=1)
        first = g.astype(BF16).astype(F32)
        rest = g - first
        second = rest.astype(BF16).astype(F32)
        split = jnp.concatenate([first, second, rest - second], axis=0).astype(BF16)
        out = jnp.dot(thrice, split, preferred_element_type=F32)
        grad[i] = out[:, :LANES]
        grad[i + half] = out[:, LANES:]
        head_sum[...] += lax.dot_general(
            split, pair, (((1,), (1,)), ((), ())), preferred_element_type=F32
        )
        return carry

    lax.fori_loop(0, half, step, 0, unroll=UNROLL)


def scale_of(count):
    return 0.5 / jnp.maximum(count[0:1, 0:1], 1.0)


def kernel_grad_kernel(
    place, count, grad, wide, head_sum, bias_sum, loss_sum,
    low, mate, other, out0, out1, out2, out3, total, sheet,
):
    rows, chans = grad.shape[0], grad.shape[1]
    bins = bias_sum.shape[0]
    scale = scale_of(count)
    total[...] = jnp.zeros_like(total)

    def step(p, carry):
        i = 2 * p
        a = (grad[i] * scale).astype(BF16)
        b = (grad[i + 1] * scale).astype(BF16)
        low[i] = a
        low[i + 1] = b
        total[...] += lax.dot_general(
            pair_windows(wide, i),
            jnp.concatenate([a, b], axis=1),
            (((1,), (1,)), ((), ())),
            preferred_element_type=F32,
        )
        return carry

    lax.fori_loop(0, rows // 2, step, 0, unroll=UNROLL)
    share_edges(place, low, mate, other)
    half = total.shape[0] // 2
    sheet[...] = jnp.zeros_like(sheet)
    sheet[:half, :] = jnp.concatenate([total[:half], total[half:]], axis=1)
    h = (head_sum[:bins] + head_sum[bins : 2 * bins] + head_sum[2 * bins :]) * scale
    sheet[half : half + bins, :chans] = h
    note = half + bins
    sheet[note : note + 1, :bins] = jnp.sum(bias_sum[...].T, axis=0, keepdims=True) * scale
    sheet[note + 1 : note + 2, :1] = jnp.sum(loss_sum[...], axis=1, keepdims=True)
    quarter = sheet.shape[0] // 4
    for s, out in enumerate((out0, out1, out2, out3)):
        out[...] = sheet[pl.ds(pl.multiple_of((place[0] % 4 ^ s) * quarter, 8), quarter), :]


def backward_kernel(
    place, count, low, mate, other, side_mate, side_other, grad, feat, weight, out, wide, edges, sides
):
    rows, chans = grad.shape[0], grad.shape[1]
    scale = scale_of(count)
    spread_columns(place, low, mate, other, side_mate, side_other, edges, sides, wide)
    taps = weight.shape[0] // chans
    kernel = jnp.concatenate(
        [weight[(taps - 1 - t) * chans : (taps - t) * chans, :].astype(F32) for t in range(taps)],
        axis=1,
    ).astype(BF16)

    def step(p, carry):
        i = 2 * p
        back = jnp.dot(kernel, pair_windows(wide, i), preferred_element_type=F32)
        for d in range(2):
            v = feat[i + d].astype(F32)
            slope = jnp.where(v > 0, 1.0, jnp.exp(jnp.minimum(v, 0.0)))
            out[i + d] = (
                grad[i + d] * scale + slope * back[:, d * LANES : (d + 1) * LANES]
            ).astype(BF16)
        return carry

    lax.fori_loop(0, rows // 2, step, 0, unroll=UNROLL)


def finish_kernel(
    place, count, got0, got1, got2, got3, kernel_grad, head_grad, bias_grad, loss, sheet
):
    quarter = got0.shape[0]
    for s, got in enumerate((got0, got1, got2, got3)):
        sheet[pl.ds(pl.multiple_of((place[0] % 4 ^ s) * quarter, 8), quarter), :] = got[...]
    half, chans = kernel_grad.shape[0] // 2, kernel_grad.shape[1]
    bins = head_grad.shape[0]
    kernel_grad[:half, :] = sheet[:half, :chans]
    kernel_grad[half:, :] = sheet[:half, chans:]
    head_grad[...] = sheet[half : half + bins, :chans]
    note = half + -(-bins // 8) * 8
    bias_grad[...] = sheet[note : note + 1, :bins]
    loss[...] = sheet[note + 1 : note + 2, :1] / jnp.maximum(count[0:1, 0:1], 1.0)


def border_buffers(rows, chans):
    groups = (rows + 2 * STEP) // 16
    return [
        pltpu.VMEM((2 * STEP, chans, LANES), BF16),
        pltpu.VMEM((2, groups, chans, LANES), BF16),
    ]


def borders(place, own, mate, other):
    rows, chans, _ = own.shape
    edges = swapped(mate, other, "row")
    groups = (rows + 2 * STEP) // 16
    sides = run(
        pack_kernel,
        [shape((groups, chans, LANES), BF16)] * 2,
        (place, own, *edges),
        scratch=border_buffers(rows, chans),
        scalars=1,
        micros=8,
    )
    return *edges, *swapped(*sides, "col")


def partners(stage):
    if stage < 2:
        return lambda m: lambda r, c: (r ^ (m << (2 * stage)), c)
    if stage == 2:
        return lambda m: lambda r, c: (r ^ ((m & 1) << 4), c ^ (m >> 1))
    return lambda m: lambda r, c: (r, c ^ (m << 1))


def total_small(value, stages):
    for stage in stages:
        to = partners(stage)
        value = (value + send(value, to(1))) + (send(value, to(2)) + send(value, to(3)))
    return value


def mirrored(pay_near, pay_far, parts):
    length = pay_near.shape[0] // 2
    pay_near = send(pay_near, lambda r, c: (r, c ^ 2))
    near = send(pay_near, lambda r, c: (parts * (c ^ 2) + r % parts, r // parts))
    far = send(pay_far, lambda r, c: (parts * c + (r % parts ^ 2), r // parts))
    mate = lambda r, c: (r ^ 1, c)
    return pay_near, (near, far, send(near[length:], mate), send(far[length:], mate))


def total_quarters(quarters):
    near = partners(0)
    a, b, c, d = quarters
    part = (a + send(b, near(1))) + (send(c, near(2)) + send(d, near(3)))
    for stage in (1, 2, 3):
        to = partners(stage)
        part = (part + send(part, to(1))) + (send(part, to(2)) + send(part, to(3)))
    return [part] + [send(part, near(m)) for m in (1, 2, 3)]


def per_device(features, conv_weight, head_weight, head_bias, labels, valid):
    rows, cols, chans = features.shape
    bins = head_weight.shape[1]
    parts = cols // rows
    place = lax.axis_index("row") % parts + 4 * (lax.axis_index("col") % 2)
    place = place.astype(jnp.int32).reshape(1)
    feat = features.transpose(0, 2, 1)
    weight = conv_weight.reshape(-1, chans)
    tall = -(-bins // 8) * 8
    tile = (rows, chans, LANES)
    edge = (STEP, chans, LANES)
    act, mate, other, counted, feat, valid = run(
        activate_kernel,
        [shape(tile, BF16), shape(edge, BF16), shape(edge, BF16), shape((8, LANES), F32)]
        + [shape(tile, BF16), shape(valid.shape, jnp.int32)],
        (place, feat, valid),
        scalars=1,
        micros=1,
    )
    around = borders(place, act, mate, other)
    counted = total_small(counted, (1, 2))
    counted, act = lax.optimization_barrier((counted, act))
    length = (rows + 1) * rows // 2
    wide, mixed, pay_near, pay_far = run(
        forward_kernel,
        [shape((rows + 2 * STEP, 3 * chans, LANES), BF16), shape(tile, BF16)]
        + [shape((2 * length, LANES), BF16)] * 2,
        (place, act, *around, feat, weight, labels, valid),
        scratch=[pltpu.VMEM(((rows + 1) * LANES, chans), F32)] + border_buffers(rows, chans),
        scalars=1,
        micros=5,
    )
    passed, got = mirrored(pay_near, pay_far, parts)
    _, counted = lax.optimization_barrier((passed, counted))
    count = total_small(counted, (3, 0))
    grad, head_sum, bias_sum, loss_sum = run(
        softmax_kernel,
        [
            shape(tile, F32),
            shape((3 * tall, chans), F32),
            shape((tall, LANES), F32),
            shape((1, LANES), F32),
        ],
        (place, *got, mixed, head_weight.T, head_bias.reshape(1, bins), labels, valid),
        scratch=[pltpu.VMEM((length * 4, LANES), F32)]
        + [pltpu.VMEM((rows, LANES), F32)] * 4
        + [pltpu.VMEM((tall, chans), F32)],
        scalars=1,
        micros=5,
    )
    half = 9 * chans // 2
    lines = -(-(half + tall + 8) // 32) * 32
    low, mate, other, *quarters = run(
        kernel_grad_kernel,
        [shape(tile, BF16), shape(edge, BF16), shape(edge, BF16)]
        + [shape((lines // 4, LANES), F32)] * 4,
        (place, count, grad, wide, head_sum, bias_sum, loss_sum),
        scratch=[pltpu.VMEM((9 * chans, chans), F32), pltpu.VMEM((lines, LANES), F32)],
        scalars=1,
        micros=3,
    )
    sums = total_quarters(quarters)
    around = borders(place, low, mate, other)
    (grad_features,) = run(
        backward_kernel,
        [shape(tile, BF16)],
        (place, count, low, *around, grad, feat, weight),
        scratch=[pltpu.VMEM((rows + 2 * STEP, 3 * chans, LANES), BF16)]
        + border_buffers(rows, chans),
        scalars=1,
        micros=4,
    )
    kernel_grad, head_grad, bias_grad, loss = run(
        finish_kernel,
        [
            shape((9 * chans, chans), F32),
            shape((bins, chans), F32),
            shape((1, bins), F32),
            shape((1, 1), F32),
        ],
        (place, count, *sums),
        scratch=[pltpu.VMEM((lines, LANES), F32)],
        scalars=1,
        micros=1,
    )
    return (
        loss.reshape(()),
        grad_features.transpose(0, 2, 1),
        kernel_grad.reshape(conv_weight.shape),
        head_grad.T,
        bias_grad.reshape(bins),
    )


def solution(mesh):
    placed = (P("row", "col", None), P(), P(), P(), P("row", "col"), P("row", "col"))
    return jax.shard_map(
        per_device,
        mesh=mesh,
        in_specs=placed,
        out_specs=(P(), P("row", "col", None), P(), P(), P()),
        check_vma=False,
    )
```

```python
import jax
import jax.numpy as jnp
from jax import lax
from jax.experimental import pallas as pl
from jax.experimental.pallas import tpu as pltpu
from jax.sharding import PartitionSpec as P

STEP = 8
GRID = ("row", "col")
F32, BF16 = jnp.float32, jnp.bfloat16
LANES = 128
UNROLL = 16
FAR_BELOW = -1e30
VMEM = pl.BlockSpec(memory_space=pltpu.VMEM)
SMEM = pl.BlockSpec(memory_space=pltpu.SMEM)


def run(body, outs, args, scratch=(), scalars=0, micros=3):
    return pl.pallas_call(
        body,
        out_shape=outs,
        in_specs=[SMEM] * scalars + [VMEM] * (len(args) - scalars),
        out_specs=[VMEM] * len(outs),
        scratch_shapes=list(scratch),
        compiler_params=pltpu.CompilerParams(vmem_limit_bytes=48 * 1024 * 1024),
        cost_estimate=pl.CostEstimate(
            flops=0, bytes_accessed=int(micros * 3.6e6), transcendentals=0
        ),
    )(*args)


def shape(dims, kind):
    return jax.ShapeDtypeStruct(dims, kind)


def send(block, target):
    nrow, ncol = lax.axis_size("row"), lax.axis_size("col")
    pairs = []
    for r in range(nrow):
        for c in range(ncol):
            r2, c2 = target(r, c)
            pairs.append((r * ncol + c, r2 * ncol + c2))
    return lax.ppermute(block, GRID, pairs)


def swapped(to_mate, to_other, axis):
    count = lax.axis_size(axis)
    mates = [(i, i ^ 1) for i in range(count)]
    others = [(i, i + 1 if i % 2 else i - 1) for i in range(1, count - 1)]
    return lax.ppermute(to_mate, axis, mates), lax.ppermute(to_other, axis, others)


def activate_kernel(place, feat, valid, act, mate, other, counted, kept_feat, kept_valid):
    rows = feat.shape[0]

    def step(i, carry):
        kept_feat[i] = feat[i]
        v = feat[i].astype(F32)
        near = v * (1.0 + v * (0.5 + v * (1.0 / 6.0 + v * (1.0 / 24.0))))
        low = jnp.where(v > -0.03, near, jnp.exp(jnp.minimum(v, 0.0)) - 1.0)
        act[i] = jnp.where(v > 0, v, low).astype(BF16)
        return carry

    lax.fori_loop(0, rows, step, 0, unroll=4)
    share_edges(place, act, mate, other)
    lines = jnp.sum(valid[...].astype(F32), axis=0, keepdims=True)
    kept_valid[...] = valid[...]
    counted[...] = jnp.broadcast_to(jnp.sum(lines, axis=1, keepdims=True), counted.shape)


def share_edges(place, own, mate, other):
    last = own.shape[0] - STEP
    low = (1 - place[0] % 2) * last
    mate[...] = own[pl.ds(low, STEP)]
    other[...] = own[pl.ds(last - low, STEP)]


def settle_edges(place, mate, other, edges):
    odd = place[0] % 2
    edges[pl.ds((1 - odd) * STEP, STEP)] = mate[...]
    edges[pl.ds(odd * STEP, STEP)] = other[...]


def row_of(own, edges, at):
    rows = own.shape[0]
    if at < STEP:
        return edges[at]
    if at < STEP + rows:
        return own[at - STEP]
    return edges[at - rows]


def pack_kernel(place, own, mate, other, to_mate, to_other, edges, sides):
    chans = own.shape[1]
    lane = lax.broadcasted_iota(jnp.int32, (chans, LANES), 1) // STEP
    settle_edges(place, mate, other, edges)
    for group in range(sides.shape[1]):
        low = jnp.zeros((chans, LANES), F32)
        high = jnp.zeros((chans, LANES), F32)
        for slot in range(16):
            x = row_of(own, edges, group * 16 + slot).astype(F32)
            here = lane == slot
            low = jnp.where(here, pltpu.roll(x, (STEP * slot) % LANES, 1), low)
            high = jnp.where(here, pltpu.roll(x, (STEP * slot + STEP) % LANES, 1), high)
        sides[0, group] = low.astype(BF16)
        sides[1, group] = high.astype(BF16)
    to_mate[...] = sides[1 - (place[0] // 4)]
    to_other[...] = sides[(place[0] // 4)]


def spread_columns(place, own, mate, other, side_mate, side_other, edges, sides, wide):
    chans = own.shape[1]
    lane = lax.broadcasted_iota(jnp.int32, (chans, LANES), 1)
    settle_edges(place, mate, other, edges)
    sides[1 - (place[0] // 4)] = side_mate[...]
    sides[(place[0] // 4)] = side_other[...]
    for group in range(sides.shape[1]):
        from_left = sides[0, group].astype(F32)
        from_right = sides[1, group].astype(F32)
        for slot in range(16):
            at = group * 16 + slot
            middle = row_of(own, edges, at)
            x = middle.astype(F32)
            before = jnp.where(
                lane < STEP,
                pltpu.roll(from_left, (LANES - STEP * slot) % LANES, 1),
                pltpu.roll(x, STEP, 1),
            )
            after = jnp.where(
                lane >= LANES - STEP,
                pltpu.roll(from_right, (2 * LANES - STEP - STEP * slot) % LANES, 1),
                pltpu.roll(x, LANES - STEP, 1),
            )
            wide[at, 0:chans] = before.astype(BF16)
            wide[at, chans : 2 * chans] = middle
            wide[at, 2 * chans : 3 * chans] = after.astype(BF16)


def windows(wide, i):
    return jnp.concatenate([wide[i], wide[i + STEP], wide[i + 2 * STEP]], axis=0)


def pair_windows(wide, i):
    return jnp.concatenate([windows(wide, i), windows(wide, i + 1)], axis=1)


def forward_kernel(
    place, act, mate, other, side_mate, side_other, feat, weight, labels, valid,
    wide, mixed, pay_near, pay_far, turned, edges, sides,
):
    rows, chans = act.shape[0], act.shape[1]
    part = rows
    length = pay_near.shape[0] // 2
    spread_columns(place, act, mate, other, side_mate, side_other, edges, sides, wide)
    kernel = weight[...].astype(F32).T.astype(BF16)

    def step(p, carry):
        i = 2 * p
        out = jnp.dot(kernel, pair_windows(wide, i), preferred_element_type=F32)
        for d in range(2):
            total = feat[i + d].astype(F32) + out[:, d * LANES : (d + 1) * LANES]
            low = total.astype(BF16)
            mixed[i + d] = low
            turned[pl.ds(pl.multiple_of((i + d) * LANES, LANES), LANES), :] = low.astype(F32).T
        return carry

    lax.fori_loop(0, rows // 2, step, 0, unroll=UNROLL)
    turned[rows * LANES :, :] = jnp.concatenate(
        [labels[...].astype(F32).T, valid[...].astype(F32).T], axis=1
    )
    half = part // 2

    def pack(j, carry):
        for s in range(4):
            base = j * LANES + (place[0] % 4 ^ s) * part
            low = turned[pl.ds(pl.multiple_of(base, 16), half), :]
            high = turned[pl.ds(pl.multiple_of(base + half, 16), half), :]
            pay = pay_near if s < 2 else pay_far
            pay[pl.ds(pl.multiple_of(s % 2 * length + j * half, 16), half), :] = jnp.concatenate(
                [low, high], axis=1
            ).astype(BF16)
        return carry

    lax.fori_loop(0, rows + 1, pack, 0, unroll=3)


def scale_of(count):
    return 0.5 / jnp.maximum(count[0:1, 0:1], 1.0)


def gradient_kernel(
    place, count, near, far, got1, got3, mixed, head, head_bias, labels, valid, wide,
    grad, low, mate, other, out0, out1, out2, out3,
    cells, lab, lab_t, val, val_t, padded_head, head_sum, bias_sum, loss_sum, total, sheet,
):
    rows, chans = mixed.shape[0], mixed.shape[1]
    bins, real = padded_head.shape[0], head.shape[0]
    half = rows // 2
    size = rows * half
    length = size + half
    for s, got in ((0, near), (2, far), (1, got1), (3, got3)):
        q = place[0] % 4 ^ s
        cells[pl.ds(pl.multiple_of(q * size, size), size), :] = got[:size, :].astype(F32)
        cells[pl.ds(pl.multiple_of(4 * size + q * half, half), half), :] = got[size:length, :].astype(F32)
    notes = [cells[4 * size + q * half : 4 * size + (q + 1) * half, :] for q in range(4)]
    for top in range(2):
        base = top * 2 * rows
        lab_t[top * half : (top + 1) * half, :] = jnp.concatenate(
            [n[:, base : base + rows] for n in notes], axis=1
        )
        val_t[top * half : (top + 1) * half, :] = jnp.concatenate(
            [n[:, base + rows : base + 2 * rows] for n in notes], axis=1
        )
    padded_head[...] = jnp.zeros_like(padded_head)
    padded_head[:real, :] = head[...].astype(F32)
    single = padded_head[...]
    blank = jnp.zeros_like(single)
    both = jnp.concatenate(
        [jnp.concatenate([single, blank], axis=1), jnp.concatenate([blank, single], axis=1)], axis=0
    ).astype(BF16)
    thrice = jnp.concatenate([single, single, single], axis=0).T.astype(BF16)
    single = single.astype(BF16)
    line = lax.broadcasted_iota(jnp.int32, (bins, real), 0)
    across = lax.broadcasted_iota(jnp.int32, (bins, real), 1)
    bias = jnp.sum(jnp.where(line == across, head_bias[...], 0.0), axis=1, keepdims=True)
    bias = jnp.where(lax.broadcasted_iota(jnp.int32, (bins, 1), 0) < real, bias, FAR_BELOW)
    lab[...] = labels[...].astype(F32)
    val[...] = valid[...].astype(F32)
    bin_ids = lax.broadcasted_iota(jnp.int32, (bins, LANES), 0).astype(F32)
    head_sum[...] = jnp.zeros_like(head_sum)
    bias_sum[...] = jnp.zeros_like(bias_sum)
    loss_sum[...] = jnp.zeros_like(loss_sum)
    total[...] = jnp.zeros_like(total)
    scale = scale_of(count)

    def step(i, carry):
        other = cells[pl.ds(i, LANES, stride=half), :].astype(BF16)
        logits_t = lax.dot_general(both, other, (((1,), (1,)), ((), ())), preferred_element_type=F32)
        pair = jnp.concatenate([mixed[i], mixed[i + half]], axis=1)
        logits = jnp.dot(single, pair, preferred_element_type=F32)
        pieces = []
        for d in range(2):
            at = pl.ds(i + d * half, 1)
            own = logits[:, d * LANES : (d + 1) * LANES] + bias
            far = logits_t[d * bins : (d + 1) * bins] + bias
            sym = 0.5 * (own + far)
            peak = jnp.max(sym, axis=0, keepdims=True)
            raised = jnp.exp(sym - peak)
            mass = jnp.sum(raised, axis=0, keepdims=True)
            lse = peak + jnp.log(mass)
            hot = bin_ids == lab[at, :]
            hot_t = bin_ids == lab_t[at, :]
            mask, mask_t = val[at, :], val_t[at, :]
            picked = jnp.sum(jnp.where(hot, sym, 0.0), axis=0, keepdims=True)
            loss_sum[...] += mask * (lse - picked)
            share = raised * ((mask + mask_t) / mass)
            pieces.append(share - jnp.where(hot, mask, 0.0) - jnp.where(hot_t, mask_t, 0.0))
        bias_sum[...] += pieces[0] + pieces[1]
        g = jnp.concatenate(pieces, axis=1)
        first = g.astype(BF16).astype(F32)
        rest = g - first
        second = rest.astype(BF16).astype(F32)
        split = jnp.concatenate([first, second, rest - second], axis=0).astype(BF16)
        out = jnp.dot(thrice, split, preferred_element_type=F32)
        grad[i] = out[:, :LANES]
        grad[i + half] = out[:, LANES:]
        rounded = (out * scale).astype(BF16)
        low[i] = rounded[:, :LANES]
        low[i + half] = rounded[:, LANES:]
        total[...] += lax.dot_general(
            jnp.concatenate([windows(wide, i), windows(wide, i + half)], axis=1),
            rounded,
            (((1,), (1,)), ((), ())),
            preferred_element_type=F32,
        )
        head_sum[...] += lax.dot_general(
            split, pair, (((1,), (1,)), ((), ())), preferred_element_type=F32
        )
        return carry

    lax.fori_loop(0, half, step, 0, unroll=UNROLL)
    share_edges(place, low, mate, other)
    upper = total.shape[0] // 2
    sheet[...] = jnp.zeros_like(sheet)
    sheet[:upper, :] = jnp.concatenate([total[:upper], total[upper:]], axis=1)
    h = (head_sum[:bins] + head_sum[bins : 2 * bins] + head_sum[2 * bins :]) * scale
    sheet[upper : upper + bins, :chans] = h
    note = upper + bins
    sheet[note : note + 1, :bins] = jnp.sum(bias_sum[...].T, axis=0, keepdims=True) * scale
    sheet[note + 1 : note + 2, :1] = jnp.sum(loss_sum[...], axis=1, keepdims=True)
    quarter = sheet.shape[0] // 4
    for s, out in enumerate((out0, out1, out2, out3)):
        out[...] = sheet[pl.ds(pl.multiple_of((place[0] % 4 ^ s) * quarter, 8), quarter), :]


def backward_kernel(
    place, count, low, mate, other, side_mate, side_other, grad, feat, weight, out, wide, edges, sides
):
    rows, chans = grad.shape[0], grad.shape[1]
    scale = scale_of(count)
    spread_columns(place, low, mate, other, side_mate, side_other, edges, sides, wide)
    taps = weight.shape[0] // chans
    kernel = jnp.concatenate(
        [weight[(taps - 1 - t) * chans : (taps - t) * chans, :].astype(F32) for t in range(taps)],
        axis=1,
    ).astype(BF16)

    def step(p, carry):
        i = 2 * p
        back = jnp.dot(kernel, pair_windows(wide, i), preferred_element_type=F32)
        for d in range(2):
            v = feat[i + d].astype(F32)
            slope = jnp.where(v > 0, 1.0, jnp.exp(jnp.minimum(v, 0.0)))
            out[i + d] = (
                grad[i + d] * scale + slope * back[:, d * LANES : (d + 1) * LANES]
            ).astype(BF16)
        return carry

    lax.fori_loop(0, rows // 2, step, 0, unroll=UNROLL)


def finish_kernel(
    place, count, got0, got1, got2, got3, kernel_grad, head_grad, bias_grad, loss, sheet
):
    quarter = got0.shape[0]
    for s, got in enumerate((got0, got1, got2, got3)):
        sheet[pl.ds(pl.multiple_of((place[0] % 4 ^ s) * quarter, 8), quarter), :] = got[...]
    half, chans = kernel_grad.shape[0] // 2, kernel_grad.shape[1]
    bins = head_grad.shape[0]
    kernel_grad[:half, :] = sheet[:half, :chans]
    kernel_grad[half:, :] = sheet[:half, chans:]
    head_grad[...] = sheet[half : half + bins, :chans]
    note = half + -(-bins // 8) * 8
    bias_grad[...] = sheet[note : note + 1, :bins]
    loss[...] = sheet[note + 1 : note + 2, :1] / jnp.maximum(count[0:1, 0:1], 1.0)


def border_buffers(rows, chans):
    groups = (rows + 2 * STEP) // 16
    return [
        pltpu.VMEM((2 * STEP, chans, LANES), BF16),
        pltpu.VMEM((2, groups, chans, LANES), BF16),
    ]


def borders(place, own, mate, other):
    rows, chans, _ = own.shape
    edges = swapped(mate, other, "row")
    groups = (rows + 2 * STEP) // 16
    sides = run(
        pack_kernel,
        [shape((groups, chans, LANES), BF16)] * 2,
        (place, own, *edges),
        scratch=border_buffers(rows, chans),
        scalars=1,
        micros=8,
    )
    return *edges, *swapped(*sides, "col")


def partners(stage):
    if stage < 2:
        return lambda m: lambda r, c: (r ^ (m << (2 * stage)), c)
    if stage == 2:
        return lambda m: lambda r, c: (r ^ ((m & 1) << 4), c ^ (m >> 1))
    return lambda m: lambda r, c: (r, c ^ (m << 1))


def total_small(value, stages):
    for stage in stages:
        to = partners(stage)
        value = (value + send(value, to(1))) + (send(value, to(2)) + send(value, to(3)))
    return value


def mirrored(pay_near, pay_far, parts):
    length = pay_near.shape[0] // 2
    pay_near = send(pay_near, lambda r, c: (r, c ^ 2))
    near = send(pay_near, lambda r, c: (parts * (c ^ 2) + r % parts, r // parts))
    far = send(pay_far, lambda r, c: (parts * c + (r % parts ^ 2), r // parts))
    mate = lambda r, c: (r ^ 1, c)
    return pay_near, (near, far, send(near[length:], mate), send(far[length:], mate))


def total_quarters(quarters):
    near = partners(0)
    a, b, c, d = quarters
    part = (a + send(b, near(1))) + (send(c, near(2)) + send(d, near(3)))
    for stage in (1, 2, 3):
        to = partners(stage)
        part = (part + send(part, to(1))) + (send(part, to(2)) + send(part, to(3)))
    return [part] + [send(part, near(m)) for m in (1, 2, 3)]


def per_device(features, conv_weight, head_weight, head_bias, labels, valid):
    rows, cols, chans = features.shape
    bins = head_weight.shape[1]
    parts = cols // rows
    place = lax.axis_index("row") % parts + 4 * (lax.axis_index("col") % 2)
    place = place.astype(jnp.int32).reshape(1)
    feat = features.transpose(0, 2, 1)
    weight = conv_weight.reshape(-1, chans)
    tall = -(-bins // 8) * 8
    tile = (rows, chans, LANES)
    edge = (STEP, chans, LANES)
    act, mate, other, counted, feat, valid = run(
        activate_kernel,
        [shape(tile, BF16), shape(edge, BF16), shape(edge, BF16), shape((8, LANES), F32)]
        + [shape(tile, BF16), shape(valid.shape, jnp.int32)],
        (place, feat, valid),
        scalars=1,
        micros=1,
    )
    around = borders(place, act, mate, other)
    counted = total_small(counted, (1, 2))
    counted, act = lax.optimization_barrier((counted, act))
    length = (rows + 1) * rows // 2
    wide, mixed, pay_near, pay_far = run(
        forward_kernel,
        [shape((rows + 2 * STEP, 3 * chans, LANES), BF16), shape(tile, BF16)]
        + [shape((2 * length, LANES), BF16)] * 2,
        (place, act, *around, feat, weight, labels, valid),
        scratch=[pltpu.VMEM(((rows + 1) * LANES, chans), F32)] + border_buffers(rows, chans),
        scalars=1,
        micros=5,
    )
    passed, got = mirrored(pay_near, pay_far, parts)
    _, counted = lax.optimization_barrier((passed, counted))
    count = total_small(counted, (3, 0))
    half = 9 * chans // 2
    lines = -(-(half + tall + 8) // 32) * 32
    grad, low, mate, other, *quarters = run(
        gradient_kernel,
        [shape(tile, F32), shape(tile, BF16), shape(edge, BF16), shape(edge, BF16)]
        + [shape((lines // 4, LANES), F32)] * 4,
        (place, count, *got, mixed, head_weight.T, head_bias.reshape(1, bins), labels, valid, wide),
        scratch=[pltpu.VMEM((length * 4, LANES), F32)]
        + [pltpu.VMEM((rows, LANES), F32)] * 4
        + [
            pltpu.VMEM((tall, chans), F32),
            pltpu.VMEM((3 * tall, chans), F32),
            pltpu.VMEM((tall, LANES), F32),
            pltpu.VMEM((1, LANES), F32),
            pltpu.VMEM((9 * chans, chans), F32),
            pltpu.VMEM((lines, LANES), F32),
        ],
        scalars=1,
        micros=6,
    )
    sums = total_quarters(quarters)
    around = borders(place, low, mate, other)
    (grad_features,) = run(
        backward_kernel,
        [shape(tile, BF16)],
        (place, count, low, *around, grad, feat, weight),
        scratch=[pltpu.VMEM((rows + 2 * STEP, 3 * chans, LANES), BF16)]
        + border_buffers(rows, chans),
        scalars=1,
        micros=4,
    )
    kernel_grad, head_grad, bias_grad, loss = run(
        finish_kernel,
        [
            shape((9 * chans, chans), F32),
            shape((bins, chans), F32),
            shape((1, bins), F32),
            shape((1, 1), F32),
        ],
        (place, count, *sums),
        scratch=[pltpu.VMEM((lines, LANES), F32)],
        scalars=1,
        micros=1,
    )
    return (
        loss.reshape(()),
        grad_features.transpose(0, 2, 1),
        kernel_grad.reshape(conv_weight.shape),
        head_grad.T,
        bias_grad.reshape(bins),
    )


def solution(mesh):
    placed = (P("row", "col", None), P(), P(), P(), P("row", "col"), P("row", "col"))
    return jax.shard_map(
        per_device,
        mesh=mesh,
        in_specs=placed,
        out_specs=(P(), P("row", "col", None), P(), P(), P()),
        check_vma=False,
    )
```

```python
import jax
import jax.numpy as jnp
from jax import lax
from jax.experimental import pallas as pl
from jax.experimental.pallas import tpu as pltpu
from jax.sharding import PartitionSpec as P

STEP = 8
GRID = ("row", "col")
F32, BF16 = jnp.float32, jnp.bfloat16
LANES = 128
UNROLL = 16
FAR_BELOW = -1e30
VMEM = pl.BlockSpec(memory_space=pltpu.VMEM)
SMEM = pl.BlockSpec(memory_space=pltpu.SMEM)


def run(body, outs, args, scratch=(), scalars=0, micros=3):
    return pl.pallas_call(
        body,
        out_shape=outs,
        in_specs=[SMEM] * scalars + [VMEM] * (len(args) - scalars),
        out_specs=[VMEM] * len(outs),
        scratch_shapes=list(scratch),
        compiler_params=pltpu.CompilerParams(vmem_limit_bytes=48 * 1024 * 1024),
        cost_estimate=pl.CostEstimate(
            flops=0, bytes_accessed=int(micros * 3.6e6), transcendentals=0
        ),
    )(*args)


def shape(dims, kind):
    return jax.ShapeDtypeStruct(dims, kind)


def send(block, target):
    nrow, ncol = lax.axis_size("row"), lax.axis_size("col")
    pairs = []
    for r in range(nrow):
        for c in range(ncol):
            r2, c2 = target(r, c)
            pairs.append((r * ncol + c, r2 * ncol + c2))
    return lax.ppermute(block, GRID, pairs)


def swapped(to_mate, to_other, axis):
    count = lax.axis_size(axis)
    mates = [(i, i ^ 1) for i in range(count)]
    others = [(i, i + 1 if i % 2 else i - 1) for i in range(1, count - 1)]
    return lax.ppermute(to_mate, axis, mates), lax.ppermute(to_other, axis, others)


def activate_kernel(place, feat, valid, act, mate, other, counted, kept_feat, kept_valid):
    rows = feat.shape[0]

    def step(i, carry):
        kept_feat[i] = feat[i]
        v = feat[i].astype(F32)
        near = v * (1.0 + v * (0.5 + v * (1.0 / 6.0 + v * (1.0 / 24.0))))
        low = jnp.where(v > -0.03, near, jnp.exp(jnp.minimum(v, 0.0)) - 1.0)
        act[i] = jnp.where(v > 0, v, low).astype(BF16)
        return carry

    lax.fori_loop(0, rows, step, 0, unroll=4)
    share_edges(place, act, mate, other)
    lines = jnp.sum(valid[...].astype(F32), axis=0, keepdims=True)
    kept_valid[...] = valid[...]
    counted[...] = jnp.broadcast_to(jnp.sum(lines, axis=1, keepdims=True), counted.shape)


def share_edges(place, own, mate, other):
    last = own.shape[0] - STEP
    low = (1 - place[0] % 2) * last
    mate[...] = own[pl.ds(low, STEP)]
    other[...] = own[pl.ds(last - low, STEP)]


def settle_edges(place, mate, other, edges):
    odd = place[0] % 2
    edges[pl.ds((1 - odd) * STEP, STEP)] = mate[...]
    edges[pl.ds(odd * STEP, STEP)] = other[...]


def row_of(own, edges, at):
    rows = own.shape[0]
    if at < STEP:
        return edges[at]
    if at < STEP + rows:
        return own[at - STEP]
    return edges[at - rows]


def pack_kernel(place, own, mate, other, to_mate, to_other, edges, sides):
    chans = own.shape[1]
    lane = lax.broadcasted_iota(jnp.int32, (chans, LANES), 1) // STEP
    settle_edges(place, mate, other, edges)
    for group in range(sides.shape[1]):
        low = jnp.zeros((chans, LANES), F32)
        high = jnp.zeros((chans, LANES), F32)
        for slot in range(16):
            x = row_of(own, edges, group * 16 + slot).astype(F32)
            here = lane == slot
            low = jnp.where(here, pltpu.roll(x, (STEP * slot) % LANES, 1), low)
            high = jnp.where(here, pltpu.roll(x, (STEP * slot + STEP) % LANES, 1), high)
        sides[0, group] = low.astype(BF16)
        sides[1, group] = high.astype(BF16)
    to_mate[...] = sides[1 - (place[0] // 4)]
    to_other[...] = sides[(place[0] // 4)]


def spread_columns(place, own, mate, other, side_mate, side_other, edges, sides, wide):
    chans = own.shape[1]
    lane = lax.broadcasted_iota(jnp.int32, (chans, LANES), 1)
    settle_edges(place, mate, other, edges)
    sides[1 - (place[0] // 4)] = side_mate[...]
    sides[(place[0] // 4)] = side_other[...]
    for group in range(sides.shape[1]):
        from_left = sides[0, group].astype(F32)
        from_right = sides[1, group].astype(F32)
        for slot in range(16):
            at = group * 16 + slot
            middle = row_of(own, edges, at)
            x = middle.astype(F32)
            before = jnp.where(
                lane < STEP,
                pltpu.roll(from_left, (LANES - STEP * slot) % LANES, 1),
                pltpu.roll(x, STEP, 1),
            )
            after = jnp.where(
                lane >= LANES - STEP,
                pltpu.roll(from_right, (2 * LANES - STEP - STEP * slot) % LANES, 1),
                pltpu.roll(x, LANES - STEP, 1),
            )
            wide[at, 0:chans] = before.astype(BF16)
            wide[at, chans : 2 * chans] = middle
            wide[at, 2 * chans : 3 * chans] = after.astype(BF16)


def windows(wide, i):
    return jnp.concatenate([wide[i], wide[i + STEP], wide[i + 2 * STEP]], axis=0)


def pair_windows(wide, i):
    return jnp.concatenate([windows(wide, i), windows(wide, i + 1)], axis=1)


def forward_kernel(
    place, act, mate, other, side_mate, side_other, feat, weight, labels, valid,
    wide, mixed, pay_near, pay_far, turned, edges, sides,
):
    rows, chans = act.shape[0], act.shape[1]
    part = rows
    length = pay_near.shape[0] // 2
    spread_columns(place, act, mate, other, side_mate, side_other, edges, sides, wide)
    kernel = weight[...].astype(F32).T.astype(BF16)

    def step(p, carry):
        i = 2 * p
        out = jnp.dot(kernel, pair_windows(wide, i), preferred_element_type=F32)
        for d in range(2):
            total = feat[i + d].astype(F32) + out[:, d * LANES : (d + 1) * LANES]
            low = total.astype(BF16)
            mixed[i + d] = low
            turned[pl.ds(pl.multiple_of((i + d) * LANES, LANES), LANES), :] = low.astype(F32).T
        return carry

    lax.fori_loop(0, rows // 2, step, 0, unroll=UNROLL)
    turned[rows * LANES :, :] = jnp.concatenate(
        [labels[...].astype(F32).T, valid[...].astype(F32).T], axis=1
    )
    half = part // 2

    def pack(j, carry):
        for s in range(4):
            base = j * LANES + (place[0] % 4 ^ s) * part
            low = turned[pl.ds(pl.multiple_of(base, 16), half), :]
            high = turned[pl.ds(pl.multiple_of(base + half, 16), half), :]
            pay = pay_near if s < 2 else pay_far
            pay[pl.ds(pl.multiple_of(s % 2 * length + j * half, 16), half), :] = jnp.concatenate(
                [low, high], axis=1
            ).astype(BF16)
        return carry

    lax.fori_loop(0, rows + 1, pack, 0, unroll=3)


def scale_of(count):
    return 0.5 / jnp.maximum(count[0:1, 0:1], 1.0)


def gradient_kernel(
    place, count, near, far, got1, got3, mixed, head, head_bias, labels, valid, wide,
    grad, low, mate, other, out0, out1, out2, out3,
    cells, lab, lab_t, val, val_t, padded_head, head_sum, bias_sum, loss_sum, total, sheet,
):
    rows, chans = mixed.shape[0], mixed.shape[1]
    bins, real = padded_head.shape[0], head.shape[0]
    half = rows // 2
    size = rows * half
    length = size + half
    for s, got in ((0, near), (2, far), (1, got1), (3, got3)):
        q = place[0] % 4 ^ s
        cells[pl.ds(pl.multiple_of(q * size, size), size), :] = got[:size, :].astype(F32)
        cells[pl.ds(pl.multiple_of(4 * size + q * half, half), half), :] = got[size:length, :].astype(F32)
    notes = [cells[4 * size + q * half : 4 * size + (q + 1) * half, :] for q in range(4)]
    for top in range(2):
        base = top * 2 * rows
        lab_t[top * half : (top + 1) * half, :] = jnp.concatenate(
            [n[:, base : base + rows] for n in notes], axis=1
        )
        val_t[top * half : (top + 1) * half, :] = jnp.concatenate(
            [n[:, base + rows : base + 2 * rows] for n in notes], axis=1
        )
    padded_head[...] = jnp.zeros_like(padded_head)
    padded_head[:real, :] = head[...].astype(F32)
    single = padded_head[...]
    blank = jnp.zeros_like(single)
    both = jnp.concatenate(
        [jnp.concatenate([single, blank], axis=1), jnp.concatenate([blank, single], axis=1)], axis=0
    ).astype(BF16)
    thrice = jnp.concatenate([single, single, single], axis=0).T.astype(BF16)
    single = single.astype(BF16)
    line = lax.broadcasted_iota(jnp.int32, (bins, real), 0)
    across = lax.broadcasted_iota(jnp.int32, (bins, real), 1)
    bias = jnp.sum(jnp.where(line == across, head_bias[...], 0.0), axis=1, keepdims=True)
    bias = jnp.where(lax.broadcasted_iota(jnp.int32, (bins, 1), 0) < real, bias, FAR_BELOW)
    lab[...] = labels[...].astype(F32)
    val[...] = valid[...].astype(F32)
    bin_ids = lax.broadcasted_iota(jnp.int32, (bins, LANES), 0).astype(F32)
    head_sum[...] = jnp.zeros_like(head_sum)
    bias_sum[...] = jnp.zeros_like(bias_sum)
    loss_sum[...] = jnp.zeros_like(loss_sum)
    total[...] = jnp.zeros_like(total)
    scale = scale_of(count)

    def step(i, carry):
        other = cells[pl.ds(i, LANES, stride=half), :].astype(BF16)
        logits_t = lax.dot_general(both, other, (((1,), (1,)), ((), ())), preferred_element_type=F32)
        pair = jnp.concatenate([mixed[i], mixed[i + half]], axis=1)
        logits = jnp.dot(single, pair, preferred_element_type=F32)
        pieces = []
        for d in range(2):
            at = pl.ds(i + d * half, 1)
            own = logits[:, d * LANES : (d + 1) * LANES] + bias
            far = logits_t[d * bins : (d + 1) * bins] + bias
            sym = 0.5 * (own + far)
            peak = jnp.max(sym, axis=0, keepdims=True)
            raised = jnp.exp(sym - peak)
            mass = jnp.sum(raised, axis=0, keepdims=True)
            lse = peak + jnp.log(mass)
            hot = bin_ids == lab[at, :]
            hot_t = bin_ids == lab_t[at, :]
            mask, mask_t = val[at, :], val_t[at, :]
            picked = jnp.sum(jnp.where(hot, sym, 0.0), axis=0, keepdims=True)
            loss_sum[...] += mask * (lse - picked)
            share = raised * ((mask + mask_t) / mass)
            pieces.append(share - jnp.where(hot, mask, 0.0) - jnp.where(hot_t, mask_t, 0.0))
        bias_sum[...] += pieces[0] + pieces[1]
        g = jnp.concatenate(pieces, axis=1)
        first = g.astype(BF16).astype(F32)
        rest = g - first
        second = rest.astype(BF16).astype(F32)
        split = jnp.concatenate([first, second, rest - second], axis=0).astype(BF16)
        out = jnp.dot(thrice, split, preferred_element_type=F32)
        grad[i] = out[:, :LANES]
        grad[i + half] = out[:, LANES:]
        rounded = (out * scale).astype(BF16)
        low[i] = rounded[:, :LANES]
        low[i + half] = rounded[:, LANES:]
        total[...] += lax.dot_general(
            jnp.concatenate([windows(wide, i), windows(wide, i + half)], axis=1),
            rounded,
            (((1,), (1,)), ((), ())),
            preferred_element_type=F32,
        )
        head_sum[...] += lax.dot_general(
            split, pair, (((1,), (1,)), ((), ())), preferred_element_type=F32
        )
        return carry

    lax.fori_loop(0, half, step, 0, unroll=UNROLL)
    share_edges(place, low, mate, other)
    upper = total.shape[0] // 2
    sheet[...] = jnp.zeros_like(sheet)
    sheet[:upper, :] = jnp.concatenate([total[:upper], total[upper:]], axis=1)
    h = (head_sum[:bins] + head_sum[bins : 2 * bins] + head_sum[2 * bins :]) * scale
    sheet[upper : upper + bins, :chans] = h
    note = upper + bins
    sheet[note : note + 1, :bins] = jnp.sum(bias_sum[...].T, axis=0, keepdims=True) * scale
    sheet[note + 1 : note + 2, :1] = jnp.sum(loss_sum[...], axis=1, keepdims=True)
    quarter = sheet.shape[0] // 4
    for s, out in enumerate((out0, out1, out2, out3)):
        out[...] = sheet[pl.ds(pl.multiple_of((place[0] % 4 ^ s) * quarter, 8), quarter), :]


def backward_kernel(
    place, count, low, mate, other, side_mate, side_other, grad, feat, weight, out, wide, edges, sides
):
    rows, chans = grad.shape[0], grad.shape[1]
    scale = scale_of(count)
    spread_columns(place, low, mate, other, side_mate, side_other, edges, sides, wide)
    taps = weight.shape[0] // chans
    kernel = jnp.concatenate(
        [weight[(taps - 1 - t) * chans : (taps - t) * chans, :].astype(F32) for t in range(taps)],
        axis=1,
    ).astype(BF16)

    def step(p, carry):
        i = 2 * p
        back = jnp.dot(kernel, pair_windows(wide, i), preferred_element_type=F32)
        for d in range(2):
            v = feat[i + d].astype(F32)
            slope = jnp.where(v > 0, 1.0, jnp.exp(jnp.minimum(v, 0.0)))
            out[i + d] = (
                grad[i + d] * scale + slope * back[:, d * LANES : (d + 1) * LANES]
            ).astype(BF16)
        return carry

    lax.fori_loop(0, rows // 2, step, 0, unroll=UNROLL)


def finish_kernel(
    place, count, got0, got1, got2, got3, kernel_grad, head_grad, bias_grad, loss, sheet
):
    quarter = got0.shape[0]
    for s, got in enumerate((got0, got1, got2, got3)):
        sheet[pl.ds(pl.multiple_of((place[0] % 4 ^ s) * quarter, 8), quarter), :] = got[...]
    half, chans = kernel_grad.shape[0] // 2, kernel_grad.shape[1]
    bins = head_grad.shape[0]
    kernel_grad[:half, :] = sheet[:half, :chans]
    kernel_grad[half:, :] = sheet[:half, chans:]
    head_grad[...] = sheet[half : half + bins, :chans]
    note = half + -(-bins // 8) * 8
    bias_grad[...] = sheet[note : note + 1, :bins]
    loss[...] = sheet[note + 1 : note + 2, :1] / jnp.maximum(count[0:1, 0:1], 1.0)


def border_buffers(rows, chans):
    groups = (rows + 2 * STEP) // 16
    return [
        pltpu.VMEM((2 * STEP, chans, LANES), BF16),
        pltpu.VMEM((2, groups, chans, LANES), BF16),
    ]


def borders(place, own, mate, other):
    rows, chans, _ = own.shape
    edges = swapped(mate, other, "row")
    groups = (rows + 2 * STEP) // 16
    sides = run(
        pack_kernel,
        [shape((groups, chans, LANES), BF16)] * 2,
        (place, own, *edges),
        scratch=border_buffers(rows, chans),
        scalars=1,
        micros=8,
    )
    return *edges, *swapped(*sides, "col")


def partners(stage):
    if stage < 2:
        return lambda m: lambda r, c: (r ^ (m << (2 * stage)), c)
    if stage == 2:
        return lambda m: lambda r, c: (r ^ ((m & 1) << 4), c ^ (m >> 1))
    return lambda m: lambda r, c: (r, c ^ (m << 1))


def total_small(value, stages):
    for stage in stages:
        to = partners(stage)
        value = (value + send(value, to(1))) + (send(value, to(2)) + send(value, to(3)))
    return value


def mirrored(pay_near, pay_far, parts):
    length = pay_near.shape[0] // 2
    pay_near = send(pay_near, lambda r, c: (r, c ^ 2))
    near = send(pay_near, lambda r, c: (parts * (c ^ 2) + r % parts, r // parts))
    far = send(pay_far, lambda r, c: (parts * c + (r % parts ^ 2), r // parts))
    mate = lambda r, c: (r ^ 1, c)
    return pay_near, (near, far, send(near[length:], mate), send(far[length:], mate))


def total_quarters(quarters):
    near = partners(0)
    a, b, c, d = quarters
    part = (a + send(b, near(1))) + (send(c, near(2)) + send(d, near(3)))
    for stage in (1, 2, 3):
        to = partners(stage)
        part = (part + send(part, to(1))) + (send(part, to(2)) + send(part, to(3)))
    return [part] + [send(part, near(m)) for m in (1, 2, 3)]


def per_device(features, conv_weight, head_weight, head_bias, labels, valid):
    rows, cols, chans = features.shape
    bins = head_weight.shape[1]
    parts = cols // rows
    place = lax.axis_index("row") % parts + 4 * (lax.axis_index("col") % 2)
    place = place.astype(jnp.int32).reshape(1)
    feat = features.transpose(0, 2, 1)
    weight = conv_weight.reshape(-1, chans)
    tall = -(-bins // 8) * 8
    tile = (rows, chans, LANES)
    edge = (STEP, chans, LANES)
    act, mate, other, counted, feat, valid = run(
        activate_kernel,
        [shape(tile, BF16), shape(edge, BF16), shape(edge, BF16), shape((8, LANES), F32)]
        + [shape(tile, BF16), shape(valid.shape, jnp.int32)],
        (place, feat, valid),
        scalars=1,
        micros=1,
    )
    around = borders(place, act, mate, other)
    counted = total_small(counted, (0, 1, 2))
    counted, act = lax.optimization_barrier((counted, act))
    length = (rows + 1) * rows // 2
    wide, mixed, pay_near, pay_far = run(
        forward_kernel,
        [shape((rows + 2 * STEP, 3 * chans, LANES), BF16), shape(tile, BF16)]
        + [shape((2 * length, LANES), BF16)] * 2,
        (place, act, *around, feat, weight, labels, valid),
        scratch=[pltpu.VMEM(((rows + 1) * LANES, chans), F32)] + border_buffers(rows, chans),
        scalars=1,
        micros=5,
    )
    passed, got = mirrored(pay_near, pay_far, parts)
    _, counted = lax.optimization_barrier((passed, counted))
    count = total_small(counted, (3,))
    half = 9 * chans // 2
    lines = -(-(half + tall + 8) // 32) * 32
    grad, low, mate, other, *quarters = run(
        gradient_kernel,
        [shape(tile, F32), shape(tile, BF16), shape(edge, BF16), shape(edge, BF16)]
        + [shape((lines // 4, LANES), F32)] * 4,
        (place, count, *got, mixed, head_weight.T, head_bias.reshape(1, bins), labels, valid, wide),
        scratch=[pltpu.VMEM((length * 4, LANES), F32)]
        + [pltpu.VMEM((rows, LANES), F32)] * 4
        + [
            pltpu.VMEM((tall, chans), F32),
            pltpu.VMEM((3 * tall, chans), F32),
            pltpu.VMEM((tall, LANES), F32),
            pltpu.VMEM((1, LANES), F32),
            pltpu.VMEM((9 * chans, chans), F32),
            pltpu.VMEM((lines, LANES), F32),
        ],
        scalars=1,
        micros=6,
    )
    sums = total_quarters(quarters)
    around = borders(place, low, mate, other)
    (grad_features,) = run(
        backward_kernel,
        [shape(tile, BF16)],
        (place, count, low, *around, grad, feat, weight),
        scratch=[pltpu.VMEM((rows + 2 * STEP, 3 * chans, LANES), BF16)]
        + border_buffers(rows, chans),
        scalars=1,
        micros=4,
    )
    kernel_grad, head_grad, bias_grad, loss = run(
        finish_kernel,
        [
            shape((9 * chans, chans), F32),
            shape((bins, chans), F32),
            shape((1, bins), F32),
            shape((1, 1), F32),
        ],
        (place, count, *sums),
        scratch=[pltpu.VMEM((lines, LANES), F32)],
        scalars=1,
        micros=1,
    )
    return (
        loss.reshape(()),
        grad_features.transpose(0, 2, 1),
        kernel_grad.reshape(conv_weight.shape),
        head_grad.T,
        bias_grad.reshape(bins),
    )


def solution(mesh):
    placed = (P("row", "col", None), P(), P(), P(), P("row", "col"), P("row", "col"))
    return jax.shard_map(
        per_device,
        mesh=mesh,
        in_specs=placed,
        out_specs=(P(), P("row", "col", None), P(), P(), P()),
        check_vma=False,
    )
```

```python
import jax
import jax.numpy as jnp
from jax import lax
from jax.experimental import pallas as pl
from jax.experimental.pallas import tpu as pltpu
from jax.sharding import PartitionSpec as P

STEP = 8
GRID = ("row", "col")
F32, BF16 = jnp.float32, jnp.bfloat16
LANES = 128
UNROLL = 16
FAR_BELOW = -1e30
VMEM = pl.BlockSpec(memory_space=pltpu.VMEM)
SMEM = pl.BlockSpec(memory_space=pltpu.SMEM)


def run(body, outs, args, scratch=(), scalars=0, micros=3):
    return pl.pallas_call(
        body,
        out_shape=outs,
        in_specs=[SMEM] * scalars + [VMEM] * (len(args) - scalars),
        out_specs=[VMEM] * len(outs),
        scratch_shapes=list(scratch),
        compiler_params=pltpu.CompilerParams(vmem_limit_bytes=48 * 1024 * 1024),
        cost_estimate=pl.CostEstimate(
            flops=0, bytes_accessed=int(micros * 3.6e6), transcendentals=0
        ),
    )(*args)


def shape(dims, kind):
    return jax.ShapeDtypeStruct(dims, kind)


def send(block, target):
    nrow, ncol = lax.axis_size("row"), lax.axis_size("col")
    pairs = []
    for r in range(nrow):
        for c in range(ncol):
            r2, c2 = target(r, c)
            pairs.append((r * ncol + c, r2 * ncol + c2))
    return lax.ppermute(block, GRID, pairs)


def swapped(to_mate, to_other, axis):
    count = lax.axis_size(axis)
    mates = [(i, i ^ 1) for i in range(count)]
    others = [(i, i + 1 if i % 2 else i - 1) for i in range(1, count - 1)]
    return lax.ppermute(to_mate, axis, mates), lax.ppermute(to_other, axis, others)


def activate_kernel(place, feat, valid, act, mate, other, counted, kept_feat, kept_valid):
    rows = feat.shape[0]

    def step(i, carry):
        kept_feat[i] = feat[i]
        v = feat[i].astype(F32)
        near = v * (1.0 + v * (0.5 + v * (1.0 / 6.0 + v * (1.0 / 24.0))))
        low = jnp.where(v > -0.03, near, jnp.exp(jnp.minimum(v, 0.0)) - 1.0)
        act[i] = jnp.where(v > 0, v, low).astype(BF16)
        return carry

    lax.fori_loop(0, rows, step, 0, unroll=4)
    share_edges(place, act, mate, other)
    lines = jnp.sum(valid[...].astype(F32), axis=0, keepdims=True)
    kept_valid[...] = valid[...]
    counted[...] = jnp.broadcast_to(jnp.sum(lines, axis=1, keepdims=True), counted.shape)


def share_edges(place, own, mate, other):
    last = own.shape[0] - STEP
    low = (1 - place[0] % 2) * last
    mate[...] = own[pl.ds(low, STEP)]
    other[...] = own[pl.ds(last - low, STEP)]


def settle_edges(place, mate, other, edges):
    odd = place[0] % 2
    edges[pl.ds((1 - odd) * STEP, STEP)] = mate[...]
    edges[pl.ds(odd * STEP, STEP)] = other[...]


def row_of(own, edges, at):
    rows = own.shape[0]
    if at < STEP:
        return edges[at]
    if at < STEP + rows:
        return own[at - STEP]
    return edges[at - rows]


def pack_kernel(place, own, mate, other, to_mate, to_other, edges, sides):
    chans = own.shape[1]
    lane = lax.broadcasted_iota(jnp.int32, (chans, LANES), 1) // STEP
    settle_edges(place, mate, other, edges)
    for group in range(sides.shape[1]):
        low = jnp.zeros((chans, LANES), F32)
        high = jnp.zeros((chans, LANES), F32)
        for slot in range(16):
            x = row_of(own, edges, group * 16 + slot).astype(F32)
            here = lane == slot
            low = jnp.where(here, pltpu.roll(x, (STEP * slot) % LANES, 1), low)
            high = jnp.where(here, pltpu.roll(x, (STEP * slot + STEP) % LANES, 1), high)
        sides[0, group] = low.astype(BF16)
        sides[1, group] = high.astype(BF16)
    to_mate[...] = sides[1 - (place[0] // 4)]
    to_other[...] = sides[(place[0] // 4)]


def spread_columns(place, own, mate, other, side_mate, side_other, edges, sides, wide):
    chans = own.shape[1]
    lane = lax.broadcasted_iota(jnp.int32, (chans, LANES), 1)
    settle_edges(place, mate, other, edges)
    sides[1 - (place[0] // 4)] = side_mate[...]
    sides[(place[0] // 4)] = side_other[...]
    for group in range(sides.shape[1]):
        from_left = sides[0, group].astype(F32)
        from_right = sides[1, group].astype(F32)
        for slot in range(16):
            at = group * 16 + slot
            middle = row_of(own, edges, at)
            x = middle.astype(F32)
            before = jnp.where(
                lane < STEP,
                pltpu.roll(from_left, (LANES - STEP * slot) % LANES, 1),
                pltpu.roll(x, STEP, 1),
            )
            after = jnp.where(
                lane >= LANES - STEP,
                pltpu.roll(from_right, (2 * LANES - STEP - STEP * slot) % LANES, 1),
                pltpu.roll(x, LANES - STEP, 1),
            )
            wide[at, 0:chans] = before.astype(BF16)
            wide[at, chans : 2 * chans] = middle
            wide[at, 2 * chans : 3 * chans] = after.astype(BF16)


def windows(wide, i):
    return jnp.concatenate([wide[i], wide[i + STEP], wide[i + 2 * STEP]], axis=0)


def pair_windows(wide, i):
    return jnp.concatenate([windows(wide, i), windows(wide, i + 1)], axis=1)


def forward_kernel(
    place, act, mate, other, side_mate, side_other, feat, weight, labels, valid,
    wide, mixed, pay_near, pay_far, turned, edges, sides,
):
    rows, chans = act.shape[0], act.shape[1]
    part = rows
    length = pay_near.shape[0] // 2
    spread_columns(place, act, mate, other, side_mate, side_other, edges, sides, wide)
    kernel = weight[...].astype(F32).T.astype(BF16)

    def step(p, carry):
        i = 2 * p
        out = jnp.dot(kernel, pair_windows(wide, i), preferred_element_type=F32)
        for d in range(2):
            total = feat[i + d].astype(F32) + out[:, d * LANES : (d + 1) * LANES]
            low = total.astype(BF16)
            mixed[i + d] = low
            turned[pl.ds(pl.multiple_of((i + d) * LANES, LANES), LANES), :] = low.astype(F32).T
        return carry

    lax.fori_loop(0, rows // 2, step, 0, unroll=UNROLL)
    turned[rows * LANES :, :] = jnp.concatenate(
        [labels[...].astype(F32).T, valid[...].astype(F32).T], axis=1
    )
    half = part // 2

    def pack(j, carry):
        for s in range(4):
            base = j * LANES + (place[0] % 4 ^ s) * part
            low = turned[pl.ds(pl.multiple_of(base, 16), half), :]
            high = turned[pl.ds(pl.multiple_of(base + half, 16), half), :]
            pay = pay_near if s < 2 else pay_far
            pay[pl.ds(pl.multiple_of(s % 2 * length + j * half, 16), half), :] = jnp.concatenate(
                [low, high], axis=1
            ).astype(BF16)
        return carry

    lax.fori_loop(0, rows + 1, pack, 0, unroll=3)


def scale_of(count):
    return 0.5 / jnp.maximum(count[0:1, 0:1], 1.0)


def gradient_kernel(
    place, count, near, far, got1, got3, mixed, head, head_bias, labels, valid, wide,
    grad, low, mate, other, out0, out1, out2, out3,
    cells, lab, lab_t, val, val_t, padded_head, head_sum, bias_sum, loss_sum, total, sheet,
):
    rows, chans = mixed.shape[0], mixed.shape[1]
    bins, real = padded_head.shape[0], head.shape[0]
    half = rows // 2
    size = rows * half
    length = size + half
    for s, got in ((0, near), (2, far), (1, got1), (3, got3)):
        q = place[0] % 4 ^ s
        cells[pl.ds(pl.multiple_of(q * size, size), size), :] = got[:size, :].astype(F32)
        cells[pl.ds(pl.multiple_of(4 * size + q * half, half), half), :] = got[size:length, :].astype(F32)
    notes = [cells[4 * size + q * half : 4 * size + (q + 1) * half, :] for q in range(4)]
    for top in range(2):
        base = top * 2 * rows
        lab_t[top * half : (top + 1) * half, :] = jnp.concatenate(
            [n[:, base : base + rows] for n in notes], axis=1
        )
        val_t[top * half : (top + 1) * half, :] = jnp.concatenate(
            [n[:, base + rows : base + 2 * rows] for n in notes], axis=1
        )
    padded_head[...] = jnp.zeros_like(padded_head)
    padded_head[:real, :] = head[...].astype(F32)
    single = padded_head[...]
    blank = jnp.zeros_like(single)
    both = jnp.concatenate(
        [jnp.concatenate([single, blank], axis=1), jnp.concatenate([blank, single], axis=1)], axis=0
    ).astype(BF16)
    thrice = jnp.concatenate([single, single, single], axis=0).T.astype(BF16)
    single = single.astype(BF16)
    line = lax.broadcasted_iota(jnp.int32, (bins, real), 0)
    across = lax.broadcasted_iota(jnp.int32, (bins, real), 1)
    bias = jnp.sum(jnp.where(line == across, head_bias[...], 0.0), axis=1, keepdims=True)
    bias = jnp.where(lax.broadcasted_iota(jnp.int32, (bins, 1), 0) < real, bias, FAR_BELOW)
    lab[...] = labels[...].astype(F32)
    val[...] = valid[...].astype(F32)
    bin_ids = lax.broadcasted_iota(jnp.int32, (bins, LANES), 0).astype(F32)
    head_sum[...] = jnp.zeros_like(head_sum)
    bias_sum[...] = jnp.zeros_like(bias_sum)
    loss_sum[...] = jnp.zeros_like(loss_sum)
    total[...] = jnp.zeros_like(total)
    scale = scale_of(count)

    def step(i, carry):
        other = cells[pl.ds(i, LANES, stride=half), :].astype(BF16)
        logits_t = lax.dot_general(both, other, (((1,), (1,)), ((), ())), preferred_element_type=F32)
        pair = jnp.concatenate([mixed[i], mixed[i + half]], axis=1)
        logits = jnp.dot(single, pair, preferred_element_type=F32)
        pieces = []
        for d in range(2):
            at = pl.ds(i + d * half, 1)
            own = logits[:, d * LANES : (d + 1) * LANES] + bias
            far = logits_t[d * bins : (d + 1) * bins] + bias
            sym = 0.5 * (own + far)
            peak = jnp.max(sym, axis=0, keepdims=True)
            raised = jnp.exp(sym - peak)
            mass = jnp.sum(raised, axis=0, keepdims=True)
            lse = peak + jnp.log(mass)
            hot = bin_ids == lab[at, :]
            hot_t = bin_ids == lab_t[at, :]
            mask, mask_t = val[at, :], val_t[at, :]
            picked = jnp.sum(jnp.where(hot, sym, 0.0), axis=0, keepdims=True)
            loss_sum[...] += mask * (lse - picked)
            share = raised * ((mask + mask_t) / mass)
            pieces.append(share - jnp.where(hot, mask, 0.0) - jnp.where(hot_t, mask_t, 0.0))
        bias_sum[...] += pieces[0] + pieces[1]
        g = jnp.concatenate(pieces, axis=1)
        first = g.astype(BF16).astype(F32)
        rest = g - first
        second = rest.astype(BF16).astype(F32)
        split = jnp.concatenate([first, second, rest - second], axis=0).astype(BF16)
        out = jnp.dot(thrice, split, preferred_element_type=F32)
        grad[i] = out[:, :LANES]
        grad[i + half] = out[:, LANES:]
        rounded = (out * scale).astype(BF16)
        low[i] = rounded[:, :LANES]
        low[i + half] = rounded[:, LANES:]
        total[...] += lax.dot_general(
            jnp.concatenate([windows(wide, i), windows(wide, i + half)], axis=1),
            rounded,
            (((1,), (1,)), ((), ())),
            preferred_element_type=F32,
        )
        head_sum[...] += lax.dot_general(
            split, pair, (((1,), (1,)), ((), ())), preferred_element_type=F32
        )
        return carry

    lax.fori_loop(0, half, step, 0, unroll=UNROLL)
    share_edges(place, low, mate, other)
    upper = total.shape[0] // 2
    sheet[...] = jnp.zeros_like(sheet)
    sheet[:upper, :] = jnp.concatenate([total[:upper], total[upper:]], axis=1)
    h = (head_sum[:bins] + head_sum[bins : 2 * bins] + head_sum[2 * bins :]) * scale
    sheet[upper : upper + bins, :chans] = h
    note = upper + bins
    sheet[note : note + 1, :bins] = jnp.sum(bias_sum[...].T, axis=0, keepdims=True) * scale
    sheet[note + 1 : note + 2, :1] = jnp.sum(loss_sum[...], axis=1, keepdims=True)
    quarter = sheet.shape[0] // 4
    for s, out in enumerate((out0, out1, out2, out3)):
        out[...] = sheet[pl.ds(pl.multiple_of((place[0] % 4 ^ s) * quarter, 8), quarter), :]


def backward_kernel(
    place, count, low, mate, other, side_mate, side_other, grad, feat, weight, out, wide, edges, sides
):
    rows, chans = grad.shape[0], grad.shape[1]
    scale = scale_of(count)
    spread_columns(place, low, mate, other, side_mate, side_other, edges, sides, wide)
    taps = weight.shape[0] // chans
    kernel = jnp.concatenate(
        [weight[(taps - 1 - t) * chans : (taps - t) * chans, :].astype(F32) for t in range(taps)],
        axis=1,
    ).astype(BF16)

    def step(p, carry):
        i = 2 * p
        back = jnp.dot(kernel, pair_windows(wide, i), preferred_element_type=F32)
        for d in range(2):
            v = feat[i + d].astype(F32)
            slope = jnp.where(v > 0, 1.0, jnp.exp(jnp.minimum(v, 0.0)))
            out[i + d] = (
                grad[i + d] * scale + slope * back[:, d * LANES : (d + 1) * LANES]
            ).astype(BF16)
        return carry

    lax.fori_loop(0, rows // 2, step, 0, unroll=UNROLL)


def finish_kernel(
    place, count, got0, got1, got2, got3, kernel_grad, head_grad, bias_grad, loss, sheet
):
    quarter = got0.shape[0]
    for s, got in enumerate((got0, got1, got2, got3)):
        sheet[pl.ds(pl.multiple_of((place[0] % 4 ^ s) * quarter, 8), quarter), :] = got[...]
    half, chans = kernel_grad.shape[0] // 2, kernel_grad.shape[1]
    bins = head_grad.shape[0]
    kernel_grad[:half, :] = sheet[:half, :chans]
    kernel_grad[half:, :] = sheet[:half, chans:]
    head_grad[...] = sheet[half : half + bins, :chans]
    note = half + -(-bins // 8) * 8
    bias_grad[...] = sheet[note : note + 1, :bins]
    loss[...] = sheet[note + 1 : note + 2, :1] / jnp.maximum(count[0:1, 0:1], 1.0)


def border_buffers(rows, chans):
    groups = (rows + 2 * STEP) // 16
    return [
        pltpu.VMEM((2 * STEP, chans, LANES), BF16),
        pltpu.VMEM((2, groups, chans, LANES), BF16),
    ]


def borders(place, own, mate, other):
    rows, chans, _ = own.shape
    edges = swapped(mate, other, "row")
    groups = (rows + 2 * STEP) // 16
    sides = run(
        pack_kernel,
        [shape((groups, chans, LANES), BF16)] * 2,
        (place, own, *edges),
        scratch=border_buffers(rows, chans),
        scalars=1,
        micros=8,
    )
    return *edges, *swapped(*sides, "col")


def partners(stage):
    if stage < 2:
        return lambda m: lambda r, c: (r ^ (m << (2 * stage)), c)
    if stage == 2:
        return lambda m: lambda r, c: (r ^ ((m & 1) << 4), c ^ (m >> 1))
    return lambda m: lambda r, c: (r, c ^ (m << 1))


def total_small(value, stages):
    for stage in stages:
        to = partners(stage)
        value = (value + send(value, to(1))) + (send(value, to(2)) + send(value, to(3)))
    return value


def mirrored(pay_near, pay_far, parts):
    length = pay_near.shape[0] // 2
    pay_near = send(pay_near, lambda r, c: (r, c ^ 2))
    near = send(pay_near, lambda r, c: (parts * (c ^ 2) + r % parts, r // parts))
    far = send(pay_far, lambda r, c: (parts * c + (r % parts ^ 2), r // parts))
    mate = lambda r, c: (r ^ 1, c)
    return pay_near, (near, far, send(near[length:], mate), send(far[length:], mate))


def total_quarters(quarters):
    near = partners(0)
    a, b, c, d = quarters
    part = (a + send(b, near(1))) + (send(c, near(2)) + send(d, near(3)))
    for stage in (1, 2, 3):
        to = partners(stage)
        part = (part + send(part, to(1))) + (send(part, to(2)) + send(part, to(3)))
    return [part] + [send(part, near(m)) for m in (1, 2, 3)]


def per_device(features, conv_weight, head_weight, head_bias, labels, valid):
    rows, cols, chans = features.shape
    bins = head_weight.shape[1]
    parts = cols // rows
    place = lax.axis_index("row") % parts + 4 * (lax.axis_index("col") % 2)
    place = place.astype(jnp.int32).reshape(1)
    feat = features.transpose(0, 2, 1)
    weight = conv_weight.reshape(-1, chans)
    tall = -(-bins // 8) * 8
    tile = (rows, chans, LANES)
    edge = (STEP, chans, LANES)
    act, mate, other, counted, feat, valid = run(
        activate_kernel,
        [shape(tile, BF16), shape(edge, BF16), shape(edge, BF16), shape((8, LANES), F32)]
        + [shape(tile, BF16), shape(valid.shape, jnp.int32)],
        (place, feat, valid),
        scalars=1,
        micros=1,
    )
    around = borders(place, act, mate, other)
    counted = total_small(counted, (1, 2))
    counted, act = lax.optimization_barrier((counted, act))
    length = (rows + 1) * rows // 2
    wide, mixed, pay_near, pay_far = run(
        forward_kernel,
        [shape((rows + 2 * STEP, 3 * chans, LANES), BF16), shape(tile, BF16)]
        + [shape((2 * length, LANES), BF16)] * 2,
        (place, act, *around, feat, weight, labels, valid),
        scratch=[pltpu.VMEM(((rows + 1) * LANES, chans), F32)] + border_buffers(rows, chans),
        scalars=1,
        micros=5,
    )
    passed, got = mirrored(pay_near, pay_far, parts)
    _, counted = lax.optimization_barrier((passed, counted))
    count = total_small(counted, (0, 3))
    half = 9 * chans // 2
    lines = -(-(half + tall + 8) // 32) * 32
    grad, low, mate, other, *quarters = run(
        gradient_kernel,
        [shape(tile, F32), shape(tile, BF16), shape(edge, BF16), shape(edge, BF16)]
        + [shape((lines // 4, LANES), F32)] * 4,
        (place, count, *got, mixed, head_weight.T, head_bias.reshape(1, bins), labels, valid, wide),
        scratch=[pltpu.VMEM((length * 4, LANES), F32)]
        + [pltpu.VMEM((rows, LANES), F32)] * 4
        + [
            pltpu.VMEM((tall, chans), F32),
            pltpu.VMEM((3 * tall, chans), F32),
            pltpu.VMEM((tall, LANES), F32),
            pltpu.VMEM((1, LANES), F32),
            pltpu.VMEM((9 * chans, chans), F32),
            pltpu.VMEM((lines, LANES), F32),
        ],
        scalars=1,
        micros=6,
    )
    sums = total_quarters(quarters)
    around = borders(place, low, mate, other)
    (grad_features,) = run(
        backward_kernel,
        [shape(tile, BF16)],
        (place, count, low, *around, grad, feat, weight),
        scratch=[pltpu.VMEM((rows + 2 * STEP, 3 * chans, LANES), BF16)]
        + border_buffers(rows, chans),
        scalars=1,
        micros=4,
    )
    kernel_grad, head_grad, bias_grad, loss = run(
        finish_kernel,
        [
            shape((9 * chans, chans), F32),
            shape((bins, chans), F32),
            shape((1, bins), F32),
            shape((1, 1), F32),
        ],
        (place, count, *sums),
        scratch=[pltpu.VMEM((lines, LANES), F32)],
        scalars=1,
        micros=1,
    )
    return (
        loss.reshape(()),
        grad_features.transpose(0, 2, 1),
        kernel_grad.reshape(conv_weight.shape),
        head_grad.T,
        bias_grad.reshape(bins),
    )


def solution(mesh):
    placed = (P("row", "col", None), P(), P(), P(), P("row", "col"), P("row", "col"))
    return jax.shard_map(
        per_device,
        mesh=mesh,
        in_specs=placed,
        out_specs=(P(), P("row", "col", None), P(), P(), P()),
        check_vma=False,
    )
```
